32 devices in a mesh: tables: 4 (over y, core), rows: 8 (over z, x).
Axes of the slice: x: 2, y: 2, z: 4, core: 2. Of those that a mesh axis runs over, the one named last changes fastest.
Arguments:
- tables_in: bfloat16 [1024, 16, 512], P('rows', 'tables')
- in_weight: bfloat16 [2, 512, 1536], replicated, may hold values from -0.25 to 0.25
- query_bias: bfloat16 [2, 512], replicated, may hold values from -1.75 to 1.75
- value_bias: bfloat16 [2, 512], replicated, may hold values from -1.75 to 1.75
- out_weight: bfloat16 [2, 512, 512], replicated, may hold values from -3 to 3
- out_bias: bfloat16 [2, 512], replicated, may hold values from -1.75 to 1.75
- attn_gain: bfloat16 [2, 512], replicated, may hold values from 0.5 to 1.5
- attn_shift: bfloat16 [2, 512], replicated, may hold values from -1.75 to 1.75
- up_weight: bfloat16 [2, 512, 1024], replicated, may hold values from -0.25 to 0.25
- up_bias: bfloat16 [2, 1024], replicated, may hold values from -3 to 3
- down_weight: bfloat16 [2, 1024, 512], replicated, may hold values from -0.1875 to 0.1875
- down_bias: bfloat16 [2, 512], replicated, may hold values from -1.75 to 1.75
- ffn_gain: bfloat16 [2, 512], replicated, may hold values from 0.5 to 1.5
- ffn_shift: bfloat16 [2, 512], replicated, may hold values from -1.75 to 1.75
- cotangent: bfloat16 [1024, 16, 512], P('rows', 'tables'), may hold values from -6 to 6
- lengths: int32 [16], P('tables'), may hold values from 128 to 1024, as said below
- train_counts: int32 [16], P('tables'), may hold values from 1 to 1023, as said below
Outputs:
- activations: float32 [1024, 16, 512], P('rows', 'tables')
- input_grad: float32 [1024, 16, 512], P('rows', 'tables')
- in_weight_grad: float32 [2, 512, 1536], replicated
- query_bias_grad: float32 [2, 512], replicated
- value_bias_grad: float32 [2, 512], replicated
- out_weight_grad: float32 [2, 512, 512], replicated
- out_bias_grad: float32 [2, 512], replicated
- attn_gain_grad: float32 [2, 512], replicated
- attn_shift_grad: float32 [2, 512], replicated
- up_weight_grad: float32 [2, 512, 1024], replicated
- up_bias_grad: float32 [2, 1024], replicated
- down_weight_grad: float32 [2, 1024, 512], replicated
- down_bias_grad: float32 [2, 512], replicated
- ffn_gain_grad: float32 [2, 512], replicated
- ffn_shift_grad: float32 [2, 512], replicated
- root_means: float32 [2, 3], replicated
The draws below stay inside these ranges and needn't reach their ends.
Inputs may be any that keep to these rules, and one draw needn't show every extreme that they name: `lengths`: in each group of 4 consecutive tables one table, drawn from the seed, has length 1024. `train_counts`: A table's train count is at least a quarter of its length, rounded down, and below its length; the table of length 1024 in each group has more than 896 train rows, and that of the first group has 1023.
All inputs are finite; a program needn't handle non-finite values.
Results may differ from the reference program's by a relative error of at most 0.024.
The reference program's roundings to bfloat16 on the way count: a program that leaves them out, or rounds other values in their place, can miss the bound.
Values may be sent and summed in bfloat16 or wider, within the bound.
A program may use at most 448 MiB of HBM per device.

```python
import jax
import jax.numpy as jnp
from jax import lax

D = 512
HEADS = 4
FF = 1024
HEAD_DIM = 128
LAYERS = 2
TB = 4
R_DEV = 128
MIN_LEN = 128
SEQ = 1024
TABLES = 16


def table_sizes(key):
    keys_four = jax.random.split(key, 4)
    draws_len = jax.random.randint(keys_four[0], (TABLES,), 0, 1025, dtype=jnp.int32)
    shaped = draws_len * draws_len // 1024
    lengths = MIN_LEN + (SEQ - MIN_LEN) * shaped // 1024
    picked = jax.random.randint(keys_four[1], (TABLES // TB,), 0, TB, dtype=jnp.int32)
    full_table = jnp.arange(TABLES, dtype=jnp.int32) % TB == jnp.repeat(picked, TB)
    lengths = jnp.where(full_table, SEQ, lengths)
    spread = jax.random.randint(keys_four[2], (TABLES,), 0, 1 << 20, dtype=jnp.int32)
    low_count = lengths // 4
    counts = low_count + spread % (lengths - low_count)
    near_end = SEQ - 1 - jax.random.randint(keys_four[3], (TABLES,), 0, R_DEV // 2, dtype=jnp.int32)
    first_group = jnp.arange(TABLES, dtype=jnp.int32) < TB
    near_end = jnp.where(first_group, SEQ - 1, near_end)
    counts = jnp.where(full_table, near_end, counts)
    return (lengths.astype(jnp.int32), counts.astype(jnp.int32))


def draw_lengths(key, part):
    shared = table_sizes(key)
    return shared[0]


def draw_train_counts(key, part):
    shared = table_sizes(key)
    return shared[1]


def draw_tables_in(key, part):
    key = jax.random.fold_in(key, 3)
    row_index = jnp.arange(SEQ, dtype=jnp.float32)[:, None]
    table_index = jnp.arange(TABLES, dtype=jnp.float32)[None, :]
    positions = (table_index * SEQ + row_index) / (TABLES * SEQ)
    noise_draw = jax.random.normal(key, (SEQ, TABLES, D), jnp.float32)
    scale_rows = 1.0 + 2.0 * positions
    return (noise_draw * scale_rows[:, :, None]).astype(jnp.bfloat16)


def shard_levels(own_key, dims, pieces, smallest, top_value):
    gain, own = 1.0, jax.random.fold_in(own_key, 6)
    for position, shards_of in pieces:
        steps = jnp.exp(jax.random.uniform(jax.random.fold_in(own, position), (shards_of,), jnp.float32, smallest / len(pieces), top_value / len(pieces)))
        gain = gain * jnp.repeat(steps, dims[position] // shards_of).reshape([-1 if axis == position else 1 for axis in range(len(dims))])
    return gain


def gaussian(stream_key, dims, deviation, limit, shards=(), held_as=jnp.bfloat16):
    drawn = deviation * jax.random.normal(stream_key, dims, jnp.float32)
    if shards:
        drawn = drawn * shard_levels(stream_key, dims, shards, -0.22, 0.18)
    return jnp.clip(drawn, -limit, limit).astype(held_as)


def setup_inputs(seed: int = 0) -> dict:
    keys = jax.random.split(jax.random.key(seed), 18)
    tables_in = draw_tables_in(jax.random.fold_in(keys[17], 71), 0)
    in_weight = gaussian(keys[1], (LAYERS, D, 3 * D), D ** -0.5, 0.25)
    query_bias = gaussian(keys[2], (LAYERS, D), 0.3, 1.75)
    value_bias = gaussian(keys[3], (LAYERS, D), 0.3, 1.75)
    out_weight = gaussian(keys[4], (LAYERS, D, D), (max(1, 8 * D // SEQ)) ** -0.5, 3.0)
    out_bias = gaussian(keys[5], (LAYERS, D), 0.3, 1.75)
    attn_gain = jnp.clip(1.0 + 0.1 * jax.random.normal(keys[6], (LAYERS, D), jnp.float32), 0.5, 1.5).astype(jnp.bfloat16)
    attn_shift = gaussian(keys[7], (LAYERS, D), 0.3, 1.75)
    up_weight = gaussian(keys[8], (LAYERS, D, FF), D ** -0.5, 0.25)
    up_bias = gaussian(keys[9], (LAYERS, FF), 0.5, 3.0)
    down_weight = gaussian(keys[10], (LAYERS, FF, D), FF ** -0.5, 0.1875)
    down_bias = gaussian(keys[11], (LAYERS, D), 0.3, 1.75)
    ffn_gain = jnp.clip(1.0 + 0.1 * jax.random.normal(keys[12], (LAYERS, D), jnp.float32), 0.5, 1.5).astype(jnp.bfloat16)
    ffn_shift = gaussian(keys[13], (LAYERS, D), 0.3, 1.75)
    cotangent = gaussian(keys[14], (SEQ, TABLES, D), 1.0, 6.0, ((0, 8), (1, 4)))
    lengths = draw_lengths(jax.random.fold_in(keys[17], 71), 0)
    train_counts = draw_train_counts(jax.random.fold_in(keys[17], 71), 0)
    return dict(tables_in=tables_in, in_weight=in_weight, query_bias=query_bias, value_bias=value_bias, out_weight=out_weight, out_bias=out_bias, attn_gain=attn_gain, attn_shift=attn_shift, up_weight=up_weight, up_bias=up_bias, down_weight=down_weight, down_bias=down_bias, ffn_gain=ffn_gain, ffn_shift=ffn_shift, cotangent=cotangent, lengths=lengths, train_counts=train_counts)


@jax.custom_vjp
def low(v):
    return lax.optimization_barrier(v.astype(jnp.bfloat16)).astype(jnp.float32)

@jax.custom_vjp
def low_back(v):
    return v

def low_keep(v):
    return (low(v), None)

def low_pass(kept, grad):
    return (grad,)

def back_keep(v):
    return (v, None)

def back_low(kept, grad):
    return (low(grad),)
low.defvjp(low_keep, low_pass)
low_back.defvjp(back_keep, back_low)
EPSILON = 1e-05
MASKED = -1e+30
HIGHEST = lax.Precision.HIGHEST

def layer_norm(values, gain_row, offsets):
    average = lax.optimization_barrier(jnp.mean(values, axis=-1, keepdims=True))
    centered = values - average
    variance = lax.optimization_barrier(jnp.mean(centered * centered, axis=-1, keepdims=True))
    return centered * lax.rsqrt(variance + EPSILON) * gain_row + offsets

def gelu_exact(values):
    return jax.nn.gelu(values, approximate=False)

def attend_table(operands):
    queries, key_rows, value_rows, train_count = operands
    scores = low_back(jnp.einsum('ihe,jhe->hij', queries, key_rows, precision=HIGHEST))
    usable = jnp.arange(SEQ, dtype=jnp.int32)[None, None, :] < train_count
    scores = jnp.where(usable, scores, MASKED)
    row_max = lax.optimization_barrier(jnp.max(scores, axis=-1, keepdims=True))
    exponent = jnp.exp(scores - row_max)
    attn_probs = exponent / lax.optimization_barrier(jnp.sum(exponent, axis=-1, keepdims=True))
    return jnp.einsum('hij,jhe->ihe', low(attn_probs), value_rows, precision=HIGHEST)

def by_table(values):
    return jnp.transpose(values.reshape(SEQ, TABLES, HEADS, HEAD_DIM), (1, 0, 2, 3))

def encoder_layer(stream, in_weight, query_bias, value_bias, out_weight, out_bias, attn_gain, attn_shift, up_weight, up_bias, down_weight, down_bias, ffn_gain, ffn_shift, train_counts):
    in_low = low(stream)
    projected = jnp.einsum('itd,de->ite', in_low, in_weight, precision=HIGHEST)
    queries = low_back(low((projected[:, :, :D] + query_bias) * HEAD_DIM ** (-0.5)))
    key_rows = low_back(low(projected[:, :, D:2 * D]))
    value_rows = low_back(low(projected[:, :, 2 * D:] + value_bias))
    attended = lax.map(jax.checkpoint(attend_table), (by_table(queries), by_table(key_rows), by_table(value_rows), train_counts))
    attended = jnp.transpose(attended, (1, 0, 2, 3)).reshape(SEQ, TABLES, D)
    attended = low_back(low(attended))
    branch = low_back(jnp.einsum('itd,de->ite', attended, out_weight, precision=HIGHEST) + out_bias)
    first_out = layer_norm(stream + branch, attn_gain, attn_shift)
    hidden = low_back(jnp.einsum('itd,df->itf', low(first_out), up_weight, precision=HIGHEST) + up_bias)
    ffn_out = low_back(jnp.einsum('itf,fd->itd', low(gelu_exact(hidden)), down_weight, precision=HIGHEST) + down_bias)
    return (layer_norm(first_out + ffn_out, ffn_gain, ffn_shift), branch, ffn_out)

def encoder_stack(tables_in, in_weight, query_bias, value_bias, out_weight, out_bias, attn_gain, attn_shift, up_weight, up_bias, down_weight, down_bias, ffn_gain, ffn_shift, train_counts, valid_rows):
    stream = tables_in
    valid_cells = valid_rows[:, :, None]
    squares = []
    for layer_index in range(LAYERS):
        in_square = jnp.sum(valid_cells * stream * stream)
        stream, branch, ffn_out = encoder_layer(stream, in_weight[layer_index], query_bias[layer_index], value_bias[layer_index], out_weight[layer_index], out_bias[layer_index], attn_gain[layer_index], attn_shift[layer_index], up_weight[layer_index], up_bias[layer_index], down_weight[layer_index], down_bias[layer_index], ffn_gain[layer_index], ffn_shift[layer_index], train_counts)
        squares.append(jnp.stack([in_square, jnp.sum(valid_cells * branch * branch), jnp.sum(valid_cells * ffn_out * ffn_out)]))
    return (stream * valid_cells, jnp.stack(squares))

def reference(tables_in, in_weight, query_bias, value_bias, out_weight, out_bias, attn_gain, attn_shift, up_weight, up_bias, down_weight, down_bias, ffn_gain, ffn_shift, cotangent, lengths, train_counts):
    valid_rows = (jnp.arange(SEQ, dtype=jnp.int32)[:, None] < lengths[None, :]).astype(jnp.float32)
    params = [tensor.astype(jnp.float32) for tensor in (tables_in, in_weight, query_bias, value_bias, out_weight, out_bias, attn_gain, attn_shift, up_weight, up_bias, down_weight, down_bias, ffn_gain, ffn_shift)]

    def stacked(*floats):
        return encoder_stack(*floats, train_counts, valid_rows)
    activations, pull_back, squares = jax.vjp(stacked, *params, has_aux=True)
    layer_grads = pull_back(cotangent.astype(jnp.float32))
    row_count = jnp.sum(lengths).astype(jnp.float32)
    root_means = jnp.sqrt(squares / (row_count * D))
    return (activations, layer_grads[0], layer_grads[1], layer_grads[2], layer_grads[3], layer_grads[4], layer_grads[5], layer_grads[6], layer_grads[7], layer_grads[8], layer_grads[9], layer_grads[10], layer_grads[11], layer_grads[12], layer_grads[13], root_means)
```

```python
import functools

import jax
import jax.numpy as jnp
from jax import lax
from jax.experimental import pallas as pl
from jax.experimental.pallas import tpu as pltpu
from jax.sharding import PartitionSpec as P

D = 512
HEADS = 4
LAYERS = 2


EPSILON = 1e-05
MASKED = -1e30


def norm_forward(values, gain_row, offsets):
    average = jnp.mean(values, axis=-1, keepdims=True)
    centered = values - average
    variance = jnp.mean(centered * centered, axis=-1, keepdims=True)
    inverse = lax.rsqrt(variance + EPSILON)
    normed = centered * inverse
    return (normed * gain_row + offsets, normed, inverse)


def norm_backward(upstream, normed, inverse, gain_row):
    scaled = upstream * gain_row
    average = jnp.mean(scaled, axis=-1, keepdims=True)
    projection = jnp.mean(scaled * normed, axis=-1, keepdims=True)
    return inverse * (scaled - average - normed * projection)


def gelu_exact(values):
    return jax.nn.gelu(values, approximate=False)


def split_heads(values):
    return values.reshape(values.shape[0], values.shape[1], HEADS, values.shape[2] // HEADS)


def merge_heads(values):
    return values.reshape(values.shape[0], values.shape[1], values.shape[2] * values.shape[3])


def table_scores(queries, key_rows, usable):
    scores = jnp.einsum(
        "ibhe,jbhe->bhij",
        split_heads(queries),
        split_heads(key_rows),
        preferred_element_type=jnp.float32,
    )
    return jnp.where(usable[:, None, None, :], scores, MASKED)


def row_sums(values):
    return jnp.sum(values.astype(jnp.float32), axis=(0, 1))


def gathered_device(
    tables_in,
    in_weight,
    query_bias,
    value_bias,
    out_weight,
    out_bias,
    attn_gain,
    attn_shift,
    up_weight,
    up_bias,
    down_weight,
    down_bias,
    ffn_gain,
    ffn_shift,
    cotangent,
    lengths,
    train_counts,
):
    local_rows = tables_in.shape[0]
    seq_rows = local_rows * lax.axis_size("rows")
    positions = lax.axis_index("rows") * local_rows + jnp.arange(local_rows, dtype=jnp.int32)
    valid_rows = (positions[:, None] < lengths[None, :]).astype(jnp.float32)
    valid_cells = valid_rows[:, :, None]
    usable = jnp.arange(seq_rows, dtype=jnp.int32)[None, :] < train_counts[:, None]
    score_scale = (D // HEADS) ** (-0.5)
    column_scale = jnp.concatenate(
        [jnp.full((D,), score_scale, jnp.float32), jnp.ones((2 * D,), jnp.float32)]
    )
    stream = tables_in.astype(jnp.float32)
    stored = []
    squares = []
    for layer_index in range(LAYERS):
        in_low = stream.astype(jnp.bfloat16)
        projected = jnp.einsum(
            "ibd,de->ibe", in_low, in_weight[layer_index], preferred_element_type=jnp.float32
        )
        queries = ((projected[:, :, :D] + query_bias[layer_index]) * score_scale).astype(
            jnp.bfloat16
        )
        key_rows = projected[:, :, D : 2 * D].astype(jnp.bfloat16)
        value_rows = (projected[:, :, 2 * D :] + value_bias[layer_index]).astype(jnp.bfloat16)
        all_keys, all_values = (
            lax.all_gather(key_rows, "rows", axis=0, tiled=True),
            lax.all_gather(value_rows, "rows", axis=0, tiled=True),
        )
        scores = table_scores(queries, all_keys, usable)
        row_max = jnp.max(scores, axis=-1, keepdims=True)
        exponent = jnp.exp(scores - row_max)
        row_total = jnp.sum(exponent, axis=-1, keepdims=True)
        probs_low = (exponent / row_total).astype(jnp.bfloat16)
        log_total = (row_max + jnp.log(row_total))[..., 0]
        attended = merge_heads(
            jnp.einsum(
                "bhij,jbhe->ibhe",
                probs_low,
                split_heads(all_values),
                preferred_element_type=jnp.float32,
            )
        ).astype(jnp.bfloat16)
        branch = (
            jnp.einsum(
                "ibd,de->ibe", attended, out_weight[layer_index], preferred_element_type=jnp.float32
            )
            + out_bias[layer_index]
        )
        first_out, first_norm, first_inverse = norm_forward(
            stream + branch, attn_gain[layer_index], attn_shift[layer_index]
        )
        mid_low = first_out.astype(jnp.bfloat16)
        hidden = (
            jnp.einsum(
                "ibd,df->ibf", mid_low, up_weight[layer_index], preferred_element_type=jnp.float32
            )
            + up_bias[layer_index]
        )
        act_low = gelu_exact(hidden).astype(jnp.bfloat16)
        ffn_out = (
            jnp.einsum(
                "ibf,fd->ibd", act_low, down_weight[layer_index], preferred_element_type=jnp.float32
            )
            + down_bias[layer_index]
        )
        second_out, second_norm, second_inverse = norm_forward(
            first_out + ffn_out, ffn_gain[layer_index], ffn_shift[layer_index]
        )
        squares.append(
            jnp.stack(
                [
                    jnp.sum(valid_cells * stream * stream),
                    jnp.sum(valid_cells * branch * branch),
                    jnp.sum(valid_cells * ffn_out * ffn_out),
                ]
            )
        )
        gathered = (all_keys, all_values)
        stored.append(
            (
                in_low,
                queries,
                key_rows,
                value_rows,
                gathered,
                log_total,
                attended,
                first_norm,
                first_inverse,
                mid_low,
                hidden,
                act_low,
                second_norm,
                second_inverse,
            )
        )
        stream = second_out
    activations = stream * valid_cells
    upstream = cotangent.astype(jnp.float32) * valid_cells
    layer_grads = [None] * LAYERS
    for layer_index in reversed(range(LAYERS)):
        (
            in_low,
            queries,
            key_rows,
            value_rows,
            gathered,
            log_total,
            attended,
            first_norm,
            first_inverse,
            mid_low,
            hidden,
            act_low,
            second_norm,
            second_inverse,
        ) = stored[layer_index]
        ffn_gain_grad = jnp.sum(upstream * second_norm, axis=(0, 1))
        ffn_shift_grad = jnp.sum(upstream, axis=(0, 1))
        second_grad = norm_backward(upstream, second_norm, second_inverse, ffn_gain[layer_index])
        ffn_low = second_grad.astype(jnp.bfloat16)
        down_weight_grad = jnp.einsum(
            "ibf,ibd->fd", act_low, ffn_low, preferred_element_type=jnp.float32
        )
        act_grad = jnp.einsum(
            "ibd,fd->ibf", ffn_low, down_weight[layer_index], preferred_element_type=jnp.float32
        )
        hidden_low = jax.vjp(gelu_exact, hidden)[1](act_grad)[0].astype(jnp.bfloat16)
        up_weight_grad = jnp.einsum(
            "ibd,ibf->df", mid_low, hidden_low, preferred_element_type=jnp.float32
        )
        first_grad = second_grad + jnp.einsum(
            "ibf,df->ibd", hidden_low, up_weight[layer_index], preferred_element_type=jnp.float32
        )
        attn_gain_grad = jnp.sum(first_grad * first_norm, axis=(0, 1))
        attn_shift_grad = jnp.sum(first_grad, axis=(0, 1))
        residual_grad = norm_backward(first_grad, first_norm, first_inverse, attn_gain[layer_index])
        branch_low = residual_grad.astype(jnp.bfloat16)
        out_weight_grad = jnp.einsum(
            "ibd,ibe->de", attended, branch_low, preferred_element_type=jnp.float32
        )
        attended_low = jnp.einsum(
            "ibe,de->ibd", branch_low, out_weight[layer_index], preferred_element_type=jnp.float32
        ).astype(jnp.bfloat16)
        all_keys, all_values = gathered
        scores = table_scores(queries, all_keys, usable)
        attn_probs = jnp.exp(scores - log_total[..., None])
        probs_low = attn_probs.astype(jnp.bfloat16)
        probs_grad = jnp.einsum(
            "ibhe,jbhe->bhij",
            split_heads(attended_low),
            split_heads(all_values),
            preferred_element_type=jnp.float32,
        )
        center = jnp.sum(attn_probs * probs_grad, axis=-1)
        scores_low = (attn_probs * (probs_grad - center[..., None])).astype(jnp.bfloat16)
        query_low = merge_heads(
            jnp.einsum(
                "bhij,jbhe->ibhe",
                scores_low,
                split_heads(all_keys),
                preferred_element_type=jnp.float32,
            )
        ).astype(jnp.bfloat16)
        key_part = jnp.einsum(
            "bhij,ibhe->jbhe", scores_low, split_heads(queries), preferred_element_type=jnp.float32
        )
        value_part = jnp.einsum(
            "bhij,ibhe->jbhe",
            probs_low,
            split_heads(attended_low),
            preferred_element_type=jnp.float32,
        )
        key_sums = lax.psum_scatter(
            jnp.concatenate([merge_heads(key_part), merge_heads(value_part)], axis=-1).astype(
                jnp.bfloat16
            ),
            "rows",
            scatter_dimension=0,
            tiled=True,
        )
        proj_low = jnp.concatenate([query_low, key_sums], axis=-1)
        in_weight_grad = (
            jnp.einsum("ibd,ibe->de", in_low, proj_low, preferred_element_type=jnp.float32)
            * column_scale
        )
        query_bias_grad = row_sums(query_low) * score_scale
        value_bias_grad = row_sums(proj_low[:, :, 2 * D :])
        weight_now = in_weight[layer_index]
        query_input = (
            jnp.einsum(
                "ibe,de->ibd", query_low, weight_now[:, :D], preferred_element_type=jnp.float32
            )
            * score_scale
        )
        other_input = jnp.einsum(
            "ibe,de->ibd", proj_low[:, :, D:], weight_now[:, D:], preferred_element_type=jnp.float32
        )
        upstream = residual_grad + query_input + other_input
        layer_grads[layer_index] = (
            in_weight_grad,
            query_bias_grad,
            value_bias_grad,
            out_weight_grad,
            row_sums(branch_low),
            attn_gain_grad,
            attn_shift_grad,
            up_weight_grad,
            row_sums(hidden_low),
            down_weight_grad,
            row_sums(ffn_low),
            ffn_gain_grad,
            ffn_shift_grad,
        )
    stacked = [
        jnp.stack([layer_grads[layer_index][member] for layer_index in range(LAYERS)])
        for member in range(13)
    ]
    totals = lax.psum(
        (
            stacked[0],
            stacked[1],
            stacked[2],
            stacked[3],
            stacked[4],
            stacked[5],
            stacked[6],
            stacked[7],
            stacked[8],
            stacked[9],
            stacked[10],
            stacked[11],
            stacked[12],
            jnp.stack(squares),
            jnp.sum(valid_rows),
        ),
        ("tables", "rows"),
    )
    root_means = jnp.sqrt(totals[13] / (totals[14] * D))
    return (
        activations,
        upstream,
        totals[0],
        totals[1],
        totals[2],
        totals[3],
        totals[4],
        totals[5],
        totals[6],
        totals[7],
        totals[8],
        totals[9],
        totals[10],
        totals[11],
        totals[12],
        root_means,
    )


MESH = pl.DeviceIdType.MESH
NT = (((1,), (1,)), ((), ()))
NN = (((1,), (0,)), ((), ()))
TN = (((0,), (0,)), ((), ()))
TILE = 256
VECTORS = 9


def dot(left, right, dims=NN):
    return lax.dot_general(left, right, dims, preferred_element_type=jnp.float32)


def column_sum(values):
    return jnp.sum(values, axis=0, keepdims=True)


def row_mean(values):
    return jnp.mean(values, axis=-1, keepdims=True)


def table_kernel(
    local,
    block_tables,
    seq,
    x_hbm,
    cot_hbm,
    meta_ref,
    w_in,
    w_out,
    w_up,
    w_down,
    vectors,
    act_hbm,
    xgrad_hbm,
    g_in,
    g_out,
    g_up,
    g_down,
    small,
    in_low,
    cot_low,
    stream,
    queries,
    kv,
    attended,
    stats,
    norm1,
    inverse1,
    mid_low,
    slope,
    act_low,
    norm2,
    inverse2,
    meta,
    bias_row,
    bias_col,
    valid,
    upstream,
    ffn_low,
    hidden_low,
    branch_low,
    attended_low,
    stats_rows,
    dq_t,
    dkv_own,
    dkv_send,
    dkv_recv,
    proj_low,
    staged,
    x_send,
    x_recv,
    cot_send,
    cot_recv,
    act_send,
    act_recv,
    xg_send,
    xg_recv,
    local_sem,
    kv_sem,
    dkv_sem,
    meta_sem,
):
    rows = block_tables * local
    dim = in_low.shape[-1]
    head_dim = dim // HEADS
    scale = head_dim**-0.5
    tiles = rows // TILE
    t = lax.axis_index("tables")
    r = lax.axis_index("rows")
    core = lax.rem(t, 2)
    side = r // block_tables
    slot = lax.rem(r, block_tables)
    peer = (t + 1 - 2 * core, r)
    own_rows = pl.multiple_of(core * rows, rows)
    peer_rows = pl.multiple_of((1 - core) * rows, rows)

    def partner(k):
        return (t - core + side, block_tables * core + k)

    def is_self(k):
        return jnp.logical_and(core == side, slot == k)

    barrier = pltpu.get_barrier_semaphore()
    pl.semaphore_signal(barrier, inc=1, device_id=peer, device_id_type=MESH)
    for k in range(block_tables):

        @pl.when(jnp.logical_not(is_self(k)))
        def _():
            pl.semaphore_signal(barrier, inc=1, device_id=partner(k), device_id_type=MESH)

    pl.semaphore_wait(barrier, jnp.where(core == side, block_tables, block_tables + 1))

    def spread(source, target, send_sem, recv_sem, own_sem):
        def remote(k, at):
            return pltpu.make_async_remote_copy(
                src_ref=source(k),
                dst_ref=target(at),
                send_sem=send_sem.at[k],
                recv_sem=recv_sem.at[at],
                device_id=partner(k),
                device_id_type=MESH,
            )

        def kept(k):
            return pltpu.make_async_copy(source(k), target(k), own_sem)

        def start():
            for k in range(block_tables):

                @pl.when(is_self(k))
                def _():
                    kept(k).start()

                @pl.when(jnp.logical_not(is_self(k)))
                def _():
                    remote(k, slot).start()

        def arrive():
            for k in range(block_tables):

                @pl.when(is_self(k))
                def _():
                    kept(k).wait()

                @pl.when(jnp.logical_not(is_self(k)))
                def _():
                    remote(k, k).wait_recv()

        def left():
            for k in range(block_tables):

                @pl.when(jnp.logical_not(is_self(k)))
                def _():
                    remote(k, slot).wait_send()

        return start, arrive, left

    def by_table(ref):
        return lambda k: ref.at[k]

    def by_rows(ref):
        return lambda k: ref.at[pl.ds(k * local, local)]

    x_start, x_arrive, x_left = spread(by_table(x_hbm), by_rows(in_low.at[0]), x_send, x_recv, local_sem.at[0])
    cot_start, cot_arrive, cot_left = spread(by_table(cot_hbm), by_rows(cot_low), cot_send, cot_recv, local_sem.at[1])
    act_start, act_arrive, act_left = spread(by_rows(staged.at[0]), by_table(act_hbm), act_send, act_recv, local_sem.at[2])
    xg_start, xg_arrive, xg_left = spread(by_rows(staged.at[1]), by_table(xgrad_hbm), xg_send, xg_recv, local_sem.at[3])

    def swap(source, target, sems):
        return pltpu.make_async_remote_copy(
            src_ref=source,
            dst_ref=target,
            send_sem=sems.at[0],
            recv_sem=sems.at[1],
            device_id=peer,
            device_id_type=MESH,
        )

    x_start()
    cot_start()
    meta_own = pltpu.make_async_copy(meta_ref, meta.at[core], local_sem.at[4])
    meta_own.start()
    meta_copy = swap(meta_ref, meta.at[core], meta_sem)
    meta_copy.start()

    small[...] = jnp.zeros_like(small)
    meta_own.wait()
    meta_copy.wait()
    length = meta[side, pl.ds(slot, 1), :][:, :1]
    train = meta[side, pl.ds(slot + block_tables, 1), :][:, :1]
    bias_row[...] = jnp.where(lax.broadcasted_iota(jnp.int32, (1, seq), 1) < train, 0.0, MASKED)
    bias_col[...] = jnp.where(lax.broadcasted_iota(jnp.int32, (seq, 1), 0) < train, 0.0, MASKED)
    valid[...] = jnp.where(
        lax.broadcasted_iota(jnp.int32, (rows, 1), 0) + core * rows < length, 1.0, 0.0
    )
    x_arrive()

    def vector(index, layer, width):
        return vectors[pl.ds(layer * VECTORS + index, 1), pl.ds(0, width)]

    def add_small(layer, index, values):
        at = (pl.ds(layer * 16 + index, 1), pl.ds(0, values.shape[-1]))
        small[at] = small[at] + values

    def each_tile(body):
        def step(i, carry):
            body(pl.ds(pl.multiple_of(i * TILE, TILE), TILE))
            return carry

        lax.fori_loop(0, tiles, step, 0)

    def head_cols(h):
        return pl.ds(pl.multiple_of(h * head_dim, head_dim), head_dim)

    def forward(layer):
        def project(at):
            projected = dot(in_low[layer, at, :], w_in[layer])
            queries[layer, at, :] = (
                (projected[:, :dim] + vector(0, layer, dim)) * scale
            ).astype(jnp.bfloat16)
            own = pl.ds(pl.multiple_of(own_rows + at.start, TILE), TILE)
            kv[layer, own, pl.ds(0, dim)] = projected[:, dim : 2 * dim].astype(jnp.bfloat16)
            kv[layer, own, pl.ds(dim, dim)] = (
                projected[:, 2 * dim :] + vector(1, layer, dim)
            ).astype(jnp.bfloat16)

        each_tile(project)
        mine = kv.at[layer, pl.ds(own_rows, rows)]
        kv_copy = swap(mine, mine, kv_sem.at[layer])
        kv_copy.start()
        kv_copy.wait()

        def attend(step, carry):
            h = step // tiles
            at = pl.ds(pl.multiple_of(lax.rem(step, tiles) * TILE, TILE), TILE)
            cols = head_cols(h)
            key_rows = kv[layer, :, cols]
            value_rows = kv[layer, :, pl.ds(pl.multiple_of(dim + h * head_dim, head_dim), head_dim)]
            scores = dot(queries[layer, at, cols], key_rows, NT) + bias_row[...]
            row_max = jnp.max(scores, axis=-1, keepdims=True)
            exponent = jnp.exp(scores - row_max)
            total = jnp.sum(exponent, axis=-1, keepdims=True)
            probs = (exponent * (1.0 / total)).astype(jnp.bfloat16)
            attended[layer, at, cols] = dot(probs, value_rows).astype(jnp.bfloat16)
            lane = lax.broadcasted_iota(jnp.int32, (TILE, head_dim), 1)
            kept = jnp.where(h == 0, jnp.zeros((TILE, head_dim), jnp.float32), stats[layer, at, :])
            stats[layer, at, :] = jnp.where(lane == h, row_max + jnp.log(total), kept)
            return carry

        lax.fori_loop(0, HEADS * tiles, attend, 0)

        def dense(at):
            below = in_low[0, at, :].astype(jnp.float32) if layer == 0 else stream[at, :]
            branch = dot(attended[layer, at, :], w_out[layer]) + vector(2, layer, dim)
            valid_cells = valid[at, :]
            add_small(layer, 10, column_sum(below * below * valid_cells))
            add_small(layer, 11, column_sum(branch * branch * valid_cells))
            summed = below + branch
            centered = summed - row_mean(summed)
            inverse = lax.rsqrt(row_mean(centered * centered) + EPSILON)
            normed = centered * inverse
            norm1[layer, at, :] = normed
            inverse1[layer, at, :] = inverse
            first_out = normed * vector(3, layer, dim) + vector(4, layer, dim)
            mid = first_out.astype(jnp.bfloat16)
            mid_low[layer, at, :] = mid
            hidden = dot(mid, w_up[layer]) + vector(5, layer, 2 * dim)
            cdf = 0.5 + 0.5 * lax.erf(hidden * (0.5**0.5))
            slope[layer, at, :] = cdf + hidden * (
                jnp.exp(hidden * hidden * -0.5) * 0.3989422804014327
            )
            act = (hidden * cdf).astype(jnp.bfloat16)
            act_low[layer, at, :] = act
            ffn_out = dot(act, w_down[layer]) + vector(6, layer, dim)
            add_small(layer, 12, column_sum(ffn_out * ffn_out * valid_cells))
            summed = first_out + ffn_out
            centered = summed - row_mean(summed)
            inverse = lax.rsqrt(row_mean(centered * centered) + EPSILON)
            normed = centered * inverse
            norm2[layer, at, :] = normed
            inverse2[layer, at, :] = inverse
            out = normed * vector(7, layer, dim) + vector(8, layer, dim)
            if layer + 1 < LAYERS:
                stream[at, :] = out
                in_low[layer + 1, at, :] = out.astype(jnp.bfloat16)
            else:
                staged[0, at, :] = (out * valid_cells).astype(jnp.bfloat16)

        each_tile(dense)

    for layer in range(LAYERS):
        forward(layer)
    act_start()
    cot_arrive()

    def backward(layer):
        def dense(at):
            if layer == LAYERS - 1:
                up = cot_low[at, :].astype(jnp.float32) * valid[at, :]
            else:
                up = upstream[at, :]
            normed = norm2[layer, at, :]
            add_small(layer, 8, column_sum(up * normed))
            add_small(layer, 9, column_sum(up))
            scaled = up * vector(7, layer, dim)
            second = inverse2[layer, at, :] * (
                scaled - row_mean(scaled) - normed * row_mean(scaled * normed)
            )
            ffn = second.astype(jnp.bfloat16)
            ffn_low[at, :] = ffn
            add_small(layer, 7, column_sum(ffn.astype(jnp.float32)))
            hidden = (dot(ffn, w_down[layer], NT) * slope[layer, at, :]).astype(jnp.bfloat16)
            hidden_low[at, :] = hidden
            add_small(layer, 6, column_sum(hidden.astype(jnp.float32)))
            first = second + dot(hidden, w_up[layer], NT)
            normed = norm1[layer, at, :]
            add_small(layer, 4, column_sum(first * normed))
            add_small(layer, 5, column_sum(first))
            scaled = first * vector(3, layer, dim)
            residual = inverse1[layer, at, :] * (
                scaled - row_mean(scaled) - normed * row_mean(scaled * normed)
            )
            upstream[at, :] = residual
            branch = residual.astype(jnp.bfloat16)
            branch_low[at, :] = branch
            add_small(layer, 3, column_sum(branch.astype(jnp.float32)))
            low = dot(branch, w_out[layer], NT).astype(jnp.bfloat16)
            attended_low[at, :] = low
            product = low.astype(jnp.float32) * attended[layer, at, :].astype(jnp.float32)
            lane = lax.broadcasted_iota(jnp.int32, (TILE, head_dim), 1)
            held = stats[layer, at, :]
            for h in range(HEADS):
                center = jnp.sum(product[:, h * head_dim : (h + 1) * head_dim], axis=-1, keepdims=True)
                held = jnp.where(lane == HEADS + h, center, held)
            stats_rows[:, at] = jnp.transpose(held)[: 2 * HEADS, :]

        each_tile(dense)
        g_down[layer] = dot(act_low[layer], ffn_low[...], TN).astype(jnp.bfloat16)
        g_up[layer] = dot(mid_low[layer], hidden_low[...], TN).astype(jnp.bfloat16)
        g_out[layer] = dot(attended[layer], branch_low[...], TN).astype(jnp.bfloat16)

        def attend(base, first, keep):
            def step(i, carry):
                h = i // tiles
                j = pl.multiple_of(lax.rem(i, tiles) * TILE, TILE)
                at = pl.ds(pl.multiple_of(base + j, TILE), TILE)
                cols = head_cols(h)
                value_cols = pl.ds(pl.multiple_of(dim + h * head_dim, head_dim), head_dim)
                key_rows = kv[layer, at, cols]
                query_rows = queries[layer, :, cols]
                grads = attended_low[:, cols]
                probs = jnp.exp(
                    dot(key_rows, query_rows, NT) + bias_col[at, :] - stats_rows[pl.ds(h, 1), :]
                )
                value_part = dot(probs.astype(jnp.bfloat16), grads)
                probs_grad = dot(kv[layer, at, value_cols], grads, NT)
                scores_low = (probs * (probs_grad - stats_rows[pl.ds(HEADS + h, 1), :])).astype(
                    jnp.bfloat16
                )
                key_part = dot(scores_low, query_rows)
                query_part = dot(key_rows, scores_low, TN)
                if first:
                    query_part = jnp.where(j == 0, query_part, query_part + dq_t[cols, :])
                else:
                    query_part = query_part + dq_t[cols, :]
                dq_t[cols, :] = query_part
                keep(pl.ds(j, TILE), cols, key_part)
                keep(pl.ds(j, TILE), value_cols, value_part)
                return carry

            lax.fori_loop(0, HEADS * tiles, step, 0)

        def keep_sent(at, cols, part):
            dkv_send[layer, at, cols] = part.astype(jnp.bfloat16)

        def keep_own(at, cols, part):
            dkv_own[at, cols] = part

        attend(peer_rows, True, keep_sent)
        copy = swap(dkv_send.at[layer], dkv_recv.at[layer], dkv_sem.at[layer])
        copy.start()
        attend(own_rows, False, keep_own)
        copy.wait()

        def finish(at):
            query = jnp.transpose(dq_t[:, at]).astype(jnp.bfloat16)
            pair = (dkv_own[at, :] + dkv_recv[layer, at, :].astype(jnp.float32)).astype(jnp.bfloat16)
            proj_low[at, pl.ds(0, dim)] = query
            proj_low[at, pl.ds(dim, 2 * dim)] = pair
            add_small(layer, 0, column_sum(query.astype(jnp.float32)) * scale)
            add_small(layer, 1, column_sum(pair[:, dim:].astype(jnp.float32)))
            grad = (
                upstream[at, :]
                + dot(query, w_in[layer, :, pl.ds(0, dim)], NT) * scale
                + dot(pair, w_in[layer, :, pl.ds(dim, 2 * dim)], NT)
            )
            if layer > 0:
                upstream[at, :] = grad
            else:
                staged[1, at, :] = grad.astype(jnp.bfloat16)

        each_tile(finish)
        if layer == 0:
            xg_start()
        g_in[layer, :, pl.ds(0, dim)] = (
            dot(in_low[layer], proj_low[:, pl.ds(0, dim)], TN) * scale
        ).astype(jnp.bfloat16)
        g_in[layer, :, pl.ds(dim, 2 * dim)] = dot(
            in_low[layer], proj_low[:, pl.ds(dim, 2 * dim)], TN
        ).astype(jnp.bfloat16)

    for layer in reversed(range(LAYERS)):
        backward(layer)
    act_arrive()
    xg_arrive()
    x_left()
    cot_left()
    act_left()
    xg_left()


def table_device(tables, row_parts, *operands):
    (
        tables_in,
        in_weight,
        query_bias,
        value_bias,
        out_weight,
        out_bias,
        attn_gain,
        attn_shift,
        up_weight,
        up_bias,
        down_weight,
        down_bias,
        ffn_gain,
        ffn_shift,
        cotangent,
        lengths,
        train_counts,
    ) = operands
    local, block_tables, dim = tables_in.shape
    rows = local * block_tables
    seq = local * row_parts
    hidden = up_weight.shape[-1]
    head_dim = dim // HEADS
    f32, bf16 = jnp.float32, jnp.bfloat16
    vectors = jnp.stack(
        [
            jnp.pad(v.astype(f32), ((0, 0), (0, hidden - v.shape[-1])))
            for v in (
                query_bias,
                value_bias,
                out_bias,
                attn_gain,
                attn_shift,
                up_bias,
                down_bias,
                ffn_gain,
                ffn_shift,
            )
        ],
        axis=1,
    ).reshape(LAYERS * VECTORS, hidden)
    meta = jnp.broadcast_to(jnp.concatenate([lengths, train_counts])[:, None], (2 * block_tables, 128))
    vmem = pl.BlockSpec(memory_space=pltpu.VMEM)
    hbm = pl.BlockSpec(memory_space=pl.ANY)
    block = (block_tables, local, dim)
    dma = pltpu.SemaphoreType.DMA
    act, xgrad, g_in, g_out, g_up, g_down, small = pl.pallas_call(
        functools.partial(table_kernel, local, block_tables, seq),
        out_shape=(
            jax.ShapeDtypeStruct(block, bf16),
            jax.ShapeDtypeStruct(block, bf16),
            jax.ShapeDtypeStruct(in_weight.shape, bf16),
            jax.ShapeDtypeStruct(out_weight.shape, bf16),
            jax.ShapeDtypeStruct(up_weight.shape, bf16),
            jax.ShapeDtypeStruct(down_weight.shape, bf16),
            jax.ShapeDtypeStruct((LAYERS * 16, hidden), f32),
        ),
        in_specs=[hbm, hbm] + [vmem] * 6,
        out_specs=(hbm, hbm) + (vmem,) * 5,
        scratch_shapes=[
            pltpu.VMEM((LAYERS, rows, dim), bf16),
            pltpu.VMEM((rows, dim), bf16),
            pltpu.VMEM((rows, dim), f32),
            pltpu.VMEM((LAYERS, rows, dim), bf16),
            pltpu.VMEM((LAYERS, seq, 2 * dim), bf16),
            pltpu.VMEM((LAYERS, rows, dim), bf16),
            pltpu.VMEM((LAYERS, rows, head_dim), f32),
            pltpu.VMEM((LAYERS, rows, dim), f32),
            pltpu.VMEM((LAYERS, rows, 1), f32),
            pltpu.VMEM((LAYERS, rows, dim), bf16),
            pltpu.VMEM((LAYERS, rows, hidden), f32),
            pltpu.VMEM((LAYERS, rows, hidden), bf16),
            pltpu.VMEM((LAYERS, rows, dim), f32),
            pltpu.VMEM((LAYERS, rows, 1), f32),
            pltpu.VMEM((2, 2 * block_tables, 128), jnp.int32),
            pltpu.VMEM((1, seq), f32),
            pltpu.VMEM((seq, 1), f32),
            pltpu.VMEM((rows, 1), f32),
            pltpu.VMEM((rows, dim), f32),
            pltpu.VMEM((rows, dim), bf16),
            pltpu.VMEM((rows, hidden), bf16),
            pltpu.VMEM((rows, dim), bf16),
            pltpu.VMEM((rows, dim), bf16),
            pltpu.VMEM((2 * HEADS, rows), f32),
            pltpu.VMEM((dim, rows), f32),
            pltpu.VMEM((rows, 2 * dim), f32),
            pltpu.VMEM((LAYERS, rows, 2 * dim), bf16),
            pltpu.VMEM((LAYERS, rows, 2 * dim), bf16),
            pltpu.VMEM((rows, 3 * dim), bf16),
            pltpu.VMEM((2, rows, dim), bf16),
        ]
        + [dma((block_tables,))] * 8
        + [dma((5,)), dma((LAYERS, 2)), dma((LAYERS, 2)), dma((2,))],
        compiler_params=pltpu.CompilerParams(
            collective_id=0, has_side_effects=True, vmem_limit_bytes=62 * 1024 * 1024
        ),
    )(
        jnp.swapaxes(tables_in, 0, 1),
        jnp.swapaxes(cotangent, 0, 1),
        meta,
        in_weight,
        out_weight,
        up_weight,
        down_weight,
        vectors,
    )
    count = jnp.sum(lengths.astype(f32)) / row_parts
    totals = lax.psum((g_in, g_out, g_up, g_down, small, count), ("tables", "rows"))
    g_in, g_out, g_up, g_down = [total.astype(f32) for total in totals[:4]]
    small, count = totals[4:]
    small = small.reshape(LAYERS, 16, hidden)
    root_means = jnp.sqrt(jnp.sum(small[:, 10:13, :dim], axis=-1) / (count * dim))

    def widen(values):
        return jnp.swapaxes(values, 0, 1).astype(f32)

    return (
        widen(act),
        widen(xgrad),
        g_in,
        small[:, 0, :dim],
        small[:, 1, :dim],
        g_out,
        small[:, 3, :dim],
        small[:, 4, :dim],
        small[:, 5, :dim],
        g_up,
        small[:, 6],
        g_down,
        small[:, 7, :dim],
        small[:, 8, :dim],
        small[:, 9, :dim],
        root_means,
    )


def per_device(tables, row_parts, *operands):
    local, block_tables, dim = operands[0].shape
    if tables % 2 == 0 and row_parts == 2 * block_tables and local * row_parts <= 1024:
        return table_device(tables, row_parts, *operands)
    return gathered_device(*operands)


def solution(mesh):
    placed = (
        P("rows", "tables", None),
        P(),
        P(),
        P(),
        P(),
        P(),
        P(),
        P(),
        P(),
        P(),
        P(),
        P(),
        P(),
        P(),
        P("rows", "tables", None),
        P("tables"),
        P("tables"),
    )
    return jax.shard_map(
        functools.partial(per_device, mesh.shape["tables"], mesh.shape["rows"]),
        mesh=mesh,
        in_specs=placed,
        out_specs=(
            P("rows", "tables", None),
            P("rows", "tables", None),
            P(),
            P(),
            P(),
            P(),
            P(),
            P(),
            P(),
            P(),
            P(),
            P(),
            P(),
            P(),
            P(),
            P(),
        ),
        check_vma=False,
    )
```

```python
import functools

import jax
import jax.numpy as jnp
from jax import lax
from jax.experimental import pallas as pl
from jax.experimental.pallas import tpu as pltpu
from jax.sharding import PartitionSpec as P

D = 512
HEADS = 4
LAYERS = 2


EPSILON = 1e-05
MASKED = -1e30


def norm_forward(values, gain_row, offsets):
    average = jnp.mean(values, axis=-1, keepdims=True)
    centered = values - average
    variance = jnp.mean(centered * centered, axis=-1, keepdims=True)
    inverse = lax.rsqrt(variance + EPSILON)
    normed = centered * inverse
    return (normed * gain_row + offsets, normed, inverse)


def norm_backward(upstream, normed, inverse, gain_row):
    scaled = upstream * gain_row
    average = jnp.mean(scaled, axis=-1, keepdims=True)
    projection = jnp.mean(scaled * normed, axis=-1, keepdims=True)
    return inverse * (scaled - average - normed * projection)


def gelu_exact(values):
    return jax.nn.gelu(values, approximate=False)


def split_heads(values):
    return values.reshape(values.shape[0], values.shape[1], HEADS, values.shape[2] // HEADS)


def merge_heads(values):
    return values.reshape(values.shape[0], values.shape[1], values.shape[2] * values.shape[3])


def table_scores(queries, key_rows, usable):
    scores = jnp.einsum(
        "ibhe,jbhe->bhij",
        split_heads(queries),
        split_heads(key_rows),
        preferred_element_type=jnp.float32,
    )
    return jnp.where(usable[:, None, None, :], scores, MASKED)


def row_sums(values):
    return jnp.sum(values.astype(jnp.float32), axis=(0, 1))


def gathered_device(
    tables_in,
    in_weight,
    query_bias,
    value_bias,
    out_weight,
    out_bias,
    attn_gain,
    attn_shift,
    up_weight,
    up_bias,
    down_weight,
    down_bias,
    ffn_gain,
    ffn_shift,
    cotangent,
    lengths,
    train_counts,
):
    local_rows = tables_in.shape[0]
    seq_rows = local_rows * lax.axis_size("rows")
    positions = lax.axis_index("rows") * local_rows + jnp.arange(local_rows, dtype=jnp.int32)
    valid_rows = (positions[:, None] < lengths[None, :]).astype(jnp.float32)
    valid_cells = valid_rows[:, :, None]
    usable = jnp.arange(seq_rows, dtype=jnp.int32)[None, :] < train_counts[:, None]
    score_scale = (D // HEADS) ** (-0.5)
    column_scale = jnp.concatenate(
        [jnp.full((D,), score_scale, jnp.float32), jnp.ones((2 * D,), jnp.float32)]
    )
    stream = tables_in.astype(jnp.float32)
    stored = []
    squares = []
    for layer_index in range(LAYERS):
        in_low = stream.astype(jnp.bfloat16)
        projected = jnp.einsum(
            "ibd,de->ibe", in_low, in_weight[layer_index], preferred_element_type=jnp.float32
        )
        queries = ((projected[:, :, :D] + query_bias[layer_index]) * score_scale).astype(
            jnp.bfloat16
        )
        key_rows = projected[:, :, D : 2 * D].astype(jnp.bfloat16)
        value_rows = (projected[:, :, 2 * D :] + value_bias[layer_index]).astype(jnp.bfloat16)
        all_keys, all_values = (
            lax.all_gather(key_rows, "rows", axis=0, tiled=True),
            lax.all_gather(value_rows, "rows", axis=0, tiled=True),
        )
        scores = table_scores(queries, all_keys, usable)
        row_max = jnp.max(scores, axis=-1, keepdims=True)
        exponent = jnp.exp(scores - row_max)
        row_total = jnp.sum(exponent, axis=-1, keepdims=True)
        probs_low = (exponent / row_total).astype(jnp.bfloat16)
        log_total = (row_max + jnp.log(row_total))[..., 0]
        attended = merge_heads(
            jnp.einsum(
                "bhij,jbhe->ibhe",
                probs_low,
                split_heads(all_values),
                preferred_element_type=jnp.float32,
            )
        ).astype(jnp.bfloat16)
        branch = (
            jnp.einsum(
                "ibd,de->ibe", attended, out_weight[layer_index], preferred_element_type=jnp.float32
            )
            + out_bias[layer_index]
        )
        first_out, first_norm, first_inverse = norm_forward(
            stream + branch, attn_gain[layer_index], attn_shift[layer_index]
        )
        mid_low = first_out.astype(jnp.bfloat16)
        hidden = (
            jnp.einsum(
                "ibd,df->ibf", mid_low, up_weight[layer_index], preferred_element_type=jnp.float32
            )
            + up_bias[layer_index]
        )
        act_low = gelu_exact(hidden).astype(jnp.bfloat16)
        ffn_out = (
            jnp.einsum(
                "ibf,fd->ibd", act_low, down_weight[layer_index], preferred_element_type=jnp.float32
            )
            + down_bias[layer_index]
        )
        second_out, second_norm, second_inverse = norm_forward(
            first_out + ffn_out, ffn_gain[layer_index], ffn_shift[layer_index]
        )
        squares.append(
            jnp.stack(
                [
                    jnp.sum(valid_cells * stream * stream),
                    jnp.sum(valid_cells * branch * branch),
                    jnp.sum(valid_cells * ffn_out * ffn_out),
                ]
            )
        )
        gathered = (all_keys, all_values)
        stored.append(
            (
                in_low,
                queries,
                key_rows,
                value_rows,
                gathered,
                log_total,
                attended,
                first_norm,
                first_inverse,
                mid_low,
                hidden,
                act_low,
                second_norm,
                second_inverse,
            )
        )
        stream = second_out
    activations = stream * valid_cells
    upstream = cotangent.astype(jnp.float32) * valid_cells
    layer_grads = [None] * LAYERS
    for layer_index in reversed(range(LAYERS)):
        (
            in_low,
            queries,
            key_rows,
            value_rows,
            gathered,
            log_total,
            attended,
            first_norm,
            first_inverse,
            mid_low,
            hidden,
            act_low,
            second_norm,
            second_inverse,
        ) = stored[layer_index]
        ffn_gain_grad = jnp.sum(upstream * second_norm, axis=(0, 1))
        ffn_shift_grad = jnp.sum(upstream, axis=(0, 1))
        second_grad = norm_backward(upstream, second_norm, second_inverse, ffn_gain[layer_index])
        ffn_low = second_grad.astype(jnp.bfloat16)
        down_weight_grad = jnp.einsum(
            "ibf,ibd->fd", act_low, ffn_low, preferred_element_type=jnp.float32
        )
        act_grad = jnp.einsum(
            "ibd,fd->ibf", ffn_low, down_weight[layer_index], preferred_element_type=jnp.float32
        )
        hidden_low = jax.vjp(gelu_exact, hidden)[1](act_grad)[0].astype(jnp.bfloat16)
        up_weight_grad = jnp.einsum(
            "ibd,ibf->df", mid_low, hidden_low, preferred_element_type=jnp.float32
        )
        first_grad = second_grad + jnp.einsum(
            "ibf,df->ibd", hidden_low, up_weight[layer_index], preferred_element_type=jnp.float32
        )
        attn_gain_grad = jnp.sum(first_grad * first_norm, axis=(0, 1))
        attn_shift_grad = jnp.sum(first_grad, axis=(0, 1))
        residual_grad = norm_backward(first_grad, first_norm, first_inverse, attn_gain[layer_index])
        branch_low = residual_grad.astype(jnp.bfloat16)
        out_weight_grad = jnp.einsum(
            "ibd,ibe->de", attended, branch_low, preferred_element_type=jnp.float32
        )
        attended_low = jnp.einsum(
            "ibe,de->ibd", branch_low, out_weight[layer_index], preferred_element_type=jnp.float32
        ).astype(jnp.bfloat16)
        all_keys, all_values = gathered
        scores = table_scores(queries, all_keys, usable)
        attn_probs = jnp.exp(scores - log_total[..., None])
        probs_low = attn_probs.astype(jnp.bfloat16)
        probs_grad = jnp.einsum(
            "ibhe,jbhe->bhij",
            split_heads(attended_low),
            split_heads(all_values),
            preferred_element_type=jnp.float32,
        )
        center = jnp.sum(attn_probs * probs_grad, axis=-1)
        scores_low = (attn_probs * (probs_grad - center[..., None])).astype(jnp.bfloat16)
        query_low = merge_heads(
            jnp.einsum(
                "bhij,jbhe->ibhe",
                scores_low,
                split_heads(all_keys),
                preferred_element_type=jnp.float32,
            )
        ).astype(jnp.bfloat16)
        key_part = jnp.einsum(
            "bhij,ibhe->jbhe", scores_low, split_heads(queries), preferred_element_type=jnp.float32
        )
        value_part = jnp.einsum(
            "bhij,ibhe->jbhe",
            probs_low,
            split_heads(attended_low),
            preferred_element_type=jnp.float32,
        )
        key_sums = lax.psum_scatter(
            jnp.concatenate([merge_heads(key_part), merge_heads(value_part)], axis=-1).astype(
                jnp.bfloat16
            ),
            "rows",
            scatter_dimension=0,
            tiled=True,
        )
        proj_low = jnp.concatenate([query_low, key_sums], axis=-1)
        in_weight_grad = (
            jnp.einsum("ibd,ibe->de", in_low, proj_low, preferred_element_type=jnp.float32)
            * column_scale
        )
        query_bias_grad = row_sums(query_low) * score_scale
        value_bias_grad = row_sums(proj_low[:, :, 2 * D :])
        weight_now = in_weight[layer_index]
        query_input = (
            jnp.einsum(
                "ibe,de->ibd", query_low, weight_now[:, :D], preferred_element_type=jnp.float32
            )
            * score_scale
        )
        other_input = jnp.einsum(
            "ibe,de->ibd", proj_low[:, :, D:], weight_now[:, D:], preferred_element_type=jnp.float32
        )
        upstream = residual_grad + query_input + other_input
        layer_grads[layer_index] = (
            in_weight_grad,
            query_bias_grad,
            value_bias_grad,
            out_weight_grad,
            row_sums(branch_low),
            attn_gain_grad,
            attn_shift_grad,
            up_weight_grad,
            row_sums(hidden_low),
            down_weight_grad,
            row_sums(ffn_low),
            ffn_gain_grad,
            ffn_shift_grad,
        )
    stacked = [
        jnp.stack([layer_grads[layer_index][member] for layer_index in range(LAYERS)])
        for member in range(13)
    ]
    totals = lax.psum(
        (
            stacked[0],
            stacked[1],
            stacked[2],
            stacked[3],
            stacked[4],
            stacked[5],
            stacked[6],
            stacked[7],
            stacked[8],
            stacked[9],
            stacked[10],
            stacked[11],
            stacked[12],
            jnp.stack(squares),
            jnp.sum(valid_rows),
        ),
        ("tables", "rows"),
    )
    root_means = jnp.sqrt(totals[13] / (totals[14] * D))
    return (
        activations,
        upstream,
        totals[0],
        totals[1],
        totals[2],
        totals[3],
        totals[4],
        totals[5],
        totals[6],
        totals[7],
        totals[8],
        totals[9],
        totals[10],
        totals[11],
        totals[12],
        root_means,
    )


MESH = pl.DeviceIdType.MESH
NT = (((1,), (1,)), ((), ()))
NN = (((1,), (0,)), ((), ()))
TN = (((0,), (0,)), ((), ()))
TILE = 256
VECTORS = 9
GROUPS = 2


def dot(left, right, dims=NN):
    return lax.dot_general(left, right, dims, preferred_element_type=jnp.float32)


def column_sum(values):
    return jnp.sum(values, axis=0, keepdims=True)


def row_mean(values):
    return jnp.mean(values, axis=-1, keepdims=True)


def reduce_job(part, total, recv, sems, halves, z_peers, quarter):
    rows = part.shape[0]
    offsets, sizes, copies, back = [0], [rows], [], []
    for n, (partner, bit) in enumerate(halves):
        size = sizes[-1] // 2
        keep = pl.multiple_of(offsets[-1] + bit * size, size)
        give = pl.multiple_of(offsets[-1] + (1 - bit) * size, size)
        copies.append(
            pltpu.make_async_remote_copy(
                src_ref=part.at[pl.ds(give, size)],
                dst_ref=recv[n],
                send_sem=sems.at[0, n],
                recv_sem=sems.at[1, n],
                device_id=partner,
                device_id_type=MESH,
            )
        )
        offsets.append(keep)
        sizes.append(size)
        back.append(
            pltpu.make_async_remote_copy(
                src_ref=total.at[pl.ds(keep, size)],
                dst_ref=total.at[pl.ds(keep, size)],
                send_sem=sems.at[0, 3 + n],
                recv_sem=sems.at[1, 3 + n],
                device_id=partner,
                device_id_type=MESH,
            )
        )
    size = sizes[-1] // (len(z_peers) + 1)
    base = offsets[-1]

    def piece(index):
        return pl.ds(pl.multiple_of(base + index * size, size), size)

    mine = piece(quarter)
    spread, gather = [], []
    for n, (peer, index) in enumerate(z_peers):
        spread.append(
            pltpu.make_async_remote_copy(
                src_ref=part.at[piece(index)],
                dst_ref=recv[3].at[n],
                send_sem=sems.at[0, 6 + n],
                recv_sem=sems.at[1, 6 + n],
                device_id=peer,
                device_id_type=MESH,
            )
        )
        gather.append(
            pltpu.make_async_remote_copy(
                src_ref=part.at[mine],
                dst_ref=total.at[mine],
                send_sem=sems.at[0, 9 + n],
                recv_sem=sems.at[1, 9 + n],
                device_id=peer,
                device_id_type=MESH,
            )
        )
    kept = pltpu.make_async_copy(part.at[mine], total.at[mine], sems.at[0, 12])

    def add(n):
        size = sizes[n + 1]
        step = min(size, 128)

        def chunk(i, carry):
            start = i * step
            at = pl.ds(pl.multiple_of(offsets[n + 1] + start, step), step)
            other = recv[n][pl.ds(pl.multiple_of(start, step), step), :].astype(jnp.float32)
            part[at, :] = (part[at, :].astype(jnp.float32) + other).astype(part.dtype)
            return carry

        lax.fori_loop(0, size // step, chunk, 0)

    def first():
        copies[0].start()

    def fold(n):
        def run():
            copies[n].wait()
            add(n)
            if n + 1 < len(copies):
                copies[n + 1].start()
            else:
                for copy in spread:
                    copy.start()

        return run

    def settle():
        for copy in spread:
            copy.wait()
        others = [recv[3][n].astype(jnp.float32) for n in range(len(spread))]
        own = part[mine, :].astype(jnp.float32)
        part[mine, :] = ((own + others[0]) + (others[1] + others[2])).astype(part.dtype)
        kept.start()
        for copy in gather:
            copy.start()

    def collect():
        kept.wait()
        for copy in gather:
            copy.wait()
        back[-1].start()

    def unfold(n):
        def run():
            back[n].wait()
            if n > 0:
                back[n - 1].start()

        return run

    return [first] + [fold(n) for n in range(3)] + [settle, collect] + [unfold(n) for n in (2, 1, 0)]


def small_job(part, total, recv, sems, halves, z_peers):
    offset, size, copies, back, kept_cols = 0, part.shape[1], [], [], []
    for n, (partner, bit) in enumerate(halves):
        size = size // 2
        keep = pl.ds(pl.multiple_of(offset + bit * size, size), size)
        give = pl.ds(pl.multiple_of(offset + (1 - bit) * size, size), size)
        copies.append(
            pltpu.make_async_remote_copy(
                src_ref=part.at[:, give],
                dst_ref=recv[n],
                send_sem=sems.at[0, n],
                recv_sem=sems.at[1, n],
                device_id=partner,
                device_id_type=MESH,
            )
        )
        back.append(
            pltpu.make_async_remote_copy(
                src_ref=total.at[:, keep],
                dst_ref=total.at[:, keep],
                send_sem=sems.at[0, 3 + n],
                recv_sem=sems.at[1, 3 + n],
                device_id=partner,
                device_id_type=MESH,
            )
        )
        kept_cols.append(keep)
        offset = offset + bit * size
    mine = kept_cols[-1]
    spread = [
        pltpu.make_async_remote_copy(
            src_ref=part.at[:, mine],
            dst_ref=recv[3].at[n],
            send_sem=sems.at[0, 6 + n],
            recv_sem=sems.at[1, 6 + n],
            device_id=peer,
            device_id_type=MESH,
        )
        for n, (peer, _) in enumerate(z_peers)
    ]

    def first():
        copies[0].start()

    def fold(n):
        def run():
            copies[n].wait()
            part[:, kept_cols[n]] = part[:, kept_cols[n]] + recv[n][...]
            if n + 1 < len(copies):
                copies[n + 1].start()
            else:
                for copy in spread:
                    copy.start()

        return run

    def settle():
        for copy in spread:
            copy.wait()
        total[:, mine] = (part[:, mine] + recv[3][0]) + (recv[3][1] + recv[3][2])
        back[-1].start()

    def unfold(n):
        def run():
            back[n].wait()
            if n > 0:
                back[n - 1].start()

        return run

    return [first] + [fold(n) for n in range(3)] + [settle] + [unfold(n) for n in (2, 1, 0)]


def table_kernel(
    local,
    block_tables,
    seq,
    x_hbm,
    cot_hbm,
    meta_ref,
    w_in_hbm,
    w_out_hbm,
    w_up_hbm,
    w_down_hbm,
    *refs,
):
    vector_refs, refs = refs[:VECTORS], refs[VECTORS:]
    (
        act_hbm,
        xgrad_hbm,
        t_in,
        t_out,
        t_up,
        t_down,
        t_small,
        w_in,
        w_out,
        w_up,
        w_down,
        vectors,
        g_in,
        g_out,
        g_up,
        g_down,
        small,
        in_low,
        cot_low,
        stream,
        queries,
        kv,
        attended,
        stats,
        norm1,
        inverse1,
        mid_low,
        slope,
        act_low,
        norm2,
        inverse2,
        meta,
        bias_row,
        bias_col,
        valid,
        ffn_low,
        hidden_low,
        branch_low,
        attended_low,
        stats_rows,
        dq_t,
        dkv_own,
        dkv_send,
        dkv_recv,
        proj_low,
        staged,
        recv_in,
        recv_out,
        recv_up,
        recv_down,
        recv_small,
        x_send,
        x_recv,
        cot_send,
        cot_recv,
        act_send,
        act_recv,
        xg_send,
        xg_recv,
        local_sem,
        kv_sem,
        dkv_sem,
        meta_sem,
        job_sem,
    ) = refs
    upstream = stream
    rows = block_tables * local
    dim = in_low.shape[-1]
    head_dim = dim // HEADS
    scale = head_dim**-0.5
    tiles = rows // TILE
    group_heads = HEADS // GROUPS
    group_width = group_heads * head_dim
    t = lax.axis_index("tables")
    r = lax.axis_index("rows")
    core = lax.rem(t, 2)
    side = r // block_tables
    slot = lax.rem(r, block_tables)
    peer = (t + 1 - 2 * core, r)
    own_rows = pl.multiple_of(core * rows, rows)
    peer_rows = pl.multiple_of((1 - core) * rows, rows)

    x_side, y_side, z_side = lax.rem(r, 2), t // 2, r // 2
    x_next = (t, r + 1 - 2 * x_side)
    y_next = (t + 2 - 4 * y_side, r)
    z_next = [
        (z_side + 1 - 2 * lax.rem(z_side, 2)),
        lax.rem(z_side + 2, 4),
        3 - z_side,
    ]
    z_peers = [((t, 2 * z + x_side), z) for z in z_next]

    def choose(first, second):
        return core * second + (1 - core) * first

    halves = [
        (peer, core),
        (
            (choose(x_next[0], y_next[0]), choose(x_next[1], y_next[1])),
            choose(x_side, y_side),
        ),
        (
            (choose(y_next[0], x_next[0]), choose(y_next[1], x_next[1])),
            choose(y_side, x_side),
        ),
    ]

    def partner(k):
        return (t - core + side, block_tables * core + k)

    def is_self(k):
        return jnp.logical_and(core == side, slot == k)

    barrier = pltpu.get_barrier_semaphore()
    greeted = [peer, x_next, y_next] + [device for device, _ in z_peers]
    for device in greeted:
        pl.semaphore_signal(barrier, inc=1, device_id=device, device_id_type=MESH)
    for k in range(block_tables):

        @pl.when(jnp.logical_not(is_self(k)))
        def _():
            pl.semaphore_signal(barrier, inc=1, device_id=partner(k), device_id_type=MESH)

    pl.semaphore_wait(
        barrier, len(greeted) + jnp.where(core == side, block_tables - 1, block_tables)
    )

    def spread(source, target, send_sem, recv_sem, own_sem):
        def remote(k, at):
            return pltpu.make_async_remote_copy(
                src_ref=source(k),
                dst_ref=target(at),
                send_sem=send_sem.at[k],
                recv_sem=recv_sem.at[at],
                device_id=partner(k),
                device_id_type=MESH,
            )

        def kept(k):
            return pltpu.make_async_copy(source(k), target(k), own_sem)

        def start():
            for k in range(block_tables):

                @pl.when(is_self(k))
                def _():
                    kept(k).start()

                @pl.when(jnp.logical_not(is_self(k)))
                def _():
                    remote(k, slot).start()

        def arrive():
            for k in range(block_tables):

                @pl.when(is_self(k))
                def _():
                    kept(k).wait()

                @pl.when(jnp.logical_not(is_self(k)))
                def _():
                    remote(k, k).wait_recv()

        def left():
            for k in range(block_tables):

                @pl.when(jnp.logical_not(is_self(k)))
                def _():
                    remote(k, slot).wait_send()

        return start, arrive, left

    def by_table(ref):
        return lambda k: ref.at[k]

    def by_rows(ref):
        return lambda k: ref.at[pl.ds(k * local, local)]

    x_start, x_arrive, x_left = spread(by_table(x_hbm), by_rows(in_low.at[0]), x_send, x_recv, local_sem.at[0])
    cot_start, cot_arrive, cot_left = spread(by_table(cot_hbm), by_rows(cot_low), cot_send, cot_recv, local_sem.at[1])
    act_start, act_arrive, act_left = spread(by_rows(staged.at[0]), by_table(act_hbm), act_send, act_recv, local_sem.at[2])
    xg_start, xg_arrive, xg_left = spread(by_rows(staged.at[1]), by_table(xgrad_hbm), xg_send, xg_recv, local_sem.at[3])

    def swap(source, target, sems):
        return pltpu.make_async_remote_copy(
            src_ref=source,
            dst_ref=target,
            send_sem=sems.at[0],
            recv_sem=sems.at[1],
            device_id=peer,
            device_id_type=MESH,
        )

    x_start()
    loads = [
        pltpu.make_async_copy(source, target, local_sem.at[5 + n])
        for n, (source, target) in enumerate(
            ((w_in_hbm, w_in), (w_out_hbm, w_out), (w_up_hbm, w_up), (w_down_hbm, w_down))
        )
    ]
    for load in loads:
        load.start()
    cot_start()
    for n, ref in enumerate(vector_refs):
        for layer in range(LAYERS):
            vectors[pl.ds(layer * VECTORS + n, 1), pl.ds(0, ref.shape[1])] = ref[...].astype(
                jnp.float32
            )[layer : layer + 1, :]
    meta_own = pltpu.make_async_copy(meta_ref, meta.at[core], local_sem.at[4])
    meta_own.start()
    meta_copy = swap(meta_ref, meta.at[core], meta_sem)
    meta_copy.start()

    small[...] = jnp.zeros_like(small)
    meta_own.wait()
    meta_copy.wait()
    length = meta[side, pl.ds(slot, 1), :][:, :1]
    train = meta[side, pl.ds(slot + block_tables, 1), :][:, :1]
    bias_row[...] = jnp.where(lax.broadcasted_iota(jnp.int32, (1, seq), 1) < train, 0.0, MASKED)
    bias_col[...] = jnp.where(lax.broadcasted_iota(jnp.int32, (seq, 1), 0) < train, 0.0, MASKED)
    valid[...] = jnp.where(
        lax.broadcasted_iota(jnp.int32, (rows, 1), 0) + core * rows < length, 1.0, 0.0
    )
    small[0, pl.ds(13, 1), pl.ds(0, 128)] = jnp.broadcast_to(column_sum(valid[...]), (1, 128))
    x_arrive()
    loads[0].wait()

    def vector(index, layer, width):
        return vectors[pl.ds(layer * VECTORS + index, 1), pl.ds(0, width)]

    def add_small(layer, index, values):
        at = (layer, pl.ds(index, 1), pl.ds(0, values.shape[-1]))
        small[at] = small[at] + values

    def each_tile(body):
        def step(i, carry):
            body(pl.ds(pl.multiple_of(i * TILE, TILE), TILE))
            return carry

        lax.fori_loop(0, tiles, step, 0)

    def head_cols(h):
        return pl.ds(pl.multiple_of(h * head_dim, head_dim), head_dim)

    def forward(layer):
        def project(at):
            projected = dot(in_low[layer, at, :], w_in[layer])
            queries[layer, at, :] = (
                (projected[:, :dim] + vector(0, layer, dim)) * scale
            ).astype(jnp.bfloat16)
            own = pl.ds(pl.multiple_of(own_rows + at.start, TILE), TILE)
            kv[layer, own, pl.ds(0, dim)] = projected[:, dim : 2 * dim].astype(jnp.bfloat16)
            kv[layer, own, pl.ds(dim, dim)] = (
                projected[:, 2 * dim :] + vector(1, layer, dim)
            ).astype(jnp.bfloat16)

        each_tile(project)
        mine = kv.at[layer, pl.ds(own_rows, rows)]
        kv_copy = swap(mine, mine, kv_sem.at[layer])
        kv_copy.start()
        kv_copy.wait()

        def attend(step, carry):
            h = step // tiles
            at = pl.ds(pl.multiple_of(lax.rem(step, tiles) * TILE, TILE), TILE)
            cols = head_cols(h)
            key_rows = kv[layer, :, cols]
            value_rows = kv[layer, :, pl.ds(pl.multiple_of(dim + h * head_dim, head_dim), head_dim)]
            scores = dot(queries[layer, at, cols], key_rows, NT) + bias_row[...]
            row_max = jnp.max(scores, axis=-1, keepdims=True)
            exponent = jnp.exp(scores - row_max)
            total = jnp.sum(exponent, axis=-1, keepdims=True)
            probs = (exponent * (1.0 / total)).astype(jnp.bfloat16)
            attended[layer, at, cols] = dot(probs, value_rows).astype(jnp.bfloat16)
            lane = lax.broadcasted_iota(jnp.int32, (TILE, head_dim), 1)
            kept = jnp.where(h == 0, jnp.zeros((TILE, head_dim), jnp.float32), stats[layer, at, :])
            stats[layer, at, :] = jnp.where(lane == h, row_max + jnp.log(total), kept)
            return carry

        lax.fori_loop(0, HEADS * tiles, attend, 0)
        if layer == 0:
            for load in loads[1:]:
                load.wait()

        def dense(at):
            below = in_low[0, at, :].astype(jnp.float32) if layer == 0 else stream[at, :]
            branch = dot(attended[layer, at, :], w_out[layer]) + vector(2, layer, dim)
            valid_cells = valid[at, :]
            add_small(layer, 10, column_sum(below * below * valid_cells))
            add_small(layer, 11, column_sum(branch * branch * valid_cells))
            summed = below + branch
            centered = summed - row_mean(summed)
            inverse = lax.rsqrt(row_mean(centered * centered) + EPSILON)
            normed = centered * inverse
            norm1[layer, at, :] = normed
            inverse1[layer, at, :] = inverse
            first_out = normed * vector(3, layer, dim) + vector(4, layer, dim)
            mid = first_out.astype(jnp.bfloat16)
            mid_low[layer, at, :] = mid
            hidden = dot(mid, w_up[layer]) + vector(5, layer, 2 * dim)
            cdf = 0.5 + 0.5 * lax.erf(hidden * (0.5**0.5))
            slope[layer, at, :] = cdf + hidden * (
                jnp.exp(hidden * hidden * -0.5) * 0.3989422804014327
            )
            act = (hidden * cdf).astype(jnp.bfloat16)
            act_low[layer, at, :] = act
            ffn_out = dot(act, w_down[layer]) + vector(6, layer, dim)
            add_small(layer, 12, column_sum(ffn_out * ffn_out * valid_cells))
            summed = first_out + ffn_out
            centered = summed - row_mean(summed)
            inverse = lax.rsqrt(row_mean(centered * centered) + EPSILON)
            normed = centered * inverse
            norm2[layer, at, :] = normed
            inverse2[layer, at, :] = inverse
            out = normed * vector(7, layer, dim) + vector(8, layer, dim)
            if layer + 1 < LAYERS:
                stream[at, :] = out
                in_low[layer + 1, at, :] = out.astype(jnp.bfloat16)
            else:
                staged[0, at, :] = (out * valid_cells).astype(jnp.bfloat16)

        each_tile(dense)

    for layer in range(LAYERS):
        forward(layer)
    act_start()
    cot_arrive()

    jobs = []

    def begin(steps):
        jobs.append(list(steps))
        jobs[-1].pop(0)()

    def tick():
        for steps in jobs:
            if steps:
                steps.pop(0)()

    def job(index, part, total, recv):
        return reduce_job(part, total, recv, job_sem.at[index], halves, z_peers, z_side)

    def backward(layer):
        first_job = (LAYERS - 1 - layer) * 6

        def recv_of(refs):
            return [ref.at[layer] for ref in refs]

        def enter(at):
            if layer == LAYERS - 1:
                up = cot_low[at, :].astype(jnp.float32) * valid[at, :]
            else:
                up = upstream[at, :]
            normed = norm2[layer, at, :]
            add_small(layer, 8, column_sum(up * normed))
            add_small(layer, 9, column_sum(up))
            scaled = up * vector(7, layer, dim)
            second = inverse2[layer, at, :] * (
                scaled - row_mean(scaled) - normed * row_mean(scaled * normed)
            )
            upstream[at, :] = second
            ffn = second.astype(jnp.bfloat16)
            ffn_low[at, :] = ffn
            add_small(layer, 7, column_sum(ffn.astype(jnp.float32)))

        each_tile(enter)
        g_down[layer] = dot(act_low[layer], ffn_low[...], TN).astype(jnp.bfloat16)
        tick()
        begin(job(first_job, g_down.at[layer], t_down.at[layer], recv_of(recv_down)))

        def dense(at):
            hidden = (dot(ffn_low[at, :], w_down[layer], NT) * slope[layer, at, :]).astype(
                jnp.bfloat16
            )
            hidden_low[at, :] = hidden
            add_small(layer, 6, column_sum(hidden.astype(jnp.float32)))
            first = upstream[at, :] + dot(hidden, w_up[layer], NT)
            normed = norm1[layer, at, :]
            add_small(layer, 4, column_sum(first * normed))
            add_small(layer, 5, column_sum(first))
            scaled = first * vector(3, layer, dim)
            residual = inverse1[layer, at, :] * (
                scaled - row_mean(scaled) - normed * row_mean(scaled * normed)
            )
            upstream[at, :] = residual
            branch = residual.astype(jnp.bfloat16)
            branch_low[at, :] = branch
            add_small(layer, 3, column_sum(branch.astype(jnp.float32)))
            low = dot(branch, w_out[layer], NT).astype(jnp.bfloat16)
            attended_low[at, :] = low
            product = low.astype(jnp.float32) * attended[layer, at, :].astype(jnp.float32)
            lane = lax.broadcasted_iota(jnp.int32, (TILE, head_dim), 1)
            held = stats[layer, at, :]
            for h in range(HEADS):
                center = jnp.sum(product[:, h * head_dim : (h + 1) * head_dim], axis=-1, keepdims=True)
                held = jnp.where(lane == HEADS + h, center, held)
            stats_rows[:, at] = jnp.transpose(held)[: 2 * HEADS, :]

        each_tile(dense)
        tick()
        g_up[layer] = dot(mid_low[layer], hidden_low[...], TN).astype(jnp.bfloat16)
        begin(job(first_job + 1, g_up.at[layer], t_up.at[layer], recv_of(recv_up)))
        g_out[layer] = dot(attended[layer], branch_low[...], TN).astype(jnp.bfloat16)
        tick()
        begin(job(first_job + 2, g_out.at[layer], t_out.at[layer], recv_of(recv_out)))

        def attend(group, base, first, keep):
            def step(i, carry):
                h = group * group_heads + i // tiles
                j = pl.multiple_of(lax.rem(i, tiles) * TILE, TILE)
                at = pl.ds(pl.multiple_of(base + j, TILE), TILE)
                cols = head_cols(h)
                value_cols = pl.ds(pl.multiple_of(dim + h * head_dim, head_dim), head_dim)
                key_rows = kv[layer, at, cols]
                query_rows = queries[layer, :, cols]
                grads = attended_low[:, cols]
                probs = jnp.exp(
                    dot(key_rows, query_rows, NT) + bias_col[at, :] - stats_rows[pl.ds(h, 1), :]
                )
                value_part = dot(probs.astype(jnp.bfloat16), grads)
                probs_grad = dot(kv[layer, at, value_cols], grads, NT)
                scores_low = (probs * (probs_grad - stats_rows[pl.ds(HEADS + h, 1), :])).astype(
                    jnp.bfloat16
                )
                key_part = dot(scores_low, query_rows)
                query_part = dot(key_rows, scores_low, TN)
                if first:
                    query_part = jnp.where(j == 0, query_part, query_part + dq_t[cols, :])
                else:
                    query_part = query_part + dq_t[cols, :]
                dq_t[cols, :] = query_part
                inside = i // tiles * head_dim
                keep(pl.ds(j, TILE), pl.ds(pl.multiple_of(inside, head_dim), head_dim), key_part)
                keep(
                    pl.ds(j, TILE),
                    pl.ds(pl.multiple_of(group_width + inside, head_dim), head_dim),
                    value_part,
                )
                return carry

            lax.fori_loop(0, group_heads * tiles, step, 0)

        for group in range(GROUPS):

            def keep_sent(at, cols, part):
                dkv_send[layer, group, at, cols] = part.astype(jnp.bfloat16)

            def keep_own(at, cols, part):
                dkv_own[at, cols] = part

            attend(group, peer_rows, True, keep_sent)
            copy = swap(
                dkv_send.at[layer, group], dkv_recv.at[layer, group], dkv_sem.at[layer, group]
            )
            copy.start()
            tick()
            attend(group, own_rows, False, keep_own)
            tick()
            copy.wait()

            def finish(at):
                group_rows = pl.ds(group * group_width, group_width)
                query = jnp.transpose(dq_t[group_rows, at]).astype(jnp.bfloat16)
                pair = (dkv_own[at, :] + dkv_recv[layer, group, at, :].astype(jnp.float32)).astype(
                    jnp.bfloat16
                )
                proj_low[group, at, pl.ds(0, group_width)] = query
                proj_low[group, at, pl.ds(group_width, 2 * group_width)] = pair
                cols = pl.ds(group * group_width, group_width)
                small[layer, pl.ds(0, 1), cols] += column_sum(query.astype(jnp.float32)) * scale
                small[layer, pl.ds(1, 1), cols] += column_sum(
                    pair[:, group_width:].astype(jnp.float32)
                )

            each_tile(finish)
            grad = dot(in_low[layer], proj_low[group], TN)
            g_in[layer, group, :, pl.ds(0, group_width)] = (grad[:, :group_width] * scale).astype(
                jnp.bfloat16
            )
            g_in[layer, group, :, pl.ds(group_width, 2 * group_width)] = grad[
                :, group_width:
            ].astype(jnp.bfloat16)
            begin(
                job(
                    first_job + 3 + group,
                    g_in.at[layer, group],
                    t_in.at[layer, group],
                    [ref.at[layer, group] for ref in recv_in],
                )
            )
        begin(
            small_job(
                small.at[layer],
                t_small.at[layer],
                [ref.at[layer] for ref in recv_small],
                job_sem.at[first_job + 5],
                halves,
                z_peers,
            )
        )

        def pass_down(at):
            grad = upstream[at, :]
            for group in range(GROUPS):
                for n in range(3):
                    part = dot(
                        proj_low[group, at, pl.ds(n * group_width, group_width)],
                        w_in[layer, :, pl.ds(n * dim + group * group_width, group_width)],
                        NT,
                    )
                    grad = grad + (part * scale if n == 0 else part)
            if layer > 0:
                upstream[at, :] = grad
            else:
                staged[1, at, :] = grad.astype(jnp.bfloat16)

        each_tile(pass_down)
        if layer == 0:
            xg_start()
        tick()

    for layer in reversed(range(LAYERS)):
        backward(layer)
    while any(jobs):
        tick()
    act_arrive()
    xg_arrive()
    x_left()
    cot_left()
    act_left()
    xg_left()


def widen_kernel(f_in, f_out, f_up, f_down, f_act, f_xgrad, small, *outs):
    act, xgrad, in_weight, out_weight, up_weight, down_weight, root_means = outs[:7]
    groups, width = f_in.shape[1], f_in.shape[3] // 3
    for group in range(groups):
        for n in range(3):
            in_weight[0, :, pl.ds((n * groups + group) * width, width)] = f_in[
                0, group, :, pl.ds(n * width, width)
            ].astype(jnp.float32)
    out_weight[...] = f_out[...].astype(jnp.float32)
    up_weight[...] = f_up[...].astype(jnp.float32)
    down_weight[...] = f_down[...].astype(jnp.float32)
    for k in range(f_act.shape[0]):
        act[:, k, :] = f_act[k].astype(jnp.float32)
        xgrad[:, k, :] = f_xgrad[k].astype(jnp.float32)

    @pl.when(pl.program_id(0) == 0)
    def _():
        for ref, row in zip(outs[7:], (0, 1, 3, 4, 5, 6, 7, 8, 9)):
            for layer in range(LAYERS):
                ref[pl.ds(layer, 1), :] = small[layer, pl.ds(row, 1), pl.ds(0, ref.shape[1])]
        dim = f_act.shape[2]
        count = small[0, pl.ds(13, 1), pl.ds(0, 1)]
        for layer in range(LAYERS):
            sums = jnp.sum(small[layer, pl.ds(8, 8), pl.ds(0, dim)], axis=-1, keepdims=True)
            for n in range(3):
                root_means[pl.ds(layer, 1), pl.ds(n, 1)] = jnp.sqrt(
                    sums[2 + n : 3 + n, :] / (count * dim)
                )


def table_device(tables, row_parts, *operands):
    (
        tables_in,
        in_weight,
        query_bias,
        value_bias,
        out_weight,
        out_bias,
        attn_gain,
        attn_shift,
        up_weight,
        up_bias,
        down_weight,
        down_bias,
        ffn_gain,
        ffn_shift,
        cotangent,
        lengths,
        train_counts,
    ) = operands
    local, block_tables, dim = tables_in.shape
    rows = local * block_tables
    seq = local * row_parts
    hidden = up_weight.shape[-1]
    head_dim = dim // HEADS
    f32, bf16 = jnp.float32, jnp.bfloat16
    groups = GROUPS
    meta = jnp.broadcast_to(jnp.concatenate([lengths, train_counts])[:, None], (2 * block_tables, 128))
    vmem = pl.BlockSpec(memory_space=pltpu.VMEM)
    hbm = pl.BlockSpec(memory_space=pl.ANY)
    block = (block_tables, local, dim)
    dma = pltpu.SemaphoreType.DMA
    in_part = (LAYERS, groups, dim, 3 * dim // groups)
    shards = 8 * row_parts // 2

    def received(shape):
        lead, (height, width) = shape[:-2], shape[-2:]
        return [
            [pltpu.VMEM(lead + (height // n, width), bf16) for n in (2, 4, 8)]
            + [pltpu.VMEM(lead + (3, height // shards, width), bf16)]
        ]

    act, xgrad, *sums, small = pl.pallas_call(
        functools.partial(table_kernel, local, block_tables, seq),
        out_shape=(
            jax.ShapeDtypeStruct(block, bf16),
            jax.ShapeDtypeStruct(block, bf16),
            jax.ShapeDtypeStruct(in_part, bf16),
            jax.ShapeDtypeStruct(out_weight.shape, bf16),
            jax.ShapeDtypeStruct(up_weight.shape, bf16),
            jax.ShapeDtypeStruct(down_weight.shape, bf16),
            jax.ShapeDtypeStruct((LAYERS, 16, hidden), f32),
        ),
        in_specs=[hbm, hbm, vmem] + [hbm] * 4 + [vmem] * VECTORS,
        out_specs=(hbm,) * 6 + (vmem,),
        scratch_shapes=[
            pltpu.VMEM(in_weight.shape, bf16),
            pltpu.VMEM(out_weight.shape, bf16),
            pltpu.VMEM(up_weight.shape, bf16),
            pltpu.VMEM(down_weight.shape, bf16),
            pltpu.VMEM((LAYERS * VECTORS, hidden), f32),
            pltpu.VMEM(in_part, bf16),
            pltpu.VMEM(out_weight.shape, bf16),
            pltpu.VMEM(up_weight.shape, bf16),
            pltpu.VMEM(down_weight.shape, bf16),
            pltpu.VMEM((LAYERS, 16, hidden), f32),
            pltpu.VMEM((LAYERS, rows, dim), bf16),
            pltpu.VMEM((rows, dim), bf16),
            pltpu.VMEM((rows, dim), f32),
            pltpu.VMEM((LAYERS, rows, dim), bf16),
            pltpu.VMEM((LAYERS, seq, 2 * dim), bf16),
            pltpu.VMEM((LAYERS, rows, dim), bf16),
            pltpu.VMEM((LAYERS, rows, head_dim), f32),
            pltpu.VMEM((LAYERS, rows, dim), f32),
            pltpu.VMEM((LAYERS, rows, 1), f32),
            pltpu.VMEM((LAYERS, rows, dim), bf16),
            pltpu.VMEM((LAYERS, rows, hidden), f32),
            pltpu.VMEM((LAYERS, rows, hidden), bf16),
            pltpu.VMEM((LAYERS, rows, dim), f32),
            pltpu.VMEM((LAYERS, rows, 1), f32),
            pltpu.VMEM((2, 2 * block_tables, 128), jnp.int32),
            pltpu.VMEM((1, seq), f32),
            pltpu.VMEM((seq, 1), f32),
            pltpu.VMEM((rows, 1), f32),
            pltpu.VMEM((rows, dim), bf16),
            pltpu.VMEM((rows, hidden), bf16),
            pltpu.VMEM((rows, dim), bf16),
            pltpu.VMEM((rows, dim), bf16),
            pltpu.VMEM((2 * HEADS, rows), f32),
            pltpu.VMEM((dim, rows), f32),
            pltpu.VMEM((rows, 2 * dim // groups), f32),
            pltpu.VMEM((LAYERS, groups, rows, 2 * dim // groups), bf16),
            pltpu.VMEM((LAYERS, groups, rows, 2 * dim // groups), bf16),
            pltpu.VMEM((groups, rows, 3 * dim // groups), bf16),
            pltpu.VMEM((2, rows, dim), bf16),
        ]
        + received(in_part)
        + received(out_weight.shape)
        + received(up_weight.shape)
        + received(down_weight.shape)
        + [
            [pltpu.VMEM((LAYERS, 16, hidden // n), f32) for n in (2, 4, 8)]
            + [pltpu.VMEM((LAYERS, 3, 16, hidden // 8), f32)]
        ]
        + [dma((block_tables,))] * 8
        + [
            dma((9,)),
            dma((LAYERS, 2)),
            dma((LAYERS, groups, 2)),
            dma((2,)),
            dma((LAYERS * 6, 2, 13)),
        ],
        compiler_params=pltpu.CompilerParams(
            collective_id=0, has_side_effects=True, vmem_limit_bytes=62 * 1024 * 1024
        ),
    )(
        jnp.swapaxes(tables_in, 0, 1),
        jnp.swapaxes(cotangent, 0, 1),
        meta,
        in_weight,
        out_weight,
        up_weight,
        down_weight,
        query_bias,
        value_bias,
        out_bias,
        attn_gain,
        attn_shift,
        up_bias,
        down_bias,
        ffn_gain,
        ffn_shift,
    )
    steps = 4

    def whole(shape):
        return pl.BlockSpec(shape, lambda l, i: (0,) * len(shape))

    def sliced(height, width):
        return pl.BlockSpec((1, height // steps, width), lambda l, i: (l, i, 0))

    weights = [
        sliced(dim, 3 * dim),
        sliced(dim, dim),
        sliced(dim, hidden),
        sliced(hidden, dim),
    ]
    cut = local // (LAYERS * steps)
    table_rows = pl.BlockSpec((block_tables, cut, dim), lambda l, i: (0, l * steps + i, 0))
    row_tables = pl.BlockSpec((cut, block_tables, dim), lambda l, i: (l * steps + i, 0, 0))
    vector = jax.ShapeDtypeStruct((LAYERS, dim), f32)
    wide_vector = jax.ShapeDtypeStruct((LAYERS, hidden), f32)
    shapes = [
        jax.ShapeDtypeStruct(tables_in.shape, f32),
        jax.ShapeDtypeStruct(tables_in.shape, f32),
        jax.ShapeDtypeStruct(in_weight.shape, f32),
        jax.ShapeDtypeStruct(out_weight.shape, f32),
        jax.ShapeDtypeStruct(up_weight.shape, f32),
        jax.ShapeDtypeStruct(down_weight.shape, f32),
        jax.ShapeDtypeStruct((LAYERS, 3), f32),
    ] + [vector] * 5 + [wide_vector] + [vector] * 3
    outs = pl.pallas_call(
        widen_kernel,
        grid=(LAYERS, steps),
        out_shape=shapes,
        in_specs=[
            pl.BlockSpec((1, groups, dim // steps, 3 * dim // groups), lambda l, i: (l, 0, i, 0)),
            *weights[1:],
            table_rows,
            table_rows,
            whole((LAYERS, 16, hidden)),
        ],
        out_specs=[row_tables, row_tables, *weights] + [whole(s.shape) for s in shapes[6:]],
        compiler_params=pltpu.CompilerParams(vmem_limit_bytes=48 * 1024 * 1024),
    )(*sums, act, xgrad, small)
    act, xgrad, g_in, g_out, g_up, g_down, root_means = outs[:7]
    query, value, out, gain1, shift1, up, down, gain2, shift2 = outs[7:]
    return (
        act,
        xgrad,
        g_in,
        query,
        value,
        g_out,
        out,
        gain1,
        shift1,
        g_up,
        up,
        g_down,
        down,
        gain2,
        shift2,
        root_means,
    )


def per_device(tables, row_parts, *operands):
    local, block_tables, dim = operands[0].shape
    if tables == 4 and row_parts == 2 * block_tables and local * row_parts <= 1024:
        return table_device(tables, row_parts, *operands)
    return gathered_device(*operands)


def solution(mesh):
    placed = (
        P("rows", "tables", None),
        P(),
        P(),
        P(),
        P(),
        P(),
        P(),
        P(),
        P(),
        P(),
        P(),
        P(),
        P(),
        P(),
        P("rows", "tables", None),
        P("tables"),
        P("tables"),
    )
    return jax.shard_map(
        functools.partial(per_device, mesh.shape["tables"], mesh.shape["rows"]),
        mesh=mesh,
        in_specs=placed,
        out_specs=(
            P("rows", "tables", None),
            P("rows", "tables", None),
            P(),
            P(),
            P(),
            P(),
            P(),
            P(),
            P(),
            P(),
            P(),
            P(),
            P(),
            P(),
            P(),
            P(),
        ),
        check_vma=False,
    )
```

```python
import functools

import jax
import jax.numpy as jnp
from jax import lax
from jax.experimental import pallas as pl
from jax.experimental.pallas import tpu as pltpu
from jax.sharding import PartitionSpec as P

D = 512
HEADS = 4
LAYERS = 2


EPSILON = 1e-05
MASKED = -1e30


def norm_forward(values, gain_row, offsets):
    average = jnp.mean(values, axis=-1, keepdims=True)
    centered = values - average
    variance = jnp.mean(centered * centered, axis=-1, keepdims=True)
    inverse = lax.rsqrt(variance + EPSILON)
    normed = centered * inverse
    return (normed * gain_row + offsets, normed, inverse)


def norm_backward(upstream, normed, inverse, gain_row):
    scaled = upstream * gain_row
    average = jnp.mean(scaled, axis=-1, keepdims=True)
    projection = jnp.mean(scaled * normed, axis=-1, keepdims=True)
    return inverse * (scaled - average - normed * projection)


def gelu_exact(values):
    return jax.nn.gelu(values, approximate=False)


def split_heads(values):
    return values.reshape(values.shape[0], values.shape[1], HEADS, values.shape[2] // HEADS)


def merge_heads(values):
    return values.reshape(values.shape[0], values.shape[1], values.shape[2] * values.shape[3])


def table_scores(queries, key_rows, usable):
    scores = jnp.einsum(
        "ibhe,jbhe->bhij",
        split_heads(queries),
        split_heads(key_rows),
        preferred_element_type=jnp.float32,
    )
    return jnp.where(usable[:, None, None, :], scores, MASKED)


def row_sums(values):
    return jnp.sum(values.astype(jnp.float32), axis=(0, 1))


def gathered_device(
    tables_in,
    in_weight,
    query_bias,
    value_bias,
    out_weight,
    out_bias,
    attn_gain,
    attn_shift,
    up_weight,
    up_bias,
    down_weight,
    down_bias,
    ffn_gain,
    ffn_shift,
    cotangent,
    lengths,
    train_counts,
):
    local_rows = tables_in.shape[0]
    seq_rows = local_rows * lax.axis_size("rows")
    positions = lax.axis_index("rows") * local_rows + jnp.arange(local_rows, dtype=jnp.int32)
    valid_rows = (positions[:, None] < lengths[None, :]).astype(jnp.float32)
    valid_cells = valid_rows[:, :, None]
    usable = jnp.arange(seq_rows, dtype=jnp.int32)[None, :] < train_counts[:, None]
    score_scale = (D // HEADS) ** (-0.5)
    column_scale = jnp.concatenate(
        [jnp.full((D,), score_scale, jnp.float32), jnp.ones((2 * D,), jnp.float32)]
    )
    stream = tables_in.astype(jnp.float32)
    stored = []
    squares = []
    for layer_index in range(LAYERS):
        in_low = stream.astype(jnp.bfloat16)
        projected = jnp.einsum(
            "ibd,de->ibe", in_low, in_weight[layer_index], preferred_element_type=jnp.float32
        )
        queries = ((projected[:, :, :D] + query_bias[layer_index]) * score_scale).astype(
            jnp.bfloat16
        )
        key_rows = projected[:, :, D : 2 * D].astype(jnp.bfloat16)
        value_rows = (projected[:, :, 2 * D :] + value_bias[layer_index]).astype(jnp.bfloat16)
        all_keys, all_values = (
            lax.all_gather(key_rows, "rows", axis=0, tiled=True),
            lax.all_gather(value_rows, "rows", axis=0, tiled=True),
        )
        scores = table_scores(queries, all_keys, usable)
        row_max = jnp.max(scores, axis=-1, keepdims=True)
        exponent = jnp.exp(scores - row_max)
        row_total = jnp.sum(exponent, axis=-1, keepdims=True)
        probs_low = (exponent / row_total).astype(jnp.bfloat16)
        log_total = (row_max + jnp.log(row_total))[..., 0]
        attended = merge_heads(
            jnp.einsum(
                "bhij,jbhe->ibhe",
                probs_low,
                split_heads(all_values),
                preferred_element_type=jnp.float32,
            )
        ).astype(jnp.bfloat16)
        branch = (
            jnp.einsum(
                "ibd,de->ibe", attended, out_weight[layer_index], preferred_element_type=jnp.float32
            )
            + out_bias[layer_index]
        )
        first_out, first_norm, first_inverse = norm_forward(
            stream + branch, attn_gain[layer_index], attn_shift[layer_index]
        )
        mid_low = first_out.astype(jnp.bfloat16)
        hidden = (
            jnp.einsum(
                "ibd,df->ibf", mid_low, up_weight[layer_index], preferred_element_type=jnp.float32
            )
            + up_bias[layer_index]
        )
        act_low = gelu_exact(hidden).astype(jnp.bfloat16)
        ffn_out = (
            jnp.einsum(
                "ibf,fd->ibd", act_low, down_weight[layer_index], preferred_element_type=jnp.float32
            )
            + down_bias[layer_index]
        )
        second_out, second_norm, second_inverse = norm_forward(
            first_out + ffn_out, ffn_gain[layer_index], ffn_shift[layer_index]
        )
        squares.append(
            jnp.stack(
                [
                    jnp.sum(valid_cells * stream * stream),
                    jnp.sum(valid_cells * branch * branch),
                    jnp.sum(valid_cells * ffn_out * ffn_out),
                ]
            )
        )
        gathered = (all_keys, all_values)
        stored.append(
            (
                in_low,
                queries,
                key_rows,
                value_rows,
                gathered,
                log_total,
                attended,
                first_norm,
                first_inverse,
                mid_low,
                hidden,
                act_low,
                second_norm,
                second_inverse,
            )
        )
        stream = second_out
    activations = stream * valid_cells
    upstream = cotangent.astype(jnp.float32) * valid_cells
    layer_grads = [None] * LAYERS
    for layer_index in reversed(range(LAYERS)):
        (
            in_low,
            queries,
            key_rows,
            value_rows,
            gathered,
            log_total,
            attended,
            first_norm,
            first_inverse,
            mid_low,
            hidden,
            act_low,
            second_norm,
            second_inverse,
        ) = stored[layer_index]
        ffn_gain_grad = jnp.sum(upstream * second_norm, axis=(0, 1))
        ffn_shift_grad = jnp.sum(upstream, axis=(0, 1))
        second_grad = norm_backward(upstream, second_norm, second_inverse, ffn_gain[layer_index])
        ffn_low = second_grad.astype(jnp.bfloat16)
        down_weight_grad = jnp.einsum(
            "ibf,ibd->fd", act_low, ffn_low, preferred_element_type=jnp.float32
        )
        act_grad = jnp.einsum(
            "ibd,fd->ibf", ffn_low, down_weight[layer_index], preferred_element_type=jnp.float32
        )
        hidden_low = jax.vjp(gelu_exact, hidden)[1](act_grad)[0].astype(jnp.bfloat16)
        up_weight_grad = jnp.einsum(
            "ibd,ibf->df", mid_low, hidden_low, preferred_element_type=jnp.float32
        )
        first_grad = second_grad + jnp.einsum(
            "ibf,df->ibd", hidden_low, up_weight[layer_index], preferred_element_type=jnp.float32
        )
        attn_gain_grad = jnp.sum(first_grad * first_norm, axis=(0, 1))
        attn_shift_grad = jnp.sum(first_grad, axis=(0, 1))
        residual_grad = norm_backward(first_grad, first_norm, first_inverse, attn_gain[layer_index])
        branch_low = residual_grad.astype(jnp.bfloat16)
        out_weight_grad = jnp.einsum(
            "ibd,ibe->de", attended, branch_low, preferred_element_type=jnp.float32
        )
        attended_low = jnp.einsum(
            "ibe,de->ibd", branch_low, out_weight[layer_index], preferred_element_type=jnp.float32
        ).astype(jnp.bfloat16)
        all_keys, all_values = gathered
        scores = table_scores(queries, all_keys, usable)
        attn_probs = jnp.exp(scores - log_total[..., None])
        probs_low = attn_probs.astype(jnp.bfloat16)
        probs_grad = jnp.einsum(
            "ibhe,jbhe->bhij",
            split_heads(attended_low),
            split_heads(all_values),
            preferred_element_type=jnp.float32,
        )
        center = jnp.sum(attn_probs * probs_grad, axis=-1)
        scores_low = (attn_probs * (probs_grad - center[..., None])).astype(jnp.bfloat16)
        query_low = merge_heads(
            jnp.einsum(
                "bhij,jbhe->ibhe",
                scores_low,
                split_heads(all_keys),
                preferred_element_type=jnp.float32,
            )
        ).astype(jnp.bfloat16)
        key_part = jnp.einsum(
            "bhij,ibhe->jbhe", scores_low, split_heads(queries), preferred_element_type=jnp.float32
        )
        value_part = jnp.einsum(
            "bhij,ibhe->jbhe",
            probs_low,
            split_heads(attended_low),
            preferred_element_type=jnp.float32,
        )
        key_sums = lax.psum_scatter(
            jnp.concatenate([merge_heads(key_part), merge_heads(value_part)], axis=-1).astype(
                jnp.bfloat16
            ),
            "rows",
            scatter_dimension=0,
            tiled=True,
        )
        proj_low = jnp.concatenate([query_low, key_sums], axis=-1)
        in_weight_grad = (
            jnp.einsum("ibd,ibe->de", in_low, proj_low, preferred_element_type=jnp.float32)
            * column_scale
        )
        query_bias_grad = row_sums(query_low) * score_scale
        value_bias_grad = row_sums(proj_low[:, :, 2 * D :])
        weight_now = in_weight[layer_index]
        query_input = (
            jnp.einsum(
                "ibe,de->ibd", query_low, weight_now[:, :D], preferred_element_type=jnp.float32
            )
            * score_scale
        )
        other_input = jnp.einsum(
            "ibe,de->ibd", proj_low[:, :, D:], weight_now[:, D:], preferred_element_type=jnp.float32
        )
        upstream = residual_grad + query_input + other_input
        layer_grads[layer_index] = (
            in_weight_grad,
            query_bias_grad,
            value_bias_grad,
            out_weight_grad,
            row_sums(branch_low),
            attn_gain_grad,
            attn_shift_grad,
            up_weight_grad,
            row_sums(hidden_low),
            down_weight_grad,
            row_sums(ffn_low),
            ffn_gain_grad,
            ffn_shift_grad,
        )
    stacked = [
        jnp.stack([layer_grads[layer_index][member] for layer_index in range(LAYERS)])
        for member in range(13)
    ]
    totals = lax.psum(
        (
            stacked[0],
            stacked[1],
            stacked[2],
            stacked[3],
            stacked[4],
            stacked[5],
            stacked[6],
            stacked[7],
            stacked[8],
            stacked[9],
            stacked[10],
            stacked[11],
            stacked[12],
            jnp.stack(squares),
            jnp.sum(valid_rows),
        ),
        ("tables", "rows"),
    )
    root_means = jnp.sqrt(totals[13] / (totals[14] * D))
    return (
        activations,
        upstream,
        totals[0],
        totals[1],
        totals[2],
        totals[3],
        totals[4],
        totals[5],
        totals[6],
        totals[7],
        totals[8],
        totals[9],
        totals[10],
        totals[11],
        totals[12],
        root_means,
    )


MESH = pl.DeviceIdType.MESH
NT = (((1,), (1,)), ((), ()))
NN = (((1,), (0,)), ((), ()))
TN = (((0,), (0,)), ((), ()))
TILE = 256
VECTORS = 9
GROUPS = 4
HALVES = 2
SCHEDULE = (
    (),
    (),
    (0, 1),
    (),
    (),
    (),
    (),
    (2, 0, 1, 3, 4),
    (),
    (),
    (5,),
    (),
    (0, 1),
    (2, 6),
    (3, 4, 5),
    (),
    (2, 7, 0, 1),
    (3, 4, 5, 6, 8, 7, 9),
    (),
    (2, 0, 6, 1, 7, 9, 8, 10, 11),
    (3, 4, 5),
    (9,),
    (0,),
    (1, 2, 6, 7, 8),
    (10, 11, 12, 13, 14, 9),
    (0,),
    (2, 5),
    (0, 3, 4),
    (1, 6, 7, 8, 9, 10, 11, 15),
    (),
    (1,),
    (5, 16),
    (9,),
    (8, 12, 10, 11, 13, 3, 4, 6, 7, 14, 17),
    (),
    (2, 9, 15, 18, 19),
    (
        10, 11, 9, 2, 8, 5, 16, 5, 12, 13, 14, 19, 15, 6, 7, 12, 17, 10, 11, 16, 19, 13, 3, 4, 6, 7,
        18, 8, 14, 15, 17, 3, 19, 4, 8, 18, 10, 11, 12, 16, 19, 10, 11, 12, 13, 15, 19, 14, 17, 18,
        16, 13, 19, 15, 17, 14, 12, 19, 16, 18, 12, 13, 17, 13, 15, 18, 16, 14, 15, 17, 16, 14, 18,
        17, 18,
    ),
)


def dot(left, right, dims=NN):
    return lax.dot_general(left, right, dims, preferred_element_type=jnp.float32)


def column_sum(values):
    return jnp.sum(values, axis=0, keepdims=True)


def row_mean(values):
    return jnp.mean(values, axis=-1, keepdims=True)


def reduce_job(part, total, recv, sems, halves, z_peers, quarter):
    rows = part.shape[0]
    offsets, sizes, copies, back = [0], [rows], [], []
    for n, (partner, bit) in enumerate(halves):
        size = sizes[-1] // 2
        keep = pl.multiple_of(offsets[-1] + bit * size, size)
        give = pl.multiple_of(offsets[-1] + (1 - bit) * size, size)
        copies.append(
            pltpu.make_async_remote_copy(
                src_ref=part.at[pl.ds(give, size)],
                dst_ref=recv[n],
                send_sem=sems.at[0],
                recv_sem=sems.at[3 + n],
                device_id=partner,
                device_id_type=MESH,
            )
        )
        offsets.append(keep)
        sizes.append(size)
        back.append(
            pltpu.make_async_remote_copy(
                src_ref=total.at[pl.ds(keep, size)],
                dst_ref=total.at[pl.ds(keep, size)],
                send_sem=sems.at[0],
                recv_sem=sems.at[9 + n],
                device_id=partner,
                device_id_type=MESH,
            )
        )
    size = sizes[-1] // (len(z_peers) + 1)
    base = offsets[-1]

    def piece(index):
        return pl.ds(pl.multiple_of(base + index * size, size), size)

    mine = piece(quarter)
    spread, gather = [], []
    for n, (peer, index) in enumerate(z_peers):
        spread.append(
            pltpu.make_async_remote_copy(
                src_ref=part.at[piece(index)],
                dst_ref=recv[3].at[n],
                send_sem=sems.at[n],
                recv_sem=sems.at[6 + n],
                device_id=peer,
                device_id_type=MESH,
            )
        )
        gather.append(
            pltpu.make_async_remote_copy(
                src_ref=part.at[mine],
                dst_ref=total.at[mine],
                send_sem=sems.at[n],
                recv_sem=sems.at[12 + n],
                device_id=peer,
                device_id_type=MESH,
            )
        )
    kept = pltpu.make_async_copy(part.at[mine], total.at[mine], sems.at[15])

    def add(n):
        size = sizes[n + 1]
        step = min(size, 128)

        def chunk(i, carry):
            start = i * step
            at = pl.ds(pl.multiple_of(offsets[n + 1] + start, step), step)
            other = recv[n][pl.ds(pl.multiple_of(start, step), step), :].astype(jnp.float32)
            part[at, :] = (part[at, :].astype(jnp.float32) + other).astype(part.dtype)
            return carry

        lax.fori_loop(0, size // step, chunk, 0)

    def first():
        copies[0].start()

    def fold(n):
        def run():
            copies[n].wait()
            add(n)
            if n + 1 < len(copies):
                copies[n + 1].start()
            else:
                for copy in spread:
                    copy.start()

        return run

    def settle():
        for copy in spread:
            copy.wait()
        others = [recv[3][n].astype(jnp.float32) for n in range(len(spread))]
        own = part[mine, :].astype(jnp.float32)
        part[mine, :] = ((own + others[0]) + (others[1] + others[2])).astype(part.dtype)
        kept.start()
        for copy in gather:
            copy.start()

    def collect():
        kept.wait()
        for copy in gather:
            copy.wait()
        back[-1].start()

    def unfold(n):
        def run():
            back[n].wait()
            if n > 0:
                back[n - 1].start()

        return run

    return [first] + [fold(n) for n in range(3)] + [settle, collect] + [unfold(n) for n in (2, 1, 0)]


def small_job(part, total, recv, sems, halves, z_peers):
    offset, size, copies, back, kept_cols = 0, part.shape[1], [], [], []
    for n, (partner, bit) in enumerate(halves):
        size = size // 2
        keep = pl.ds(pl.multiple_of(offset + bit * size, size), size)
        give = pl.ds(pl.multiple_of(offset + (1 - bit) * size, size), size)
        copies.append(
            pltpu.make_async_remote_copy(
                src_ref=part.at[:, give],
                dst_ref=recv[n],
                send_sem=sems.at[0],
                recv_sem=sems.at[3 + n],
                device_id=partner,
                device_id_type=MESH,
            )
        )
        back.append(
            pltpu.make_async_remote_copy(
                src_ref=total.at[:, keep],
                dst_ref=total.at[:, keep],
                send_sem=sems.at[0],
                recv_sem=sems.at[9 + n],
                device_id=partner,
                device_id_type=MESH,
            )
        )
        kept_cols.append(keep)
        offset = offset + bit * size
    mine = kept_cols[-1]
    spread = [
        pltpu.make_async_remote_copy(
            src_ref=part.at[:, mine],
            dst_ref=recv[3].at[n],
            send_sem=sems.at[n],
            recv_sem=sems.at[6 + n],
            device_id=peer,
            device_id_type=MESH,
        )
        for n, (peer, _) in enumerate(z_peers)
    ]

    def first():
        copies[0].start()

    def fold(n):
        def run():
            copies[n].wait()
            part[:, kept_cols[n]] = part[:, kept_cols[n]] + recv[n][...]
            if n + 1 < len(copies):
                copies[n + 1].start()
            else:
                for copy in spread:
                    copy.start()

        return run

    def settle():
        for copy in spread:
            copy.wait()
        total[:, mine] = (part[:, mine] + recv[3][0]) + (recv[3][1] + recv[3][2])
        back[-1].start()

    def unfold(n):
        def run():
            back[n].wait()
            if n > 0:
                back[n - 1].start()

        return run

    return [first] + [fold(n) for n in range(3)] + [settle] + [unfold(n) for n in (2, 1, 0)]


def table_kernel(
    local,
    block_tables,
    seq,
    x_hbm,
    cot_hbm,
    lengths_ref,
    counts_ref,
    w_in_hbm,
    w_out_hbm,
    w_up_hbm,
    w_down_hbm,
    *refs,
):
    vector_refs, refs = refs[:VECTORS], refs[VECTORS:]
    (
        act_hbm,
        xgrad_hbm,
        t_in,
        t_out,
        t_up,
        t_down,
        t_small,
        w_in,
        w_out,
        w_up,
        w_down,
        vectors,
        g_in,
        g_out,
        g_up,
        g_down,
        small,
        in_low,
        cot_low,
        stream,
        queries,
        kv,
        attended,
        stats,
        norm1,
        inverse1,
        mid_low,
        slope,
        act_low,
        norm2,
        inverse2,
        meta,
        bias_row,
        bias_col,
        valid,
        ffn_low,
        hidden_low,
        branch_low,
        attended_low,
        stats_rows,
        dq_t,
        dkv_own,
        dkv_send,
        dkv_recv,
        proj_low,
        staged,
        recv_in,
        recv_out,
        recv_up,
        recv_down,
        recv_small,
        x_send,
        x_recv,
        cot_send,
        cot_recv,
        act_send,
        act_recv,
        xg_send,
        xg_recv,
        local_sem,
        kv_sem,
        dkv_sem,
        meta_sem,
        job_sem,
    ) = refs
    upstream = stream
    rows = block_tables * local
    dim = in_low.shape[-1]
    head_dim = dim // HEADS
    scale = head_dim**-0.5
    tiles = rows // TILE
    group_heads = HEADS // GROUPS
    group_width = group_heads * head_dim
    t = lax.axis_index("tables")
    r = lax.axis_index("rows")
    core = lax.rem(t, 2)
    side = r // block_tables
    slot = lax.rem(r, block_tables)
    peer = (t + 1 - 2 * core, r)
    own_rows = pl.multiple_of(core * rows, rows)
    peer_rows = pl.multiple_of((1 - core) * rows, rows)

    x_side, y_side, z_side = lax.rem(r, 2), t // 2, r // 2
    x_next = (t, r + 1 - 2 * x_side)
    y_next = (t + 2 - 4 * y_side, r)
    z_next = [
        (z_side + 1 - 2 * lax.rem(z_side, 2)),
        lax.rem(z_side + 2, 4),
        3 - z_side,
    ]
    z_peers = [((t, 2 * z + x_side), z) for z in z_next]

    def choose(first, second):
        return core * second + (1 - core) * first

    halves = [
        (peer, core),
        (
            (choose(x_next[0], y_next[0]), choose(x_next[1], y_next[1])),
            choose(x_side, y_side),
        ),
        (
            (choose(y_next[0], x_next[0]), choose(y_next[1], x_next[1])),
            choose(y_side, x_side),
        ),
    ]

    def partner(k):
        return (t - core + side, block_tables * core + k)

    def is_self(k):
        return jnp.logical_and(core == side, slot == k)

    barrier = pltpu.get_barrier_semaphore()
    greeted = [peer, x_next, y_next] + [device for device, _ in z_peers]
    for device in greeted:
        pl.semaphore_signal(barrier, inc=1, device_id=device, device_id_type=MESH)
    for k in range(block_tables):

        @pl.when(jnp.logical_not(is_self(k)))
        def _():
            pl.semaphore_signal(barrier, inc=1, device_id=partner(k), device_id_type=MESH)

    pl.semaphore_wait(
        barrier, len(greeted) + jnp.where(core == side, block_tables - 1, block_tables)
    )

    def spread(source, target, send_sem, recv_sem, own_sem):
        def remote(k, at):
            return pltpu.make_async_remote_copy(
                src_ref=source(k),
                dst_ref=target(at),
                send_sem=send_sem.at[k],
                recv_sem=recv_sem.at[at],
                device_id=partner(k),
                device_id_type=MESH,
            )

        def kept(k):
            return pltpu.make_async_copy(source(k), target(k), own_sem)

        def start():
            for k in range(block_tables):

                @pl.when(is_self(k))
                def _():
                    kept(k).start()

                @pl.when(jnp.logical_not(is_self(k)))
                def _():
                    remote(k, slot).start()

        def arrive():
            for k in range(block_tables):

                @pl.when(is_self(k))
                def _():
                    kept(k).wait()

                @pl.when(jnp.logical_not(is_self(k)))
                def _():
                    remote(k, k).wait_recv()

        def left():
            for k in range(block_tables):

                @pl.when(jnp.logical_not(is_self(k)))
                def _():
                    remote(k, slot).wait_send()

        return start, arrive, left

    def by_table(ref):
        return lambda k: ref.at[k]

    def by_rows(ref):
        return lambda k: ref.at[pl.ds(k * local, local)]

    x_start, x_arrive, x_left = spread(by_table(x_hbm), by_rows(in_low.at[0]), x_send, x_recv, local_sem.at[0])
    cot_start, cot_arrive, cot_left = spread(by_table(cot_hbm), by_rows(cot_low), cot_send, cot_recv, local_sem.at[1])
    act_start, act_arrive, act_left = spread(by_rows(staged.at[0]), by_table(act_hbm), act_send, act_recv, local_sem.at[2])
    xg_start, xg_arrive, xg_left = spread(by_rows(staged.at[1]), by_table(xgrad_hbm), xg_send, xg_recv, local_sem.at[3])

    def swap(source, target, sems):
        return pltpu.make_async_remote_copy(
            src_ref=source,
            dst_ref=target,
            send_sem=sems.at[0],
            recv_sem=sems.at[1],
            device_id=peer,
            device_id_type=MESH,
        )

    x_start()
    loads = [
        pltpu.make_async_copy(source, target, local_sem.at[4 + n])
        for n, (source, target) in enumerate(
            ((w_in_hbm, w_in), (w_out_hbm, w_out), (w_up_hbm, w_up), (w_down_hbm, w_down))
        )
    ]
    for load in loads:
        load.start()
    for n, ref in enumerate(vector_refs):
        for layer in range(LAYERS):
            vectors[pl.ds(layer * VECTORS + n, 1), pl.ds(0, ref.shape[1])] = ref[...].astype(
                jnp.float32
            )[layer : layer + 1, :]
    for k in range(block_tables):
        meta[core, pl.ds(k, 1), :] = jnp.full((1, 128), lengths_ref[k], jnp.int32)
        meta[core, pl.ds(block_tables + k, 1), :] = jnp.full((1, 128), counts_ref[k], jnp.int32)
    meta_copy = swap(meta.at[core], meta.at[core], meta_sem)
    meta_copy.start()
    small[...] = jnp.zeros_like(small)
    meta_copy.wait()
    length = meta[side, pl.ds(slot, 1), :][:, :1]
    train = meta[side, pl.ds(slot + block_tables, 1), :][:, :1]
    bias_row[...] = jnp.where(lax.broadcasted_iota(jnp.int32, (1, seq), 1) < train, 0.0, MASKED)
    bias_col[...] = jnp.where(lax.broadcasted_iota(jnp.int32, (seq, 1), 0) < train, 0.0, MASKED)
    valid[...] = jnp.where(
        lax.broadcasted_iota(jnp.int32, (rows, 1), 0) + core * rows < length, 1.0, 0.0
    )
    small[0, pl.ds(13, 1), pl.ds(0, 128)] = jnp.broadcast_to(column_sum(valid[...]), (1, 128))
    x_arrive()
    cot_start()
    loads[0].wait()

    def vector(index, layer, width):
        return vectors[pl.ds(layer * VECTORS + index, 1), pl.ds(0, width)]

    def add_small(layer, index, values):
        at = (layer, pl.ds(index, 1), pl.ds(0, values.shape[-1]))
        small[at] = small[at] + values

    def each_tile(body, after=()):
        def step(i, carry):
            body(pl.ds(pl.multiple_of(i * TILE, TILE), TILE))
            for n, run in enumerate(after):

                @pl.when(i == n)
                def _():
                    run()

            return carry

        lax.fori_loop(0, tiles, step, 0)

    def head_cols(h):
        return pl.ds(pl.multiple_of(h * head_dim, head_dim), head_dim)

    def forward(layer):
        def project(at):
            projected = dot(in_low[layer, at, :], w_in[layer])
            queries[layer, at, :] = (
                (projected[:, :dim] + vector(0, layer, dim)) * scale
            ).astype(jnp.bfloat16)
            own = pl.ds(pl.multiple_of(own_rows + at.start, TILE), TILE)
            key_rows = projected[:, dim : 2 * dim].astype(jnp.bfloat16)
            value_rows = (projected[:, 2 * dim :] + vector(1, layer, dim)).astype(jnp.bfloat16)
            for h in range(HEADS):
                cols = slice(h * head_dim, (h + 1) * head_dim)
                kv[layer, h, own, pl.ds(0, head_dim)] = key_rows[:, cols]
                kv[layer, h, own, pl.ds(head_dim, head_dim)] = value_rows[:, cols]

        each_tile(project)

        def kv_copy(h):
            mine = kv.at[layer, h, pl.ds(own_rows, rows)]
            return swap(mine, mine, kv_sem.at[layer, h])

        for h in range(HEADS):
            kv_copy(h).start()

        def attend(step, carry):
            h = step // tiles
            at = pl.ds(pl.multiple_of(lax.rem(step, tiles) * TILE, TILE), TILE)
            cols = head_cols(h)

            @pl.when(lax.rem(step, tiles) == 0)
            def _():
                kv_copy(h).wait()

            key_rows = kv[layer, h, :, pl.ds(0, head_dim)]
            value_rows = kv[layer, h, :, pl.ds(head_dim, head_dim)]
            scores = dot(queries[layer, at, cols], key_rows, NT) + bias_row[...]
            row_max = jnp.max(scores, axis=-1, keepdims=True)
            exponent = jnp.exp(scores - row_max)
            total = jnp.sum(exponent, axis=-1, keepdims=True)
            probs = (exponent * (1.0 / total)).astype(jnp.bfloat16)
            attended[layer, at, cols] = dot(probs, value_rows).astype(jnp.bfloat16)
            lane = lax.broadcasted_iota(jnp.int32, (TILE, head_dim), 1)
            kept = jnp.where(h == 0, jnp.zeros((TILE, head_dim), jnp.float32), stats[layer, at, :])
            stats[layer, at, :] = jnp.where(lane == h, row_max + jnp.log(total), kept)
            return carry

        lax.fori_loop(0, HEADS * tiles, attend, 0)
        if layer == 0:
            for load in loads[1:]:
                load.wait()

        def dense(at):
            below = in_low[0, at, :].astype(jnp.float32) if layer == 0 else stream[at, :]
            branch = dot(attended[layer, at, :], w_out[layer]) + vector(2, layer, dim)
            valid_cells = valid[at, :]
            add_small(layer, 10, column_sum(below * below * valid_cells))
            add_small(layer, 11, column_sum(branch * branch * valid_cells))
            summed = below + branch
            centered = summed - row_mean(summed)
            inverse = lax.rsqrt(row_mean(centered * centered) + EPSILON)
            normed = centered * inverse
            norm1[layer, at, :] = normed
            inverse1[layer, at, :] = inverse
            first_out = normed * vector(3, layer, dim) + vector(4, layer, dim)
            mid = first_out.astype(jnp.bfloat16)
            mid_low[layer, at, :] = mid
            hidden = dot(mid, w_up[layer]) + vector(5, layer, 2 * dim)
            cdf = 0.5 + 0.5 * lax.erf(hidden * (0.5**0.5))
            slope[layer, at, :] = cdf + hidden * (
                jnp.exp(hidden * hidden * -0.5) * 0.3989422804014327
            )
            act = (hidden * cdf).astype(jnp.bfloat16)
            act_low[layer, at, :] = act
            ffn_out = dot(act, w_down[layer]) + vector(6, layer, dim)
            add_small(layer, 12, column_sum(ffn_out * ffn_out * valid_cells))
            summed = first_out + ffn_out
            centered = summed - row_mean(summed)
            inverse = lax.rsqrt(row_mean(centered * centered) + EPSILON)
            normed = centered * inverse
            norm2[layer, at, :] = normed
            inverse2[layer, at, :] = inverse
            out = normed * vector(7, layer, dim) + vector(8, layer, dim)
            if layer + 1 < LAYERS:
                stream[at, :] = out
                in_low[layer + 1, at, :] = out.astype(jnp.bfloat16)
            else:
                staged[0, at, :] = (out * valid_cells).astype(jnp.bfloat16)

        each_tile(dense)

    for layer in range(LAYERS):
        forward(layer)
    act_start()
    cot_arrive()

    jobs = []

    points = list(SCHEDULE)

    def begin(steps):
        jobs.append(list(steps))
        jobs[-1].pop(0)()

    def tick():
        for index in points.pop(0):
            if index < len(jobs) and jobs[index]:
                jobs[index].pop(0)()

    def reduce(part, total, recv):
        begin(reduce_job(part, total, recv, job_sem.at[len(jobs)], halves, z_peers, z_side))

    def reduce_halves(part, total, recv):
        width = part.shape[1] // HALVES
        for n in range(HALVES):
            cols = pl.ds(n * width, width)
            reduce(
                part.at[:, cols],
                total.at[:, cols],
                [ref.at[:, cols] for ref in recv[:3]] + [recv[3].at[:, :, cols]],
            )

    def backward(layer):
        def recv_of(refs):
            return [ref.at[layer] for ref in refs]

        def enter(at):
            if layer == LAYERS - 1:
                up = cot_low[at, :].astype(jnp.float32) * valid[at, :]
            else:
                up = upstream[at, :]
            normed = norm2[layer, at, :]
            add_small(layer, 8, column_sum(up * normed))
            add_small(layer, 9, column_sum(up))
            scaled = up * vector(7, layer, dim)
            second = inverse2[layer, at, :] * (
                scaled - row_mean(scaled) - normed * row_mean(scaled * normed)
            )
            upstream[at, :] = second
            ffn = second.astype(jnp.bfloat16)
            ffn_low[at, :] = ffn
            add_small(layer, 7, column_sum(ffn.astype(jnp.float32)))

        each_tile(enter)
        g_down[layer] = dot(act_low[layer], ffn_low[...], TN).astype(jnp.bfloat16)
        tick()
        reduce_halves(g_down.at[layer], t_down.at[layer], recv_of(recv_down))

        def dense(at):
            hidden = (dot(ffn_low[at, :], w_down[layer], NT) * slope[layer, at, :]).astype(
                jnp.bfloat16
            )
            hidden_low[at, :] = hidden
            add_small(layer, 6, column_sum(hidden.astype(jnp.float32)))
            first = upstream[at, :] + dot(hidden, w_up[layer], NT)
            normed = norm1[layer, at, :]
            add_small(layer, 4, column_sum(first * normed))
            add_small(layer, 5, column_sum(first))
            scaled = first * vector(3, layer, dim)
            residual = inverse1[layer, at, :] * (
                scaled - row_mean(scaled) - normed * row_mean(scaled * normed)
            )
            upstream[at, :] = residual
            branch = residual.astype(jnp.bfloat16)
            branch_low[at, :] = branch
            add_small(layer, 3, column_sum(branch.astype(jnp.float32)))
            low = dot(branch, w_out[layer], NT).astype(jnp.bfloat16)
            attended_low[at, :] = low
            product = low.astype(jnp.float32) * attended[layer, at, :].astype(jnp.float32)
            lane = lax.broadcasted_iota(jnp.int32, (TILE, head_dim), 1)
            held = stats[layer, at, :]
            for h in range(HEADS):
                center = jnp.sum(product[:, h * head_dim : (h + 1) * head_dim], axis=-1, keepdims=True)
                held = jnp.where(lane == HEADS + h, center, held)
            stats_rows[:, at] = jnp.transpose(held)[: 2 * HEADS, :]

        each_tile(dense, (tick,) * tiles)
        g_up[layer] = dot(mid_low[layer], hidden_low[...], TN).astype(jnp.bfloat16)
        tick()
        reduce_halves(g_up.at[layer], t_up.at[layer], recv_of(recv_up))
        g_out[layer] = dot(attended[layer], branch_low[...], TN).astype(jnp.bfloat16)
        tick()
        reduce(g_out.at[layer], t_out.at[layer], recv_of(recv_out))

        def attend(group, base, first, keep):
            def step(i, carry):
                h = group * group_heads + i // tiles
                j = pl.multiple_of(lax.rem(i, tiles) * TILE, TILE)
                at = pl.ds(pl.multiple_of(base + j, TILE), TILE)
                cols = head_cols(h)
                key_rows = kv[layer, h, at, pl.ds(0, head_dim)]
                query_rows = queries[layer, :, cols]
                grads = attended_low[:, cols]
                probs = jnp.exp(
                    dot(key_rows, query_rows, NT) + bias_col[at, :] - stats_rows[pl.ds(h, 1), :]
                )
                value_part = dot(probs.astype(jnp.bfloat16), grads)
                probs_grad = dot(kv[layer, h, at, pl.ds(head_dim, head_dim)], grads, NT)
                scores_low = (probs * (probs_grad - stats_rows[pl.ds(HEADS + h, 1), :])).astype(
                    jnp.bfloat16
                )
                key_part = dot(scores_low, query_rows)
                query_part = dot(key_rows, scores_low, TN)
                if first:
                    query_part = jnp.where(j == 0, query_part, query_part + dq_t[cols, :])
                else:
                    query_part = query_part + dq_t[cols, :]
                dq_t[cols, :] = query_part
                inside = i // tiles * head_dim
                keep(pl.ds(j, TILE), pl.ds(pl.multiple_of(inside, head_dim), head_dim), key_part)
                keep(
                    pl.ds(j, TILE),
                    pl.ds(pl.multiple_of(group_width + inside, head_dim), head_dim),
                    value_part,
                )
                return carry

            lax.fori_loop(0, group_heads * tiles, step, 0)

        def dkv_copy(group):
            return swap(
                dkv_send.at[layer, group], dkv_recv.at[layer, group], dkv_sem.at[layer, group]
            )

        def attend_peer(group):
            def keep(at, cols, part):
                dkv_send[layer, group, at, cols] = part.astype(jnp.bfloat16)

            attend(group, peer_rows, True, keep)
            dkv_copy(group).start()
            tick()

        def attend_own(group):
            def keep(at, cols, part):
                dkv_own[group % 2, at, cols] = part

            attend(group, own_rows, False, keep)
            tick()

        def finish_group(group):
            dkv_copy(group).wait()

            def finish(at):
                group_rows = pl.ds(group * group_width, group_width)
                query = jnp.transpose(dq_t[group_rows, at]).astype(jnp.bfloat16)
                pair = (
                    dkv_own[group % 2, at, :] + dkv_recv[layer, group, at, :].astype(jnp.float32)
                ).astype(jnp.bfloat16)
                proj_low[group, at, pl.ds(0, group_width)] = query
                proj_low[group, at, pl.ds(group_width, 2 * group_width)] = pair
                cols = pl.ds(group * group_width, group_width)
                small[layer, pl.ds(0, 1), cols] += column_sum(query.astype(jnp.float32)) * scale
                small[layer, pl.ds(1, 1), cols] += column_sum(
                    pair[:, group_width:].astype(jnp.float32)
                )

            each_tile(finish)
            grad = dot(in_low[layer], proj_low[group], TN)
            g_in[layer, group, :, pl.ds(0, group_width)] = (grad[:, :group_width] * scale).astype(
                jnp.bfloat16
            )
            g_in[layer, group, :, pl.ds(group_width, 2 * group_width)] = grad[
                :, group_width:
            ].astype(jnp.bfloat16)
            tick()
            reduce(
                g_in.at[layer, group],
                t_in.at[layer, group],
                [ref.at[layer, group] for ref in recv_in],
            )

        for group in range(GROUPS):
            attend_peer(group)
            if group > 0:
                finish_group(group - 1)
            attend_own(group)
        finish_group(GROUPS - 1)
        begin(
            small_job(
                small.at[layer],
                t_small.at[layer],
                [ref.at[layer] for ref in recv_small],
                job_sem.at[len(jobs)],
                halves,
                z_peers,
            )
        )

        def pass_down(at):
            grad = upstream[at, :]
            for group in range(GROUPS):
                for n in range(3):
                    part = dot(
                        proj_low[group, at, pl.ds(n * group_width, group_width)],
                        w_in[layer, :, pl.ds(n * dim + group * group_width, group_width)],
                        NT,
                    )
                    grad = grad + (part * scale if n == 0 else part)
            if layer > 0:
                upstream[at, :] = grad
            else:
                staged[1, at, :] = grad.astype(jnp.bfloat16)

        each_tile(pass_down)
        tick()
        if layer == 0:
            xg_start()

    for layer in reversed(range(LAYERS)):
        backward(layer)
    tick()
    while any(jobs):
        for steps in jobs:
            if steps:
                steps.pop(0)()
    act_arrive()
    xg_arrive()
    x_left()
    cot_left()
    act_left()
    xg_left()


def widen_kernel(f_in, f_out, f_up, f_down, f_act, f_xgrad, small, *outs):
    act, xgrad, in_weight, out_weight, up_weight, down_weight, root_means = outs[:7]
    groups, width = f_in.shape[1], f_in.shape[3] // 3
    for group in range(groups):
        for n in range(3):
            in_weight[0, :, pl.ds((n * groups + group) * width, width)] = f_in[
                0, group, :, pl.ds(n * width, width)
            ].astype(jnp.float32)
    out_weight[...] = f_out[...].astype(jnp.float32)
    up_weight[...] = f_up[...].astype(jnp.float32)
    down_weight[...] = f_down[...].astype(jnp.float32)
    for k in range(f_act.shape[0]):
        act[:, k, :] = f_act[k].astype(jnp.float32)
        xgrad[:, k, :] = f_xgrad[k].astype(jnp.float32)

    @pl.when(pl.program_id(0) == 0)
    def _():
        for ref, row in zip(outs[7:], (0, 1, 3, 4, 5, 6, 7, 8, 9)):
            for layer in range(LAYERS):
                ref[pl.ds(layer, 1), :] = small[layer, pl.ds(row, 1), pl.ds(0, ref.shape[1])]
        dim = f_act.shape[2]
        count = small[0, pl.ds(13, 1), pl.ds(0, 1)]
        for layer in range(LAYERS):
            sums = jnp.sum(small[layer, pl.ds(8, 8), pl.ds(0, dim)], axis=-1, keepdims=True)
            for n in range(3):
                root_means[pl.ds(layer, 1), pl.ds(n, 1)] = jnp.sqrt(
                    sums[2 + n : 3 + n, :] / (count * dim)
                )


def table_device(tables, row_parts, *operands):
    (
        tables_in,
        in_weight,
        query_bias,
        value_bias,
        out_weight,
        out_bias,
        attn_gain,
        attn_shift,
        up_weight,
        up_bias,
        down_weight,
        down_bias,
        ffn_gain,
        ffn_shift,
        cotangent,
        lengths,
        train_counts,
    ) = operands
    local, block_tables, dim = tables_in.shape
    rows = local * block_tables
    seq = local * row_parts
    hidden = up_weight.shape[-1]
    head_dim = dim // HEADS
    f32, bf16 = jnp.float32, jnp.bfloat16
    groups = GROUPS
    vmem = pl.BlockSpec(memory_space=pltpu.VMEM)
    hbm = pl.BlockSpec(memory_space=pl.ANY)
    smem = pl.BlockSpec(memory_space=pltpu.SMEM)
    block = (block_tables, local, dim)
    dma = pltpu.SemaphoreType.DMA
    in_part = (LAYERS, groups, dim, 3 * dim // groups)
    shards = 8 * row_parts // 2

    def received(shape):
        lead, (height, width) = shape[:-2], shape[-2:]
        return [
            [pltpu.VMEM(lead + (height // n, width), bf16) for n in (2, 4, 8)]
            + [pltpu.VMEM(lead + (3, height // shards, width), bf16)]
        ]

    act, xgrad, *sums, small = pl.pallas_call(
        functools.partial(table_kernel, local, block_tables, seq),
        out_shape=(
            jax.ShapeDtypeStruct(block, bf16),
            jax.ShapeDtypeStruct(block, bf16),
            jax.ShapeDtypeStruct(in_part, bf16),
            jax.ShapeDtypeStruct(out_weight.shape, bf16),
            jax.ShapeDtypeStruct(up_weight.shape, bf16),
            jax.ShapeDtypeStruct(down_weight.shape, bf16),
            jax.ShapeDtypeStruct((LAYERS, 16, hidden), f32),
        ),
        in_specs=[hbm, hbm, smem, smem] + [hbm] * 4 + [vmem] * VECTORS,
        out_specs=(hbm,) * 6 + (vmem,),
        scratch_shapes=[
            pltpu.VMEM(in_weight.shape, bf16),
            pltpu.VMEM(out_weight.shape, bf16),
            pltpu.VMEM(up_weight.shape, bf16),
            pltpu.VMEM(down_weight.shape, bf16),
            pltpu.VMEM((LAYERS * VECTORS, hidden), f32),
            pltpu.VMEM(in_part, bf16),
            pltpu.VMEM(out_weight.shape, bf16),
            pltpu.VMEM(up_weight.shape, bf16),
            pltpu.VMEM(down_weight.shape, bf16),
            pltpu.VMEM((LAYERS, 16, hidden), f32),
            pltpu.VMEM((LAYERS, rows, dim), bf16),
            pltpu.VMEM((rows, dim), bf16),
            pltpu.VMEM((rows, dim), f32),
            pltpu.VMEM((LAYERS, rows, dim), bf16),
            pltpu.VMEM((LAYERS, HEADS, seq, 2 * head_dim), bf16),
            pltpu.VMEM((LAYERS, rows, dim), bf16),
            pltpu.VMEM((LAYERS, rows, head_dim), f32),
            pltpu.VMEM((LAYERS, rows, dim), f32),
            pltpu.VMEM((LAYERS, rows, 1), f32),
            pltpu.VMEM((LAYERS, rows, dim), bf16),
            pltpu.VMEM((LAYERS, rows, hidden), f32),
            pltpu.VMEM((LAYERS, rows, hidden), bf16),
            pltpu.VMEM((LAYERS, rows, dim), f32),
            pltpu.VMEM((LAYERS, rows, 1), f32),
            pltpu.VMEM((2, 2 * block_tables, 128), jnp.int32),
            pltpu.VMEM((1, seq), f32),
            pltpu.VMEM((seq, 1), f32),
            pltpu.VMEM((rows, 1), f32),
            pltpu.VMEM((rows, dim), bf16),
            pltpu.VMEM((rows, hidden), bf16),
            pltpu.VMEM((rows, dim), bf16),
            pltpu.VMEM((rows, dim), bf16),
            pltpu.VMEM((2 * HEADS, rows), f32),
            pltpu.VMEM((dim, rows), f32),
            pltpu.VMEM((2, rows, 2 * dim // groups), f32),
            pltpu.VMEM((LAYERS, groups, rows, 2 * dim // groups), bf16),
            pltpu.VMEM((LAYERS, groups, rows, 2 * dim // groups), bf16),
            pltpu.VMEM((groups, rows, 3 * dim // groups), bf16),
            pltpu.VMEM((2, rows, dim), bf16),
        ]
        + received(in_part)
        + received(out_weight.shape)
        + received(up_weight.shape)
        + received(down_weight.shape)
        + [
            [pltpu.VMEM((LAYERS, 16, hidden // n), f32) for n in (2, 4, 8)]
            + [pltpu.VMEM((LAYERS, 3, 16, hidden // 8), f32)]
        ]
        + [dma((block_tables,))] * 8
        + [
            dma((8,)),
            dma((LAYERS, HEADS, 2)),
            dma((LAYERS, groups, 2)),
            dma((2,)),
            dma((LAYERS * (2 * HALVES + 2 + groups), 16)),
        ],
        compiler_params=pltpu.CompilerParams(
            collective_id=0, has_side_effects=True, vmem_limit_bytes=62 * 1024 * 1024
        ),
    )(
        jnp.swapaxes(tables_in, 0, 1),
        jnp.swapaxes(cotangent, 0, 1),
        lengths,
        train_counts,
        in_weight,
        out_weight,
        up_weight,
        down_weight,
        query_bias,
        value_bias,
        out_bias,
        attn_gain,
        attn_shift,
        up_bias,
        down_bias,
        ffn_gain,
        ffn_shift,
    )
    steps = 4

    def whole(shape):
        return pl.BlockSpec(shape, lambda l, i: (0,) * len(shape))

    def sliced(height, width):
        return pl.BlockSpec((1, height // steps, width), lambda l, i: (l, i, 0))

    weights = [
        sliced(dim, 3 * dim),
        sliced(dim, dim),
        sliced(dim, hidden),
        sliced(hidden, dim),
    ]
    cut = local // (LAYERS * steps)
    table_rows = pl.BlockSpec((block_tables, cut, dim), lambda l, i: (0, l * steps + i, 0))
    row_tables = pl.BlockSpec((cut, block_tables, dim), lambda l, i: (l * steps + i, 0, 0))
    vector = jax.ShapeDtypeStruct((LAYERS, dim), f32)
    wide_vector = jax.ShapeDtypeStruct((LAYERS, hidden), f32)
    shapes = [
        jax.ShapeDtypeStruct(tables_in.shape, f32),
        jax.ShapeDtypeStruct(tables_in.shape, f32),
        jax.ShapeDtypeStruct(in_weight.shape, f32),
        jax.ShapeDtypeStruct(out_weight.shape, f32),
        jax.ShapeDtypeStruct(up_weight.shape, f32),
        jax.ShapeDtypeStruct(down_weight.shape, f32),
        jax.ShapeDtypeStruct((LAYERS, 3), f32),
    ] + [vector] * 5 + [wide_vector] + [vector] * 3
    outs = pl.pallas_call(
        widen_kernel,
        grid=(LAYERS, steps),
        out_shape=shapes,
        in_specs=[
            pl.BlockSpec((1, groups, dim // steps, 3 * dim // groups), lambda l, i: (l, 0, i, 0)),
            *weights[1:],
            table_rows,
            table_rows,
            whole((LAYERS, 16, hidden)),
        ],
        out_specs=[row_tables, row_tables, *weights] + [whole(s.shape) for s in shapes[6:]],
        compiler_params=pltpu.CompilerParams(vmem_limit_bytes=62 * 1024 * 1024),
    )(*sums, act, xgrad, small)
    act, xgrad, g_in, g_out, g_up, g_down, root_means = outs[:7]
    query, value, out, gain1, shift1, up, down, gain2, shift2 = outs[7:]
    return (
        act,
        xgrad,
        g_in,
        query,
        value,
        g_out,
        out,
        gain1,
        shift1,
        g_up,
        up,
        g_down,
        down,
        gain2,
        shift2,
        root_means,
    )


def per_device(tables, row_parts, *operands):
    local, block_tables, dim = operands[0].shape
    if tables == 4 and row_parts == 2 * block_tables and local * row_parts <= 1024:
        return table_device(tables, row_parts, *operands)
    return gathered_device(*operands)


def solution(mesh):
    placed = (
        P("rows", "tables", None),
        P(),
        P(),
        P(),
        P(),
        P(),
        P(),
        P(),
        P(),
        P(),
        P(),
        P(),
        P(),
        P(),
        P("rows", "tables", None),
        P("tables"),
        P("tables"),
    )
    return jax.shard_map(
        functools.partial(per_device, mesh.shape["tables"], mesh.shape["rows"]),
        mesh=mesh,
        in_specs=placed,
        out_specs=(
            P("rows", "tables", None),
            P("rows", "tables", None),
            P(),
            P(),
            P(),
            P(),
            P(),
            P(),
            P(),
            P(),
            P(),
            P(),
            P(),
            P(),
            P(),
            P(),
        ),
        check_vma=False,
    )
```

```python
import functools

import jax
import jax.numpy as jnp
from jax import lax
from jax.experimental import pallas as pl
from jax.experimental.pallas import tpu as pltpu
from jax.sharding import PartitionSpec as P

D = 512
HEADS = 4
LAYERS = 2


EPSILON = 1e-05
MASKED = -1e30


def norm_forward(values, gain_row, offsets):
    average = jnp.mean(values, axis=-1, keepdims=True)
    centered = values - average
    variance = jnp.mean(centered * centered, axis=-1, keepdims=True)
    inverse = lax.rsqrt(variance + EPSILON)
    normed = centered * inverse
    return (normed * gain_row + offsets, normed, inverse)


def norm_backward(upstream, normed, inverse, gain_row):
    scaled = upstream * gain_row
    average = jnp.mean(scaled, axis=-1, keepdims=True)
    projection = jnp.mean(scaled * normed, axis=-1, keepdims=True)
    return inverse * (scaled - average - normed * projection)


def gelu_exact(values):
    return jax.nn.gelu(values, approximate=False)


def split_heads(values):
    return values.reshape(values.shape[0], values.shape[1], HEADS, values.shape[2] // HEADS)


def merge_heads(values):
    return values.reshape(values.shape[0], values.shape[1], values.shape[2] * values.shape[3])


def table_scores(queries, key_rows, usable):
    scores = jnp.einsum(
        "ibhe,jbhe->bhij",
        split_heads(queries),
        split_heads(key_rows),
        preferred_element_type=jnp.float32,
    )
    return jnp.where(usable[:, None, None, :], scores, MASKED)


def row_sums(values):
    return jnp.sum(values.astype(jnp.float32), axis=(0, 1))


def gathered_device(
    tables_in,
    in_weight,
    query_bias,
    value_bias,
    out_weight,
    out_bias,
    attn_gain,
    attn_shift,
    up_weight,
    up_bias,
    down_weight,
    down_bias,
    ffn_gain,
    ffn_shift,
    cotangent,
    lengths,
    train_counts,
):
    local_rows = tables_in.shape[0]
    seq_rows = local_rows * lax.axis_size("rows")
    positions = lax.axis_index("rows") * local_rows + jnp.arange(local_rows, dtype=jnp.int32)
    valid_rows = (positions[:, None] < lengths[None, :]).astype(jnp.float32)
    valid_cells = valid_rows[:, :, None]
    usable = jnp.arange(seq_rows, dtype=jnp.int32)[None, :] < train_counts[:, None]
    score_scale = (D // HEADS) ** (-0.5)
    column_scale = jnp.concatenate(
        [jnp.full((D,), score_scale, jnp.float32), jnp.ones((2 * D,), jnp.float32)]
    )
    stream = tables_in.astype(jnp.float32)
    stored = []
    squares = []
    for layer_index in range(LAYERS):
        in_low = stream.astype(jnp.bfloat16)
        projected = jnp.einsum(
            "ibd,de->ibe", in_low, in_weight[layer_index], preferred_element_type=jnp.float32
        )
        queries = ((projected[:, :, :D] + query_bias[layer_index]) * score_scale).astype(
            jnp.bfloat16
        )
        key_rows = projected[:, :, D : 2 * D].astype(jnp.bfloat16)
        value_rows = (projected[:, :, 2 * D :] + value_bias[layer_index]).astype(jnp.bfloat16)
        all_keys, all_values = (
            lax.all_gather(key_rows, "rows", axis=0, tiled=True),
            lax.all_gather(value_rows, "rows", axis=0, tiled=True),
        )
        scores = table_scores(queries, all_keys, usable)
        row_max = jnp.max(scores, axis=-1, keepdims=True)
        exponent = jnp.exp(scores - row_max)
        row_total = jnp.sum(exponent, axis=-1, keepdims=True)
        probs_low = (exponent / row_total).astype(jnp.bfloat16)
        log_total = (row_max + jnp.log(row_total))[..., 0]
        attended = merge_heads(
            jnp.einsum(
                "bhij,jbhe->ibhe",
                probs_low,
                split_heads(all_values),
                preferred_element_type=jnp.float32,
            )
        ).astype(jnp.bfloat16)
        branch = (
            jnp.einsum(
                "ibd,de->ibe", attended, out_weight[layer_index], preferred_element_type=jnp.float32
            )
            + out_bias[layer_index]
        )
        first_out, first_norm, first_inverse = norm_forward(
            stream + branch, attn_gain[layer_index], attn_shift[layer_index]
        )
        mid_low = first_out.astype(jnp.bfloat16)
        hidden = (
            jnp.einsum(
                "ibd,df->ibf", mid_low, up_weight[layer_index], preferred_element_type=jnp.float32
            )
            + up_bias[layer_index]
        )
        act_low = gelu_exact(hidden).astype(jnp.bfloat16)
        ffn_out = (
            jnp.einsum(
                "ibf,fd->ibd", act_low, down_weight[layer_index], preferred_element_type=jnp.float32
            )
            + down_bias[layer_index]
        )
        second_out, second_norm, second_inverse = norm_forward(
            first_out + ffn_out, ffn_gain[layer_index], ffn_shift[layer_index]
        )
        squares.append(
            jnp.stack(
                [
                    jnp.sum(valid_cells * stream * stream),
                    jnp.sum(valid_cells * branch * branch),
                    jnp.sum(valid_cells * ffn_out * ffn_out),
                ]
            )
        )
        gathered = (all_keys, all_values)
        stored.append(
            (
                in_low,
                queries,
                key_rows,
                value_rows,
                gathered,
                log_total,
                attended,
                first_norm,
                first_inverse,
                mid_low,
                hidden,
                act_low,
                second_norm,
                second_inverse,
            )
        )
        stream = second_out
    activations = stream * valid_cells
    upstream = cotangent.astype(jnp.float32) * valid_cells
    layer_grads = [None] * LAYERS
    for layer_index in reversed(range(LAYERS)):
        (
            in_low,
            queries,
            key_rows,
            value_rows,
            gathered,
            log_total,
            attended,
            first_norm,
            first_inverse,
            mid_low,
            hidden,
            act_low,
            second_norm,
            second_inverse,
        ) = stored[layer_index]
        ffn_gain_grad = jnp.sum(upstream * second_norm, axis=(0, 1))
        ffn_shift_grad = jnp.sum(upstream, axis=(0, 1))
        second_grad = norm_backward(upstream, second_norm, second_inverse, ffn_gain[layer_index])
        ffn_low = second_grad.astype(jnp.bfloat16)
        down_weight_grad = jnp.einsum(
            "ibf,ibd->fd", act_low, ffn_low, preferred_element_type=jnp.float32
        )
        act_grad = jnp.einsum(
            "ibd,fd->ibf", ffn_low, down_weight[layer_index], preferred_element_type=jnp.float32
        )
        hidden_low = jax.vjp(gelu_exact, hidden)[1](act_grad)[0].astype(jnp.bfloat16)
        up_weight_grad = jnp.einsum(
            "ibd,ibf->df", mid_low, hidden_low, preferred_element_type=jnp.float32
        )
        first_grad = second_grad + jnp.einsum(
            "ibf,df->ibd", hidden_low, up_weight[layer_index], preferred_element_type=jnp.float32
        )
        attn_gain_grad = jnp.sum(first_grad * first_norm, axis=(0, 1))
        attn_shift_grad = jnp.sum(first_grad, axis=(0, 1))
        residual_grad = norm_backward(first_grad, first_norm, first_inverse, attn_gain[layer_index])
        branch_low = residual_grad.astype(jnp.bfloat16)
        out_weight_grad = jnp.einsum(
            "ibd,ibe->de", attended, branch_low, preferred_element_type=jnp.float32
        )
        attended_low = jnp.einsum(
            "ibe,de->ibd", branch_low, out_weight[layer_index], preferred_element_type=jnp.float32
        ).astype(jnp.bfloat16)
        all_keys, all_values = gathered
        scores = table_scores(queries, all_keys, usable)
        attn_probs = jnp.exp(scores - log_total[..., None])
        probs_low = attn_probs.astype(jnp.bfloat16)
        probs_grad = jnp.einsum(
            "ibhe,jbhe->bhij",
            split_heads(attended_low),
            split_heads(all_values),
            preferred_element_type=jnp.float32,
        )
        center = jnp.sum(attn_probs * probs_grad, axis=-1)
        scores_low = (attn_probs * (probs_grad - center[..., None])).astype(jnp.bfloat16)
        query_low = merge_heads(
            jnp.einsum(
                "bhij,jbhe->ibhe",
                scores_low,
                split_heads(all_keys),
                preferred_element_type=jnp.float32,
            )
        ).astype(jnp.bfloat16)
        key_part = jnp.einsum(
            "bhij,ibhe->jbhe", scores_low, split_heads(queries), preferred_element_type=jnp.float32
        )
        value_part = jnp.einsum(
            "bhij,ibhe->jbhe",
            probs_low,
            split_heads(attended_low),
            preferred_element_type=jnp.float32,
        )
        key_sums = lax.psum_scatter(
            jnp.concatenate([merge_heads(key_part), merge_heads(value_part)], axis=-1).astype(
                jnp.bfloat16
            ),
            "rows",
            scatter_dimension=0,
            tiled=True,
        )
        proj_low = jnp.concatenate([query_low, key_sums], axis=-1)
        in_weight_grad = (
            jnp.einsum("ibd,ibe->de", in_low, proj_low, preferred_element_type=jnp.float32)
            * column_scale
        )
        query_bias_grad = row_sums(query_low) * score_scale
        value_bias_grad = row_sums(proj_low[:, :, 2 * D :])
        weight_now = in_weight[layer_index]
        query_input = (
            jnp.einsum(
                "ibe,de->ibd", query_low, weight_now[:, :D], preferred_element_type=jnp.float32
            )
            * score_scale
        )
        other_input = jnp.einsum(
            "ibe,de->ibd", proj_low[:, :, D:], weight_now[:, D:], preferred_element_type=jnp.float32
        )
        upstream = residual_grad + query_input + other_input
        layer_grads[layer_index] = (
            in_weight_grad,
            query_bias_grad,
            value_bias_grad,
            out_weight_grad,
            row_sums(branch_low),
            attn_gain_grad,
            attn_shift_grad,
            up_weight_grad,
            row_sums(hidden_low),
            down_weight_grad,
            row_sums(ffn_low),
            ffn_gain_grad,
            ffn_shift_grad,
        )
    stacked = [
        jnp.stack([layer_grads[layer_index][member] for layer_index in range(LAYERS)])
        for member in range(13)
    ]
    totals = lax.psum(
        (
            stacked[0],
            stacked[1],
            stacked[2],
            stacked[3],
            stacked[4],
            stacked[5],
            stacked[6],
            stacked[7],
            stacked[8],
            stacked[9],
            stacked[10],
            stacked[11],
            stacked[12],
            jnp.stack(squares),
            jnp.sum(valid_rows),
        ),
        ("tables", "rows"),
    )
    root_means = jnp.sqrt(totals[13] / (totals[14] * D))
    return (
        activations,
        upstream,
        totals[0],
        totals[1],
        totals[2],
        totals[3],
        totals[4],
        totals[5],
        totals[6],
        totals[7],
        totals[8],
        totals[9],
        totals[10],
        totals[11],
        totals[12],
        root_means,
    )


MESH = pl.DeviceIdType.MESH
NT = (((1,), (1,)), ((), ()))
NN = (((1,), (0,)), ((), ()))
TN = (((0,), (0,)), ((), ()))
TILE = 256
VECTORS = 9
GROUPS = 4
HALVES = 2
PATHS = {
    "A": ("cxy", "cyx"),
    "N": ("cnyxf", "cnyxf"),
    "P": ("cxynf", "cxynf"),
    "Q": ("cyxnf", "cyxnf"),
}
KINDS = "NAAAQNAANAQPANANAAAA"
SCHEDULE = (
    (),
    (),
    (0, 1),
    (),
    (),
    (),
    (),
    (),
    (2, 1, 3, 4),
    (),
    (0, 5),
    (),
    (),
    (),
    (1, 6),
    (),
    (5, 7),
    (0, 1, 2, 3, 4, 8, 9),
    (5, 6),
    (0, 1, 7),
    (8, 9, 10, 11, 2, 5, 3, 4),
    (0, 6),
    (1, 7),
    (9,),
    (),
    (8, 5, 12, 13, 14),
    (11, 4, 10),
    (1,),
    (0, 8, 9, 15, 2),
    (1, 3, 5, 6, 7, 4),
    (12, 11, 13),
    (0, 8, 9, 10, 14, 5, 16),
    (),
    (),
    (12, 17),
    (2, 4, 6, 7, 8, 9, 11, 3, 13, 10, 18, 19),
    (
        5, 15, 0, 14, 12, 16, 4, 11, 10, 8, 17, 9, 13, 2, 6, 19, 7, 9, 15, 3, 11, 16, 10, 14, 8, 12,
        13, 4, 19, 5, 17, 18, 15, 5, 11, 13, 19, 6, 12, 7, 0, 10, 15, 18, 16, 2, 4, 3, 14, 17, 6,
        19, 7, 13, 11, 8, 0, 15, 2, 4, 3, 8, 10, 19, 18, 16, 13, 17, 14, 15, 12, 19, 18, 12, 19, 16,
        17, 11, 15, 13, 10, 18, 11, 14, 13, 10, 16, 17, 14, 15, 18, 16, 17, 15, 18,
    ),
)


def dot(left, right, dims=NN):
    return lax.dot_general(left, right, dims, preferred_element_type=jnp.float32)


def column_sum(values):
    return jnp.sum(values, axis=0, keepdims=True)


def row_mean(values):
    return jnp.mean(values, axis=-1, keepdims=True)


def reduce_job(part, total, recv, sems, halves, z_peers, quarter):
    rows = part.shape[0]
    shard = recv[3].shape[0] // 3
    offsets, sizes, copies, back = [0], [rows], [], []
    targets = recv[:3] + [recv[3].at[pl.ds(0, 2 * shard)], recv[3].at[pl.ds(2 * shard, shard)]]
    for n, (partner, bit) in enumerate(halves):
        size = sizes[-1] // 2
        keep = pl.multiple_of(offsets[-1] + bit * size, size)
        give = pl.multiple_of(offsets[-1] + (1 - bit) * size, size)
        copies.append(
            pltpu.make_async_remote_copy(
                src_ref=part.at[pl.ds(give, size)],
                dst_ref=targets[n],
                send_sem=sems.at[0],
                recv_sem=sems.at[1 + n],
                device_id=partner,
                device_id_type=MESH,
            )
        )
        offsets.append(keep)
        sizes.append(size)
        held = part if size == shard else total
        back.append(
            pltpu.make_async_remote_copy(
                src_ref=held.at[pl.ds(keep, size)],
                dst_ref=total.at[pl.ds(keep, size)],
                send_sem=sems.at[0],
                recv_sem=sems.at[6 + n],
                device_id=partner,
                device_id_type=MESH,
            )
        )
    last = len(halves) - 1
    base = offsets[-1]

    def piece(index):
        return pl.ds(pl.multiple_of(base + index * shard, shard), shard)

    mine = piece(quarter if z_peers else 0)
    spread, gather = [], []
    for n, (peer, index) in enumerate(z_peers):
        spread.append(
            pltpu.make_async_remote_copy(
                src_ref=part.at[piece(index)],
                dst_ref=recv[3].at[pl.ds(n * shard, shard)],
                send_sem=sems.at[0],
                recv_sem=sems.at[4],
                device_id=peer,
                device_id_type=MESH,
            )
        )
        gather.append(
            pltpu.make_async_remote_copy(
                src_ref=part.at[mine],
                dst_ref=total.at[mine],
                send_sem=sems.at[0],
                recv_sem=sems.at[9],
                device_id=peer,
                device_id_type=MESH,
            )
        )
    kept = pltpu.make_async_copy(part.at[mine], total.at[mine], sems.at[11])

    def wait_all(recv_sem):
        pltpu.make_async_remote_copy(
            src_ref=recv[3],
            dst_ref=recv[3],
            send_sem=sems.at[0],
            recv_sem=recv_sem,
            device_id=z_peers[0][0],
            device_id_type=MESH,
        ).wait()

    def add(n):
        size = sizes[n + 1]
        step = min(size, 128)

        def chunk(i, carry):
            start = i * step
            at = pl.ds(pl.multiple_of(offsets[n + 1] + start, step), step)
            other = targets[n][pl.ds(pl.multiple_of(start, step), step), :].astype(jnp.float32)
            part[at, :] = (part[at, :].astype(jnp.float32) + other).astype(part.dtype)
            return carry

        lax.fori_loop(0, size // step, chunk, 0)

    def first():
        copies[0].start()

    def fold(n):
        def run():
            copies[n].wait()
            add(n)
            if n < last:
                copies[n + 1].start()
            elif z_peers:
                for copy in spread:
                    copy.start()
            else:
                kept.start()
                back[last].start()

        return run

    def settle():
        wait_all(sems.at[4])
        others = [
            recv[3][pl.ds(n * shard, shard), :].astype(jnp.float32) for n in range(len(spread))
        ]
        own = part[mine, :].astype(jnp.float32)
        part[mine, :] = ((own + others[0]) + (others[1] + others[2])).astype(part.dtype)
        kept.start()
        for copy in gather:
            copy.start()

    def collect():
        kept.wait()
        wait_all(sems.at[9])
        back[last].start()

    def unfold(n):
        def run():
            back[n].wait()
            if n == last and not z_peers:
                kept.wait()
            if n > 0:
                back[n - 1].start()

        return run

    steps = [first] + [fold(n) for n in range(last + 1)]
    if z_peers:
        steps += [settle, collect]
    return steps + [unfold(n) for n in range(last, -1, -1)]


def small_job(part, total, recv, sems, halves, z_peers):
    offset, size, copies, back, kept_cols = 0, part.shape[1], [], [], []
    for n, (partner, bit) in enumerate(halves):
        size = size // 2
        keep = pl.ds(pl.multiple_of(offset + bit * size, size), size)
        give = pl.ds(pl.multiple_of(offset + (1 - bit) * size, size), size)
        copies.append(
            pltpu.make_async_remote_copy(
                src_ref=part.at[:, give],
                dst_ref=recv[n],
                send_sem=sems.at[0],
                recv_sem=sems.at[1 + n],
                device_id=partner,
                device_id_type=MESH,
            )
        )
        back.append(
            pltpu.make_async_remote_copy(
                src_ref=total.at[:, keep],
                dst_ref=total.at[:, keep],
                send_sem=sems.at[0],
                recv_sem=sems.at[6 + n],
                device_id=partner,
                device_id_type=MESH,
            )
        )
        kept_cols.append(keep)
        offset = offset + bit * size
    mine = kept_cols[-1]
    spread = [
        pltpu.make_async_remote_copy(
            src_ref=part.at[:, mine],
            dst_ref=recv[3].at[n],
            send_sem=sems.at[0],
            recv_sem=sems.at[4],
            device_id=peer,
            device_id_type=MESH,
        )
        for n, (peer, _) in enumerate(z_peers)
    ]

    def first():
        copies[0].start()

    def fold(n):
        def run():
            copies[n].wait()
            part[:, kept_cols[n]] = part[:, kept_cols[n]] + recv[n][...]
            if n + 1 < len(copies):
                copies[n + 1].start()
            else:
                for copy in spread:
                    copy.start()

        return run

    def settle():
        pltpu.make_async_remote_copy(
            src_ref=recv[3],
            dst_ref=recv[3],
            send_sem=sems.at[0],
            recv_sem=sems.at[4],
            device_id=z_peers[0][0],
            device_id_type=MESH,
        ).wait()
        total[:, mine] = (part[:, mine] + recv[3][0]) + (recv[3][1] + recv[3][2])
        back[-1].start()

    def unfold(n):
        def run():
            back[n].wait()
            if n > 0:
                back[n - 1].start()

        return run

    return [first] + [fold(n) for n in range(3)] + [settle] + [unfold(n) for n in (2, 1, 0)]


def table_kernel(
    local,
    block_tables,
    seq,
    x_hbm,
    cot_hbm,
    lengths_ref,
    counts_ref,
    w_in_hbm,
    w_out_hbm,
    w_up_hbm,
    w_down_hbm,
    *refs,
):
    vector_refs, refs = refs[:VECTORS], refs[VECTORS:]
    (
        act_hbm,
        xgrad_hbm,
        t_in,
        t_out,
        t_up,
        t_down,
        t_small,
        w_in,
        w_out,
        w_up,
        w_down,
        vectors,
        g_in,
        g_out,
        g_up,
        g_down,
        small,
        in_low,
        cot_low,
        stream,
        queries,
        kv,
        attended,
        log_totals,
        norm1,
        inverse1,
        mid_low,
        slope,
        act_low,
        norm2,
        inverse2,
        meta,
        bias_col,
        valid,
        ffn_low,
        hidden_low,
        branch_low,
        attended_low,
        centers,
        dq_t,
        dkv_own,
        dkv_send,
        dkv_recv,
        proj_low,
        staged,
        recv_in,
        recv_out,
        recv_up,
        recv_down,
        recv_small,
        x_send,
        x_recv,
        cot_send,
        cot_recv,
        act_send,
        act_recv,
        xg_send,
        xg_recv,
        local_sem,
        kv_sem,
        dkv_sem,
        meta_sem,
        job_sem,
    ) = refs
    upstream = stream
    rows = block_tables * local
    dim = in_low.shape[-1]
    head_dim = dim // HEADS
    scale = head_dim**-0.5
    tiles = rows // TILE
    group_heads = HEADS // GROUPS
    group_width = group_heads * head_dim
    t = lax.axis_index("tables")
    r = lax.axis_index("rows")
    core = lax.rem(t, 2)
    side = r // block_tables
    slot = lax.rem(r, block_tables)
    peer = (t + 1 - 2 * core, r)
    own_rows = pl.multiple_of(core * rows, rows)
    peer_rows = pl.multiple_of((1 - core) * rows, rows)

    x_side, y_side, z_side = lax.rem(r, 2), t // 2, r // 2
    x_next = (t, r + 1 - 2 * x_side)
    y_next = (t + 2 - 4 * y_side, r)
    z_next = [
        (z_side + 1 - 2 * lax.rem(z_side, 2)),
        lax.rem(z_side + 2, 4),
        3 - z_side,
    ]
    z_peers = [((t, 2 * z + x_side), z) for z in z_next]

    def choose(first, second):
        return core * second + (1 - core) * first

    sides = {
        "c": (peer, core),
        "x": (x_next, x_side),
        "y": (y_next, y_side),
        "n": (z_peers[0][0], lax.rem(z_side, 2)),
        "f": (z_peers[1][0], z_side // 2),
    }

    def both(first, second):
        if first == second:
            return sides[first]
        (one, one_bit), (two, two_bit) = sides[first], sides[second]
        device = (choose(one[0], two[0]), choose(one[1], two[1]))
        return device, choose(one_bit, two_bit)

    def path(kind):
        first, second = PATHS[kind]
        return [both(*pair) for pair in zip(first, second)]

    def partner(k):
        return (t - core + side, block_tables * core + k)

    def is_self(k):
        return jnp.logical_and(core == side, slot == k)

    barrier = pltpu.get_barrier_semaphore()
    greeted = [peer, x_next, y_next] + [device for device, _ in z_peers]
    for device in greeted:
        pl.semaphore_signal(barrier, inc=1, device_id=device, device_id_type=MESH)
    for k in range(block_tables):

        @pl.when(jnp.logical_not(is_self(k)))
        def _():
            pl.semaphore_signal(barrier, inc=1, device_id=partner(k), device_id_type=MESH)

    pl.semaphore_wait(
        barrier, len(greeted) + jnp.where(core == side, block_tables - 1, block_tables)
    )

    def spread(source, target, send_sem, recv_sem, own_sem):
        def remote(k, at):
            return pltpu.make_async_remote_copy(
                src_ref=source(k),
                dst_ref=target(at),
                send_sem=send_sem.at[k],
                recv_sem=recv_sem.at[at],
                device_id=partner(k),
                device_id_type=MESH,
            )

        def kept(k):
            return pltpu.make_async_copy(source(k), target(k), own_sem)

        def start():
            for k in range(block_tables):

                @pl.when(is_self(k))
                def _():
                    kept(k).start()

                @pl.when(jnp.logical_not(is_self(k)))
                def _():
                    remote(k, slot).start()

        def arrive():
            for k in range(block_tables):

                @pl.when(is_self(k))
                def _():
                    kept(k).wait()

                @pl.when(jnp.logical_not(is_self(k)))
                def _():
                    remote(k, k).wait_recv()

        def left():
            for k in range(block_tables):

                @pl.when(jnp.logical_not(is_self(k)))
                def _():
                    remote(k, slot).wait_send()

        return start, arrive, left

    def by_table(ref):
        return lambda k: ref.at[k]

    def by_rows(ref):
        return lambda k: ref.at[pl.ds(k * local, local)]

    x_start, x_arrive, x_left = spread(by_table(x_hbm), by_rows(in_low.at[0]), x_send, x_recv, local_sem.at[0])
    cot_start, cot_arrive, cot_left = spread(by_table(cot_hbm), by_rows(cot_low), cot_send, cot_recv, local_sem.at[1])
    act_start, act_arrive, act_left = spread(by_rows(staged.at[0]), by_table(act_hbm), act_send, act_recv, local_sem.at[2])
    xg_start, xg_arrive, xg_left = spread(by_rows(staged.at[1]), by_table(xgrad_hbm), xg_send, xg_recv, local_sem.at[3])

    def swap(source, target, sems):
        return pltpu.make_async_remote_copy(
            src_ref=source,
            dst_ref=target,
            send_sem=sems.at[0],
            recv_sem=sems.at[1],
            device_id=peer,
            device_id_type=MESH,
        )

    x_start()
    loads = [
        pltpu.make_async_copy(source, target, local_sem.at[4 + n])
        for n, (source, target) in enumerate(
            ((w_in_hbm, w_in), (w_out_hbm, w_out), (w_up_hbm, w_up), (w_down_hbm, w_down))
        )
    ]
    for load in loads:
        load.start()
    for n, ref in enumerate(vector_refs):
        for layer in range(LAYERS):
            vectors[pl.ds(layer * VECTORS + n, 1), pl.ds(0, ref.shape[1])] = ref[...].astype(
                jnp.float32
            )[layer : layer + 1, :]
    for k in range(block_tables):
        meta[core, pl.ds(k, 1), :] = jnp.full((1, 128), lengths_ref[k], jnp.int32)
        meta[core, pl.ds(block_tables + k, 1), :] = jnp.full((1, 128), counts_ref[k], jnp.int32)
    meta_copy = swap(meta.at[core], meta.at[core], meta_sem)
    meta_copy.start()
    small[...] = jnp.zeros_like(small)
    meta_copy.wait()
    length = meta[side, pl.ds(slot, 1), :][:, :1]
    train = meta[side, pl.ds(slot + block_tables, 1), :][:, :1]
    bias_col[...] = jnp.where(lax.broadcasted_iota(jnp.int32, (seq, 1), 0) < train, 0.0, MASKED)
    valid[...] = jnp.where(
        lax.broadcasted_iota(jnp.int32, (rows, 1), 0) + core * rows < length, 1.0, 0.0
    )
    small[0, pl.ds(13, 1), pl.ds(0, 128)] = jnp.broadcast_to(column_sum(valid[...]), (1, 128))
    x_arrive()
    cot_start()
    loads[0].wait()

    def vector(index, layer, width):
        return vectors[pl.ds(layer * VECTORS + index, 1), pl.ds(0, width)]

    def add_small(layer, index, values):
        at = (layer, pl.ds(index, 1), pl.ds(0, values.shape[-1]))
        small[at] = small[at] + values

    def each_tile(body, after=()):
        def step(i, carry):
            body(pl.ds(pl.multiple_of(i * TILE, TILE), TILE))
            for n, run in enumerate(after):

                @pl.when(i == n)
                def _():
                    run()

            return carry

        lax.fori_loop(0, tiles, step, 0)

    def head_cols(h):
        return pl.ds(pl.multiple_of(h * head_dim, head_dim), head_dim)

    def forward(layer):
        def project(at):
            projected = dot(in_low[layer, at, :], w_in[layer])
            queries[layer, at, :] = (
                (projected[:, :dim] + vector(0, layer, dim)) * scale
            ).astype(jnp.bfloat16)
            own = pl.ds(pl.multiple_of(own_rows + at.start, TILE), TILE)
            key_rows = projected[:, dim : 2 * dim].astype(jnp.bfloat16)
            value_rows = (projected[:, 2 * dim :] + vector(1, layer, dim)).astype(jnp.bfloat16)
            for h in range(HEADS):
                cols = slice(h * head_dim, (h + 1) * head_dim)
                kv[layer, h, own, pl.ds(0, head_dim)] = key_rows[:, cols]
                kv[layer, h, own, pl.ds(head_dim, head_dim)] = value_rows[:, cols]

        each_tile(project)

        def kv_copy(h):
            mine = kv.at[layer, h, pl.ds(own_rows, rows)]
            return swap(mine, mine, kv_sem.at[layer, h])

        for h in range(HEADS):
            kv_copy(h).start()

        def attend(h, carry):
            cols = head_cols(h)
            kv_copy(h).wait()
            scores = dot(kv[layer, h, :, pl.ds(0, head_dim)], queries[layer, :, cols], NT)
            scores = scores + bias_col[...]
            row_max = jnp.max(scores, axis=0, keepdims=True)
            exponent = jnp.exp(scores - row_max)
            total = jnp.sum(exponent, axis=0, keepdims=True)
            mixed = dot(kv[layer, h, :, pl.ds(head_dim, head_dim)], exponent.astype(jnp.bfloat16), TN)
            attended[layer, :, cols] = jnp.transpose(mixed * (1.0 / total)).astype(jnp.bfloat16)
            log_totals[layer, pl.ds(h, 1), :] = row_max + jnp.log(total)
            return carry

        lax.fori_loop(0, HEADS, attend, 0)
        if layer == 0:
            for load in loads[1:]:
                load.wait()

        def dense(at):
            below = in_low[0, at, :].astype(jnp.float32) if layer == 0 else stream[at, :]
            branch = dot(attended[layer, at, :], w_out[layer]) + vector(2, layer, dim)
            valid_cells = valid[at, :]
            add_small(layer, 10, column_sum(below * below * valid_cells))
            add_small(layer, 11, column_sum(branch * branch * valid_cells))
            summed = below + branch
            centered = summed - row_mean(summed)
            inverse = lax.rsqrt(row_mean(centered * centered) + EPSILON)
            normed = centered * inverse
            norm1[layer, at, :] = normed
            inverse1[layer, at, :] = inverse
            first_out = normed * vector(3, layer, dim) + vector(4, layer, dim)
            mid = first_out.astype(jnp.bfloat16)
            mid_low[layer, at, :] = mid
            hidden = dot(mid, w_up[layer]) + vector(5, layer, 2 * dim)
            cdf = 0.5 + 0.5 * lax.erf(hidden * (0.5**0.5))
            slope[layer, at, :] = cdf + hidden * (
                jnp.exp(hidden * hidden * -0.5) * 0.3989422804014327
            )
            act = (hidden * cdf).astype(jnp.bfloat16)
            act_low[layer, at, :] = act
            ffn_out = dot(act, w_down[layer]) + vector(6, layer, dim)
            add_small(layer, 12, column_sum(ffn_out * ffn_out * valid_cells))
            summed = first_out + ffn_out
            centered = summed - row_mean(summed)
            inverse = lax.rsqrt(row_mean(centered * centered) + EPSILON)
            normed = centered * inverse
            norm2[layer, at, :] = normed
            inverse2[layer, at, :] = inverse
            out = normed * vector(7, layer, dim) + vector(8, layer, dim)
            if layer + 1 < LAYERS:
                stream[at, :] = out
                in_low[layer + 1, at, :] = out.astype(jnp.bfloat16)
            else:
                staged[0, at, :] = (out * valid_cells).astype(jnp.bfloat16)

        each_tile(dense)

    for layer in range(LAYERS):
        forward(layer)
    act_start()
    cot_arrive()

    jobs = []

    points = list(SCHEDULE)

    def begin(steps):
        jobs.append(list(steps))
        jobs[-1].pop(0)()

    def tick():
        for index in points.pop(0):
            if index < len(jobs) and jobs[index]:
                jobs[index].pop(0)()

    def reduce(part, total, recv):
        halves = path(KINDS[len(jobs)])
        peers = z_peers if len(halves) == 3 else []
        begin(reduce_job(part, total, recv, job_sem.at[len(jobs)], halves, peers, z_side))

    def reduce_halves(part, total, recv):
        width = part.shape[1] // HALVES
        for n in range(HALVES):
            cols = pl.ds(n * width, width)
            reduce(
                part.at[:, cols],
                total.at[:, cols],
                [ref.at[:, cols] for ref in recv],
            )

    def backward(layer):
        def recv_of(refs):
            return [ref.at[layer] for ref in refs]

        def enter(at):
            if layer == LAYERS - 1:
                up = cot_low[at, :].astype(jnp.float32) * valid[at, :]
            else:
                up = upstream[at, :]
            normed = norm2[layer, at, :]
            add_small(layer, 8, column_sum(up * normed))
            add_small(layer, 9, column_sum(up))
            scaled = up * vector(7, layer, dim)
            second = inverse2[layer, at, :] * (
                scaled - row_mean(scaled) - normed * row_mean(scaled * normed)
            )
            upstream[at, :] = second
            ffn = second.astype(jnp.bfloat16)
            ffn_low[at, :] = ffn
            add_small(layer, 7, column_sum(ffn.astype(jnp.float32)))

        each_tile(enter)
        g_down[layer] = dot(act_low[layer], ffn_low[...], TN).astype(jnp.bfloat16)
        tick()
        reduce_halves(g_down.at[layer], t_down.at[layer], recv_of(recv_down))

        def dense(at):
            hidden = (dot(ffn_low[at, :], w_down[layer], NT) * slope[layer, at, :]).astype(
                jnp.bfloat16
            )
            hidden_low[at, :] = hidden
            add_small(layer, 6, column_sum(hidden.astype(jnp.float32)))
            first = upstream[at, :] + dot(hidden, w_up[layer], NT)
            normed = norm1[layer, at, :]
            add_small(layer, 4, column_sum(first * normed))
            add_small(layer, 5, column_sum(first))
            scaled = first * vector(3, layer, dim)
            residual = inverse1[layer, at, :] * (
                scaled - row_mean(scaled) - normed * row_mean(scaled * normed)
            )
            upstream[at, :] = residual
            branch = residual.astype(jnp.bfloat16)
            branch_low[at, :] = branch
            add_small(layer, 3, column_sum(branch.astype(jnp.float32)))
            low = dot(branch, w_out[layer], NT).astype(jnp.bfloat16)
            attended_low[at, :] = low
            product = low.astype(jnp.float32) * attended[layer, at, :].astype(jnp.float32)
            lane = lax.broadcasted_iota(jnp.int32, (TILE, head_dim), 1)
            held = jnp.zeros((TILE, head_dim), jnp.float32)
            for h in range(HEADS):
                center = jnp.sum(product[:, h * head_dim : (h + 1) * head_dim], axis=-1, keepdims=True)
                held = jnp.where(lane == h, center, held)
            centers[:, at] = jnp.transpose(held)[:8, :]

        each_tile(dense, (tick,) * tiles)
        g_up[layer] = dot(mid_low[layer], hidden_low[...], TN).astype(jnp.bfloat16)
        tick()
        reduce_halves(g_up.at[layer], t_up.at[layer], recv_of(recv_up))
        g_out[layer] = dot(attended[layer], branch_low[...], TN).astype(jnp.bfloat16)
        tick()
        reduce(g_out.at[layer], t_out.at[layer], recv_of(recv_out))

        def attend(group, base, first, keep):
            def step(i, carry):
                h = group * group_heads + i // tiles
                j = pl.multiple_of(lax.rem(i, tiles) * TILE, TILE)
                at = pl.ds(pl.multiple_of(base + j, TILE), TILE)
                cols = head_cols(h)
                key_rows = kv[layer, h, at, pl.ds(0, head_dim)]
                query_rows = queries[layer, :, cols]
                grads = attended_low[:, cols]
                probs = jnp.exp(
                    dot(key_rows, query_rows, NT) + bias_col[at, :] - log_totals[layer, pl.ds(h, 1), :]
                )
                value_part = dot(probs.astype(jnp.bfloat16), grads)
                probs_grad = dot(kv[layer, h, at, pl.ds(head_dim, head_dim)], grads, NT)
                scores_low = (probs * (probs_grad - centers[pl.ds(h, 1), :])).astype(
                    jnp.bfloat16
                )
                key_part = dot(scores_low, query_rows)
                query_part = dot(key_rows, scores_low, TN)
                if first:
                    query_part = jnp.where(j == 0, query_part, query_part + dq_t[cols, :])
                else:
                    query_part = query_part + dq_t[cols, :]
                dq_t[cols, :] = query_part
                inside = i // tiles * head_dim
                keep(pl.ds(j, TILE), pl.ds(pl.multiple_of(inside, head_dim), head_dim), key_part)
                keep(
                    pl.ds(j, TILE),
                    pl.ds(pl.multiple_of(group_width + inside, head_dim), head_dim),
                    value_part,
                )
                return carry

            lax.fori_loop(0, group_heads * tiles, step, 0)

        def dkv_copy(group):
            return swap(
                dkv_send.at[layer, group], dkv_recv.at[layer, group], dkv_sem.at[layer, group]
            )

        def attend_peer(group):
            def keep(at, cols, part):
                dkv_send[layer, group, at, cols] = part.astype(jnp.bfloat16)

            attend(group, peer_rows, True, keep)
            dkv_copy(group).start()
            tick()

        def attend_own(group):
            def keep(at, cols, part):
                dkv_own[group % 2, at, cols] = part

            attend(group, own_rows, False, keep)
            tick()

        def finish_group(group):
            dkv_copy(group).wait()

            def finish(at):
                group_rows = pl.ds(group * group_width, group_width)
                query = jnp.transpose(dq_t[group_rows, at]).astype(jnp.bfloat16)
                pair = (
                    dkv_own[group % 2, at, :] + dkv_recv[layer, group, at, :].astype(jnp.float32)
                ).astype(jnp.bfloat16)
                proj_low[group, at, pl.ds(0, group_width)] = query
                proj_low[group, at, pl.ds(group_width, 2 * group_width)] = pair
                cols = pl.ds(group * group_width, group_width)
                small[layer, pl.ds(0, 1), cols] += column_sum(query.astype(jnp.float32)) * scale
                small[layer, pl.ds(1, 1), cols] += column_sum(
                    pair[:, group_width:].astype(jnp.float32)
                )

            each_tile(finish)
            grad = dot(in_low[layer], proj_low[group], TN)
            g_in[layer, group, :, pl.ds(0, group_width)] = (grad[:, :group_width] * scale).astype(
                jnp.bfloat16
            )
            g_in[layer, group, :, pl.ds(group_width, 2 * group_width)] = grad[
                :, group_width:
            ].astype(jnp.bfloat16)
            tick()
            reduce(
                g_in.at[layer, group],
                t_in.at[layer, group],
                [ref.at[layer, group] for ref in recv_in],
            )

        for group in range(GROUPS):
            attend_peer(group)
            if group > 0:
                finish_group(group - 1)
            attend_own(group)
        finish_group(GROUPS - 1)
        begin(
            small_job(
                small.at[layer],
                t_small.at[layer],
                [ref.at[layer] for ref in recv_small],
                job_sem.at[len(jobs)],
                path("A"),
                z_peers,
            )
        )

        def pass_down(at):
            grad = upstream[at, :]
            for group in range(GROUPS):
                for n in range(3):
                    part = dot(
                        proj_low[group, at, pl.ds(n * group_width, group_width)],
                        w_in[layer, :, pl.ds(n * dim + group * group_width, group_width)],
                        NT,
                    )
                    grad = grad + (part * scale if n == 0 else part)
            if layer > 0:
                upstream[at, :] = grad
            else:
                staged[1, at, :] = grad.astype(jnp.bfloat16)

        each_tile(pass_down)
        tick()
        if layer == 0:
            xg_start()

    for layer in reversed(range(LAYERS)):
        backward(layer)
    tick()
    while any(jobs):
        for steps in jobs:
            if steps:
                steps.pop(0)()
    act_arrive()
    xg_arrive()
    x_left()
    cot_left()
    act_left()
    xg_left()


def widen_kernel(f_in, f_out, f_up, f_down, f_act, f_xgrad, small, *refs):
    act, xgrad, in_weight, out_weight, up_weight, down_weight, root_means = refs[:7]
    low = refs[16:22]
    wide = refs[22:28]
    read_sem, write_sem = refs[28:]
    groups, width = f_in.shape[1], f_in.shape[3] // 3
    half = f_in.shape[2] // 2

    def table_parts(n, source, target):
        def convert():
            for k in range(source.shape[0]):
                wide[n][:, k, :] = low[n][k].astype(jnp.float32)

        return (source, low[n], convert, wide[n], target)

    def plain_part(n, source, target, layer):
        def convert():
            wide[n][layer] = low[n][layer].astype(jnp.float32)

        return (
            source.at[layer],
            low[n].at[layer],
            convert,
            wide[n].at[layer],
            target.at[layer],
        )

    def in_part(layer, start):
        at = pl.ds(start, half)

        def convert():
            for group in range(groups):
                for n in range(3):
                    wide[2][layer, at, pl.ds((n * groups + group) * width, width)] = low[2][
                        layer, group, at, pl.ds(n * width, width)
                    ].astype(jnp.float32)

        return (
            f_in.at[layer, :, at],
            low[2].at[layer, :, at],
            convert,
            wide[2].at[layer, at],
            in_weight.at[layer, at],
        )

    parts = [plain_part(3, f_out, out_weight, layer) for layer in range(LAYERS)]
    parts += [table_parts(0, f_act, act), table_parts(1, f_xgrad, xgrad)]
    for layer in range(LAYERS):
        parts += [plain_part(4, f_up, up_weight, layer), plain_part(5, f_down, down_weight, layer)]
        parts += [in_part(layer, 0), in_part(layer, half)]
    reads = [
        pltpu.make_async_copy(source, target, read_sem.at[n])
        for n, (source, target, _, _, _) in enumerate(parts)
    ]
    writes = [
        pltpu.make_async_copy(source, target, write_sem.at[n])
        for n, (_, _, _, source, target) in enumerate(parts)
    ]
    for copy in reads:
        copy.start()
    for copy, write, part in zip(reads, writes, parts):
        copy.wait()
        part[2]()
        write.start()
    for ref, row in zip(refs[7:16], (0, 1, 3, 4, 5, 6, 7, 8, 9)):
        for layer in range(LAYERS):
            ref[pl.ds(layer, 1), :] = small[layer, pl.ds(row, 1), pl.ds(0, ref.shape[1])]
    dim = f_act.shape[2]
    count = small[0, pl.ds(13, 1), pl.ds(0, 1)]
    for layer in range(LAYERS):
        sums = jnp.sum(small[layer, pl.ds(8, 8), pl.ds(0, dim)], axis=-1, keepdims=True)
        for n in range(3):
            root_means[pl.ds(layer, 1), pl.ds(n, 1)] = jnp.sqrt(
                sums[2 + n : 3 + n, :] / (count * dim)
            )
    for write in writes:
        write.wait()


def table_device(tables, row_parts, *operands):
    (
        tables_in,
        in_weight,
        query_bias,
        value_bias,
        out_weight,
        out_bias,
        attn_gain,
        attn_shift,
        up_weight,
        up_bias,
        down_weight,
        down_bias,
        ffn_gain,
        ffn_shift,
        cotangent,
        lengths,
        train_counts,
    ) = operands
    local, block_tables, dim = tables_in.shape
    rows = local * block_tables
    seq = local * row_parts
    hidden = up_weight.shape[-1]
    head_dim = dim // HEADS
    f32, bf16 = jnp.float32, jnp.bfloat16
    groups = GROUPS
    vmem = pl.BlockSpec(memory_space=pltpu.VMEM)
    hbm = pl.BlockSpec(memory_space=pl.ANY)
    smem = pl.BlockSpec(memory_space=pltpu.SMEM)
    block = (block_tables, local, dim)
    dma = pltpu.SemaphoreType.DMA
    in_part = (LAYERS, groups, dim, 3 * dim // groups)
    shards = 8 * row_parts // 2

    def received(shape):
        lead, (height, width) = shape[:-2], shape[-2:]
        return [
            [pltpu.VMEM(lead + (height // n, width), bf16) for n in (2, 4, 8)]
            + [pltpu.VMEM(lead + (3 * height // shards, width), bf16)]
        ]

    act, xgrad, *sums, small = pl.pallas_call(
        functools.partial(table_kernel, local, block_tables, seq),
        out_shape=(
            jax.ShapeDtypeStruct(block, bf16),
            jax.ShapeDtypeStruct(block, bf16),
            jax.ShapeDtypeStruct(in_part, bf16),
            jax.ShapeDtypeStruct(out_weight.shape, bf16),
            jax.ShapeDtypeStruct(up_weight.shape, bf16),
            jax.ShapeDtypeStruct(down_weight.shape, bf16),
            jax.ShapeDtypeStruct((LAYERS, 16, hidden), f32),
        ),
        in_specs=[hbm, hbm, smem, smem] + [hbm] * 4 + [vmem] * VECTORS,
        out_specs=(hbm,) * 6 + (vmem,),
        scratch_shapes=[
            pltpu.VMEM(in_weight.shape, bf16),
            pltpu.VMEM(out_weight.shape, bf16),
            pltpu.VMEM(up_weight.shape, bf16),
            pltpu.VMEM(down_weight.shape, bf16),
            pltpu.VMEM((LAYERS * VECTORS, hidden), f32),
            pltpu.VMEM(in_part, bf16),
            pltpu.VMEM(out_weight.shape, bf16),
            pltpu.VMEM(up_weight.shape, bf16),
            pltpu.VMEM(down_weight.shape, bf16),
            pltpu.VMEM((LAYERS, 16, hidden), f32),
            pltpu.VMEM((LAYERS, rows, dim), bf16),
            pltpu.VMEM((rows, dim), bf16),
            pltpu.VMEM((rows, dim), f32),
            pltpu.VMEM((LAYERS, rows, dim), bf16),
            pltpu.VMEM((LAYERS, HEADS, seq, 2 * head_dim), bf16),
            pltpu.VMEM((LAYERS, rows, dim), bf16),
            pltpu.VMEM((LAYERS, 8, rows), f32),
            pltpu.VMEM((LAYERS, rows, dim), f32),
            pltpu.VMEM((LAYERS, rows, 1), f32),
            pltpu.VMEM((LAYERS, rows, dim), bf16),
            pltpu.VMEM((LAYERS, rows, hidden), f32),
            pltpu.VMEM((LAYERS, rows, hidden), bf16),
            pltpu.VMEM((LAYERS, rows, dim), f32),
            pltpu.VMEM((LAYERS, rows, 1), f32),
            pltpu.VMEM((2, 2 * block_tables, 128), jnp.int32),
            pltpu.VMEM((seq, 1), f32),
            pltpu.VMEM((rows, 1), f32),
            pltpu.VMEM((rows, dim), bf16),
            pltpu.VMEM((rows, hidden), bf16),
            pltpu.VMEM((rows, dim), bf16),
            pltpu.VMEM((rows, dim), bf16),
            pltpu.VMEM((8, rows), f32),
            pltpu.VMEM((dim, rows), f32),
            pltpu.VMEM((2, rows, 2 * dim // groups), f32),
            pltpu.VMEM((LAYERS, groups, rows, 2 * dim // groups), bf16),
            pltpu.VMEM((LAYERS, groups, rows, 2 * dim // groups), bf16),
            pltpu.VMEM((groups, rows, 3 * dim // groups), bf16),
            pltpu.VMEM((2, rows, dim), bf16),
        ]
        + received(in_part)
        + received(out_weight.shape)
        + received(up_weight.shape)
        + received(down_weight.shape)
        + [
            [pltpu.VMEM((LAYERS, 16, hidden // n), f32) for n in (2, 4, 8)]
            + [pltpu.VMEM((LAYERS, 3, 16, hidden // 8), f32)]
        ]
        + [dma((block_tables,))] * 8
        + [
            dma((8,)),
            dma((LAYERS, HEADS, 2)),
            dma((LAYERS, groups, 2)),
            dma((2,)),
            dma((LAYERS * (2 * HALVES + 2 + groups), 12)),
        ],
        compiler_params=pltpu.CompilerParams(
            collective_id=0, has_side_effects=True, vmem_limit_bytes=62 * 1024 * 1024
        ),
    )(
        jnp.swapaxes(tables_in, 0, 1),
        jnp.swapaxes(cotangent, 0, 1),
        lengths,
        train_counts,
        in_weight,
        out_weight,
        up_weight,
        down_weight,
        query_bias,
        value_bias,
        out_bias,
        attn_gain,
        attn_shift,
        up_bias,
        down_bias,
        ffn_gain,
        ffn_shift,
    )
    vector = jax.ShapeDtypeStruct((LAYERS, dim), f32)
    wide_vector = jax.ShapeDtypeStruct((LAYERS, hidden), f32)
    shapes = [
        jax.ShapeDtypeStruct(tables_in.shape, f32),
        jax.ShapeDtypeStruct(tables_in.shape, f32),
        jax.ShapeDtypeStruct(in_weight.shape, f32),
        jax.ShapeDtypeStruct(out_weight.shape, f32),
        jax.ShapeDtypeStruct(up_weight.shape, f32),
        jax.ShapeDtypeStruct(down_weight.shape, f32),
        jax.ShapeDtypeStruct((LAYERS, 3), f32),
    ] + [vector] * 5 + [wide_vector] + [vector] * 3
    outs = pl.pallas_call(
        widen_kernel,
        out_shape=shapes,
        in_specs=[hbm] * 6 + [vmem],
        out_specs=[hbm] * 6 + [vmem] * 10,
        scratch_shapes=[
            pltpu.VMEM(shape, dtype)
            for dtype, in_shape, rows_shape in (
                (bf16, in_part, block),
                (f32, in_weight.shape, tables_in.shape),
            )
            for shape in (
                rows_shape,
                rows_shape,
                in_shape,
                out_weight.shape,
                up_weight.shape,
                down_weight.shape,
            )
        ]
        + [dma((5 * LAYERS + 2,))] * 2,
        compiler_params=pltpu.CompilerParams(vmem_limit_bytes=62 * 1024 * 1024),
    )(*sums, act, xgrad, small)
    act, xgrad, g_in, g_out, g_up, g_down, root_means = outs[:7]
    query, value, out, gain1, shift1, up, down, gain2, shift2 = outs[7:]
    return (
        act,
        xgrad,
        g_in,
        query,
        value,
        g_out,
        out,
        gain1,
        shift1,
        g_up,
        up,
        g_down,
        down,
        gain2,
        shift2,
        root_means,
    )


def per_device(tables, row_parts, *operands):
    local, block_tables, dim = operands[0].shape
    if tables == 4 and row_parts == 2 * block_tables and local * row_parts <= 1024:
        return table_device(tables, row_parts, *operands)
    return gathered_device(*operands)


def solution(mesh):
    placed = (
        P("rows", "tables", None),
        P(),
        P(),
        P(),
        P(),
        P(),
        P(),
        P(),
        P(),
        P(),
        P(),
        P(),
        P(),
        P(),
        P("rows", "tables", None),
        P("tables"),
        P("tables"),
    )
    return jax.shard_map(
        functools.partial(per_device, mesh.shape["tables"], mesh.shape["rows"]),
        mesh=mesh,
        in_specs=placed,
        out_specs=(
            P("rows", "tables", None),
            P("rows", "tables", None),
            P(),
            P(),
            P(),
            P(),
            P(),
            P(),
            P(),
            P(),
            P(),
            P(),
            P(),
            P(),
            P(),
            P(),
        ),
        check_vma=False,
    )
```

```python
import functools
import math

import jax
import jax.numpy as jnp
from jax import lax
from jax.experimental import pallas as pl
from jax.experimental.pallas import tpu as pltpu
from jax.sharding import PartitionSpec as P

D = 512
HEADS = 4
LAYERS = 2


EPSILON = 1e-05
MASKED = -1e30


def norm_forward(values, gain_row, offsets):
    average = jnp.mean(values, axis=-1, keepdims=True)
    centered = values - average
    variance = jnp.mean(centered * centered, axis=-1, keepdims=True)
    inverse = lax.rsqrt(variance + EPSILON)
    normed = centered * inverse
    return (normed * gain_row + offsets, normed, inverse)


def norm_backward(upstream, normed, inverse, gain_row):
    scaled = upstream * gain_row
    average = jnp.mean(scaled, axis=-1, keepdims=True)
    projection = jnp.mean(scaled * normed, axis=-1, keepdims=True)
    return inverse * (scaled - average - normed * projection)


def gelu_exact(values):
    return jax.nn.gelu(values, approximate=False)


def split_heads(values):
    return values.reshape(values.shape[0], values.shape[1], HEADS, values.shape[2] // HEADS)


def merge_heads(values):
    return values.reshape(values.shape[0], values.shape[1], values.shape[2] * values.shape[3])


def table_scores(queries, key_rows, usable):
    scores = jnp.einsum(
        "ibhe,jbhe->bhij",
        split_heads(queries),
        split_heads(key_rows),
        preferred_element_type=jnp.float32,
    )
    return jnp.where(usable[:, None, None, :], scores, MASKED)


def row_sums(values):
    return jnp.sum(values.astype(jnp.float32), axis=(0, 1))


def gathered_device(
    tables_in,
    in_weight,
    query_bias,
    value_bias,
    out_weight,
    out_bias,
    attn_gain,
    attn_shift,
    up_weight,
    up_bias,
    down_weight,
    down_bias,
    ffn_gain,
    ffn_shift,
    cotangent,
    lengths,
    train_counts,
):
    local_rows = tables_in.shape[0]
    seq_rows = local_rows * lax.axis_size("rows")
    positions = lax.axis_index("rows") * local_rows + jnp.arange(local_rows, dtype=jnp.int32)
    valid_rows = (positions[:, None] < lengths[None, :]).astype(jnp.float32)
    valid_cells = valid_rows[:, :, None]
    usable = jnp.arange(seq_rows, dtype=jnp.int32)[None, :] < train_counts[:, None]
    score_scale = (D // HEADS) ** (-0.5)
    column_scale = jnp.concatenate(
        [jnp.full((D,), score_scale, jnp.float32), jnp.ones((2 * D,), jnp.float32)]
    )
    stream = tables_in.astype(jnp.float32)
    stored = []
    squares = []
    for layer_index in range(LAYERS):
        in_low = stream.astype(jnp.bfloat16)
        projected = jnp.einsum(
            "ibd,de->ibe", in_low, in_weight[layer_index], preferred_element_type=jnp.float32
        )
        queries = ((projected[:, :, :D] + query_bias[layer_index]) * score_scale).astype(
            jnp.bfloat16
        )
        key_rows = projected[:, :, D : 2 * D].astype(jnp.bfloat16)
        value_rows = (projected[:, :, 2 * D :] + value_bias[layer_index]).astype(jnp.bfloat16)
        all_keys, all_values = (
            lax.all_gather(key_rows, "rows", axis=0, tiled=True),
            lax.all_gather(value_rows, "rows", axis=0, tiled=True),
        )
        scores = table_scores(queries, all_keys, usable)
        row_max = jnp.max(scores, axis=-1, keepdims=True)
        exponent = jnp.exp(scores - row_max)
        row_total = jnp.sum(exponent, axis=-1, keepdims=True)
        probs_low = (exponent / row_total).astype(jnp.bfloat16)
        log_total = (row_max + jnp.log(row_total))[..., 0]
        attended = merge_heads(
            jnp.einsum(
                "bhij,jbhe->ibhe",
                probs_low,
                split_heads(all_values),
                preferred_element_type=jnp.float32,
            )
        ).astype(jnp.bfloat16)
        branch = (
            jnp.einsum(
                "ibd,de->ibe", attended, out_weight[layer_index], preferred_element_type=jnp.float32
            )
            + out_bias[layer_index]
        )
        first_out, first_norm, first_inverse = norm_forward(
            stream + branch, attn_gain[layer_index], attn_shift[layer_index]
        )
        mid_low = first_out.astype(jnp.bfloat16)
        hidden = (
            jnp.einsum(
                "ibd,df->ibf", mid_low, up_weight[layer_index], preferred_element_type=jnp.float32
            )
            + up_bias[layer_index]
        )
        act_low = gelu_exact(hidden).astype(jnp.bfloat16)
        ffn_out = (
            jnp.einsum(
                "ibf,fd->ibd", act_low, down_weight[layer_index], preferred_element_type=jnp.float32
            )
            + down_bias[layer_index]
        )
        second_out, second_norm, second_inverse = norm_forward(
            first_out + ffn_out, ffn_gain[layer_index], ffn_shift[layer_index]
        )
        squares.append(
            jnp.stack(
                [
                    jnp.sum(valid_cells * stream * stream),
                    jnp.sum(valid_cells * branch * branch),
                    jnp.sum(valid_cells * ffn_out * ffn_out),
                ]
            )
        )
        gathered = (all_keys, all_values)
        stored.append(
            (
                in_low,
                queries,
                key_rows,
                value_rows,
                gathered,
                log_total,
                attended,
                first_norm,
                first_inverse,
                mid_low,
                hidden,
                act_low,
                second_norm,
                second_inverse,
            )
        )
        stream = second_out
    activations = stream * valid_cells
    upstream = cotangent.astype(jnp.float32) * valid_cells
    layer_grads = [None] * LAYERS
    for layer_index in reversed(range(LAYERS)):
        (
            in_low,
            queries,
            key_rows,
            value_rows,
            gathered,
            log_total,
            attended,
            first_norm,
            first_inverse,
            mid_low,
            hidden,
            act_low,
            second_norm,
            second_inverse,
        ) = stored[layer_index]
        ffn_gain_grad = jnp.sum(upstream * second_norm, axis=(0, 1))
        ffn_shift_grad = jnp.sum(upstream, axis=(0, 1))
        second_grad = norm_backward(upstream, second_norm, second_inverse, ffn_gain[layer_index])
        ffn_low = second_grad.astype(jnp.bfloat16)
        down_weight_grad = jnp.einsum(
            "ibf,ibd->fd", act_low, ffn_low, preferred_element_type=jnp.float32
        )
        act_grad = jnp.einsum(
            "ibd,fd->ibf", ffn_low, down_weight[layer_index], preferred_element_type=jnp.float32
        )
        hidden_low = jax.vjp(gelu_exact, hidden)[1](act_grad)[0].astype(jnp.bfloat16)
        up_weight_grad = jnp.einsum(
            "ibd,ibf->df", mid_low, hidden_low, preferred_element_type=jnp.float32
        )
        first_grad = second_grad + jnp.einsum(
            "ibf,df->ibd", hidden_low, up_weight[layer_index], preferred_element_type=jnp.float32
        )
        attn_gain_grad = jnp.sum(first_grad * first_norm, axis=(0, 1))
        attn_shift_grad = jnp.sum(first_grad, axis=(0, 1))
        residual_grad = norm_backward(first_grad, first_norm, first_inverse, attn_gain[layer_index])
        branch_low = residual_grad.astype(jnp.bfloat16)
        out_weight_grad = jnp.einsum(
            "ibd,ibe->de", attended, branch_low, preferred_element_type=jnp.float32
        )
        attended_low = jnp.einsum(
            "ibe,de->ibd", branch_low, out_weight[layer_index], preferred_element_type=jnp.float32
        ).astype(jnp.bfloat16)
        all_keys, all_values = gathered
        scores = table_scores(queries, all_keys, usable)
        attn_probs = jnp.exp(scores - log_total[..., None])
        probs_low = attn_probs.astype(jnp.bfloat16)
        probs_grad = jnp.einsum(
            "ibhe,jbhe->bhij",
            split_heads(attended_low),
            split_heads(all_values),
            preferred_element_type=jnp.float32,
        )
        center = jnp.sum(attn_probs * probs_grad, axis=-1)
        scores_low = (attn_probs * (probs_grad - center[..., None])).astype(jnp.bfloat16)
        query_low = merge_heads(
            jnp.einsum(
                "bhij,jbhe->ibhe",
                scores_low,
                split_heads(all_keys),
                preferred_element_type=jnp.float32,
            )
        ).astype(jnp.bfloat16)
        key_part = jnp.einsum(
            "bhij,ibhe->jbhe", scores_low, split_heads(queries), preferred_element_type=jnp.float32
        )
        value_part = jnp.einsum(
            "bhij,ibhe->jbhe",
            probs_low,
            split_heads(attended_low),
            preferred_element_type=jnp.float32,
        )
        key_sums = lax.psum_scatter(
            jnp.concatenate([merge_heads(key_part), merge_heads(value_part)], axis=-1).astype(
                jnp.bfloat16
            ),
            "rows",
            scatter_dimension=0,
            tiled=True,
        )
        proj_low = jnp.concatenate([query_low, key_sums], axis=-1)
        in_weight_grad = (
            jnp.einsum("ibd,ibe->de", in_low, proj_low, preferred_element_type=jnp.float32)
            * column_scale
        )
        query_bias_grad = row_sums(query_low) * score_scale
        value_bias_grad = row_sums(proj_low[:, :, 2 * D :])
        weight_now = in_weight[layer_index]
        query_input = (
            jnp.einsum(
                "ibe,de->ibd", query_low, weight_now[:, :D], preferred_element_type=jnp.float32
            )
            * score_scale
        )
        other_input = jnp.einsum(
            "ibe,de->ibd", proj_low[:, :, D:], weight_now[:, D:], preferred_element_type=jnp.float32
        )
        upstream = residual_grad + query_input + other_input
        layer_grads[layer_index] = (
            in_weight_grad,
            query_bias_grad,
            value_bias_grad,
            out_weight_grad,
            row_sums(branch_low),
            attn_gain_grad,
            attn_shift_grad,
            up_weight_grad,
            row_sums(hidden_low),
            down_weight_grad,
            row_sums(ffn_low),
            ffn_gain_grad,
            ffn_shift_grad,
        )
    stacked = [
        jnp.stack([layer_grads[layer_index][member] for layer_index in range(LAYERS)])
        for member in range(13)
    ]
    totals = lax.psum(
        (
            stacked[0],
            stacked[1],
            stacked[2],
            stacked[3],
            stacked[4],
            stacked[5],
            stacked[6],
            stacked[7],
            stacked[8],
            stacked[9],
            stacked[10],
            stacked[11],
            stacked[12],
            jnp.stack(squares),
            jnp.sum(valid_rows),
        ),
        ("tables", "rows"),
    )
    root_means = jnp.sqrt(totals[13] / (totals[14] * D))
    return (
        activations,
        upstream,
        totals[0],
        totals[1],
        totals[2],
        totals[3],
        totals[4],
        totals[5],
        totals[6],
        totals[7],
        totals[8],
        totals[9],
        totals[10],
        totals[11],
        totals[12],
        root_means,
    )


MESH = pl.DeviceIdType.MESH
NT = (((1,), (1,)), ((), ()))
NN = (((1,), (0,)), ((), ()))
TN = (((0,), (0,)), ((), ()))
TILE = 512
VECTORS = 9
GROUPS = (4, 2)
HALVES = 2
PATHS = {
    "A": ("cxyz", "cyxz"),
    "B": ("cxynf", "cyxnf"),
    "N": ("cnyxf", "cnyxf"),
    "D": ("cdz", "cdz"),
}
KINDS = "ABNANBBAANDAD"
SCHEDULE = (
    (),
    (),
    (0,),
    (),
    (),
    (),
    (1, 2),
    (0,),
    (3,),
    (),
    (1,),
    (0, 2, 3, 4, 5, 1),
    (),
    (),
    (),
    (),
    (),
    (),
    (2, 3, 0, 1, 6, 7, 8),
    (5,),
    (),
    (2,),
    (4, 9),
    (),
    (1,),
    (),
    (
        10, 12, 3, 8, 11, 1, 6, 9, 0, 2, 5, 4, 12, 2, 8, 7, 5, 9, 12, 11, 1, 10, 8, 3, 6, 4, 2, 9,
        0, 5, 12, 10, 8, 11, 1, 7, 9, 4, 6, 5, 10, 2, 3, 9, 11, 4, 6, 7, 5, 9, 12, 13, 8, 11, 6, 3,
        4, 9, 5, 2, 7, 10, 1, 12, 11, 0, 6, 8, 4, 9, 7, 3, 2, 11, 10, 6, 5, 4, 11, 8, 7, 0, 1, 5, 6,
        7, 9, 4, 6,
    ),
)


def dot(left, right, dims=NN):
    return lax.dot_general(left, right, dims, preferred_element_type=jnp.float32)


def column_sum(values):
    return jnp.sum(values, axis=0, keepdims=True)


def row_mean(values):
    return jnp.mean(values, axis=-1, keepdims=True)


def send(source, target, sems, stage, device):
    return pltpu.make_async_remote_copy(
        src_ref=source,
        dst_ref=target,
        send_sem=sems.at[0],
        recv_sem=sems.at[1 + stage],
        device_id=device,
        device_id_type=MESH,
    )


def reduce_job(part, total, recv, sems, stages):
    rows, used = part.shape[0], 0
    base, height = 0, rows
    spread, gather, inbox, held = [], [], [], []
    last = len(stages) - 1
    for n, (own, peers) in enumerate(stages):
        height = height // (len(peers) + 1)

        def piece(index):
            return pl.ds(pl.multiple_of(base + index * height, height), height)

        mine = piece(own)
        inbox.append(recv.at[pl.ds(used, len(peers) * height)])
        spread.append(
            [
                send(part.at[piece(index)], recv.at[pl.ds(used + m * height, height)], sems, n, device)
                for m, (device, index) in enumerate(peers)
            ]
        )
        source = part if n == last else total
        gather.append(
            [send(source.at[mine], total.at[mine], sems, 5 + n, device) for device, _ in peers]
        )
        held.append((base + own * height, height, used, len(peers)))
        used += len(peers) * height
        base = base + own * height
    kept = pltpu.make_async_copy(part.at[mine], total.at[mine], sems.at[11])

    def wait_all(stage, n):
        send(inbox[n], inbox[n], sems, stage, stages[n][1][0][0]).wait()

    def start_all(copies):
        for copy in copies:
            copy.start()

    def add(n):
        start, size, offset, count = held[n]
        step = 128 if size % 128 == 0 else size

        def chunk(i, carry):
            at = pl.ds(pl.multiple_of(start + i * step, step), step)
            sums = part[at, :].astype(jnp.float32)
            for m in range(count):
                other = pl.ds(pl.multiple_of(offset + m * size + i * step, 16), step)
                sums = sums + recv[other, :].astype(jnp.float32)
            part[at, :] = sums.astype(part.dtype)
            return carry

        lax.fori_loop(0, size // step, chunk, 0)

    def first():
        start_all(spread[0])

    def fold(n):
        def run():
            wait_all(n, n)
            add(n)
            if n < last:
                start_all(spread[n + 1])
            else:
                kept.start()
                start_all(gather[n])

        return run

    def unfold(n):
        def run():
            wait_all(5 + n, n)
            if n == last:
                kept.wait()
            if n > 0:
                start_all(gather[n - 1])

        return run

    return [first] + [fold(n) for n in range(last + 1)] + [unfold(n) for n in range(last, -1, -1)]


def small_job(part, total, recv, sems, stages):
    base, width = 0, part.shape[1]
    spread, gather, held = [], [], []
    last = len(stages) - 1
    for n, (own, peers) in enumerate(stages):
        if n < last:
            width = width // (len(peers) + 1)

        def piece(index):
            return pl.ds(pl.multiple_of(base + index * width, width), width)

        mine = piece(own) if n < last else piece(0)
        spread.append(
            [
                send(part.at[:, piece(index) if n < last else mine], recv[n].at[m], sems, n, device)
                for m, (device, index) in enumerate(peers)
            ]
        )
        gather.append(
            [send(total.at[:, mine], total.at[:, mine], sems, 5 + n, device) for device, _ in peers]
        )
        held.append(mine)
        if n < last:
            base = base + own * width

    def wait_all(stage, n):
        send(recv[n], recv[n], sems, stage, stages[n][1][0][0]).wait()

    def start_all(copies):
        for copy in copies:
            copy.start()

    def first():
        start_all(spread[0])

    def fold(n):
        def run():
            wait_all(n, n)
            own = part[:, held[n]]
            if n < last:
                for m in range(len(stages[n][1])):
                    own = own + recv[n][m]
                part[:, held[n]] = own
                start_all(spread[n + 1])
            else:
                total[:, held[n]] = (own + recv[n][0]) + (recv[n][1] + recv[n][2])
                start_all(gather[n - 1])

        return run

    def unfold(n):
        def run():
            wait_all(5 + n, n)
            if n > 0:
                start_all(gather[n - 1])

        return run

    return [first] + [fold(n) for n in range(last + 1)] + [unfold(n) for n in range(last - 1, -1, -1)]


def table_kernel(
    local,
    block_tables,
    seq,
    x_hbm,
    cot_hbm,
    lengths_ref,
    counts_ref,
    w_in_hbm,
    w_out_hbm,
    w_up_hbm,
    w_down_hbm,
    *refs,
):
    vector_refs, refs = refs[:VECTORS], refs[VECTORS:]
    (
        act_hbm,
        xgrad_hbm,
        t_in_first,
        t_in_last,
        t_mid,
        t_down,
        t_small,
        w_in,
        w_out,
        w_up,
        w_down,
        vectors,
        g_in_first,
        g_in_last,
        g_mid,
        g_down,
        small,
        in_low,
        cot_low,
        stream,
        queries,
        kv,
        attended,
        log_totals,
        norm1,
        inverse1,
        mid_low,
        slope,
        act_low,
        norm2,
        inverse2,
        meta,
        bias_col,
        valid,
        ffn_low,
        attended_low,
        centers,
        dkv_send,
        dkv_recv_first,
        dkv_recv_last,
        proj_low,
        staged,
        recv_in_first,
        recv_in_last,
        recv_mid,
        recv_down,
        recv_small,
        x_send,
        x_recv,
        cot_send,
        cot_recv,
        act_send,
        act_recv,
        xg_send,
        xg_recv,
        local_sem,
        kv_sem,
        dkv_sem,
        meta_sem,
        job_sem,
    ) = refs
    upstream = stream
    t_in, g_in, recv_in = (t_in_first, t_in_last), (g_in_first, g_in_last), (recv_in_first, recv_in_last)
    branch_low = ffn_low
    dkv_recvs = (dkv_recv_first, dkv_recv_last)
    rows = block_tables * local
    dim = in_low.shape[-1]
    head_dim = dim // HEADS
    scale = head_dim**-0.5
    tiles = rows // TILE
    t = lax.axis_index("tables")
    r = lax.axis_index("rows")
    core = lax.rem(t, 2)
    side = r // block_tables
    slot = lax.rem(r, block_tables)
    peer = (t + 1 - 2 * core, r)
    own_rows = pl.multiple_of(core * rows, rows)
    peer_rows = pl.multiple_of((1 - core) * rows, rows)

    x_side, y_side, z_side = lax.rem(r, 2), t // 2, r // 2
    x_next = (t, r + 1 - 2 * x_side)
    y_next = (t + 2 - 4 * y_side, r)
    z_next = [
        (z_side + 1 - 2 * lax.rem(z_side, 2)),
        lax.rem(z_side + 2, 4),
        3 - z_side,
    ]
    z_peers = [((t, 2 * z + x_side), z) for z in z_next]

    def choose(first, second):
        return core * second + (1 - core) * first

    y_index = t + 2 - 4 * y_side
    corner = x_side + 2 * y_side
    corners = [
        (x_next, 1 - x_side + 2 * y_side),
        (y_next, x_side + 2 - 2 * y_side),
        ((y_index, x_next[1]), 3 - corner),
    ]
    sides = {
        "c": (core, [(peer, 1 - core)]),
        "x": (x_side, [(x_next, 1 - x_side)]),
        "y": (y_side, [(y_next, 1 - y_side)]),
        "n": (lax.rem(z_side, 2), [(z_peers[0][0], 1 - lax.rem(z_side, 2))]),
        "f": (z_side // 2, [(z_peers[1][0], 1 - z_side // 2)]),
        "d": (corner, corners),
        "z": (z_side, z_peers),
    }

    def both(first, second):
        if first == second:
            return sides[first]
        (one_own, [(one, one_index)]), (two_own, [(two, two_index)]) = sides[first], sides[second]
        device = (choose(one[0], two[0]), choose(one[1], two[1]))
        return choose(one_own, two_own), [(device, choose(one_index, two_index))]

    def path(kind):
        first, second = PATHS[kind]
        return [both(*pair) for pair in zip(first, second)]

    def partner(k):
        return (t - core + side, block_tables * core + k)

    def is_self(k):
        return jnp.logical_and(core == side, slot == k)

    barrier = pltpu.get_barrier_semaphore()
    greeted = [peer, x_next, y_next] + [device for device, _ in z_peers]
    for device in greeted:
        pl.semaphore_signal(barrier, inc=1, device_id=device, device_id_type=MESH)
    for k in range(block_tables):

        @pl.when(jnp.logical_not(is_self(k)))
        def _():
            pl.semaphore_signal(barrier, inc=1, device_id=partner(k), device_id_type=MESH)

    pl.semaphore_wait(
        barrier, len(greeted) + jnp.where(core == side, block_tables - 1, block_tables)
    )

    def spread(source, target, send_sem, recv_sem, own_sem):
        def remote(k, at):
            return pltpu.make_async_remote_copy(
                src_ref=source(k),
                dst_ref=target(at),
                send_sem=send_sem.at[k],
                recv_sem=recv_sem.at[at],
                device_id=partner(k),
                device_id_type=MESH,
            )

        def kept(k):
            return pltpu.make_async_copy(source(k), target(k), own_sem)

        def start(blocks=range(block_tables)):
            for k in blocks:

                @pl.when(is_self(k))
                def _():
                    kept(k).start()

                @pl.when(jnp.logical_not(is_self(k)))
                def _():
                    remote(k, slot).start()

        def arrive():
            for k in range(block_tables):

                @pl.when(is_self(k))
                def _():
                    kept(k).wait()

                @pl.when(jnp.logical_not(is_self(k)))
                def _():
                    remote(k, k).wait_recv()

        def left():
            for k in range(block_tables):

                @pl.when(jnp.logical_not(is_self(k)))
                def _():
                    remote(k, slot).wait_send()

        return start, arrive, left

    def by_table(ref):
        return lambda k: ref.at[k]

    def by_rows(ref):
        return lambda k: ref.at[pl.ds(k * local, local)]

    x_start, x_arrive, x_left = spread(by_table(x_hbm), by_rows(in_low.at[0]), x_send, x_recv, local_sem.at[0])
    cot_start, cot_arrive, cot_left = spread(by_table(cot_hbm), by_rows(cot_low), cot_send, cot_recv, local_sem.at[1])
    act_start, act_arrive, act_left = spread(by_rows(staged.at[0]), by_table(act_hbm), act_send, act_recv, local_sem.at[2])
    xg_start, xg_arrive, xg_left = spread(by_rows(staged.at[1]), by_table(xgrad_hbm), xg_send, xg_recv, local_sem.at[3])

    def swap(source, target, sems):
        return pltpu.make_async_remote_copy(
            src_ref=source,
            dst_ref=target,
            send_sem=sems.at[0],
            recv_sem=sems.at[1],
            device_id=peer,
            device_id_type=MESH,
        )

    x_start()
    loads = [
        pltpu.make_async_copy(source, target, local_sem.at[4 + n])
        for n, (source, target) in enumerate(
            ((w_in_hbm, w_in), (w_out_hbm, w_out), (w_up_hbm, w_up), (w_down_hbm, w_down))
        )
    ]
    for load in loads:
        load.start()
    for n, ref in enumerate(vector_refs):
        for layer in range(LAYERS):
            vectors[pl.ds(layer * VECTORS + n, 1), pl.ds(0, ref.shape[1])] = ref[...].astype(
                jnp.float32
            )[layer : layer + 1, :]
    for k in range(block_tables):
        meta[core, pl.ds(k, 1), :] = jnp.full((1, 128), lengths_ref[k], jnp.int32)
        meta[core, pl.ds(block_tables + k, 1), :] = jnp.full((1, 128), counts_ref[k], jnp.int32)
    meta_copy = swap(meta.at[core], meta.at[core], meta_sem)
    meta_copy.start()
    small[...] = jnp.zeros_like(small)
    meta_copy.wait()
    length = meta[side, pl.ds(slot, 1), :][:, :1]
    train = meta[side, pl.ds(slot + block_tables, 1), :][:, :1]
    bias_col[...] = jnp.where(lax.broadcasted_iota(jnp.int32, (seq, 1), 0) < train, 0.0, MASKED)
    valid[...] = jnp.where(
        lax.broadcasted_iota(jnp.int32, (rows, 1), 0) + core * rows < length, 1.0, 0.0
    )
    small[pl.ds(13, 1), pl.ds(0, 128)] = jnp.broadcast_to(column_sum(valid[...]), (1, 128))
    x_arrive()
    cot_start()
    loads[0].wait()

    def vector(index, layer, width):
        return vectors[pl.ds(layer * VECTORS + index, 1), pl.ds(0, width)]

    def add_small(layer, index, values):
        at = (pl.ds(layer * 16 + index, 1), pl.ds(0, values.shape[-1]))
        small[at] = small[at] + values

    def each_tile(body, after=()):
        def step(i, carry):
            body(pl.ds(pl.multiple_of(i * TILE, TILE), TILE))
            for n, run in enumerate(after):

                @pl.when(i == n)
                def _():
                    run()

            return carry

        lax.fori_loop(0, tiles, step, 0)

    def head_cols(h):
        return pl.ds(pl.multiple_of(h * head_dim, head_dim), head_dim)

    def forward(layer):
        def project(at):
            projected = dot(in_low[layer, at, :], w_in[layer])
            queries[layer, at, :] = (
                (projected[:, :dim] + vector(0, layer, dim)) * scale
            ).astype(jnp.bfloat16)
            own = pl.ds(pl.multiple_of(own_rows + at.start, TILE), TILE)
            key_rows = projected[:, dim : 2 * dim].astype(jnp.bfloat16)
            value_rows = (projected[:, 2 * dim :] + vector(1, layer, dim)).astype(jnp.bfloat16)
            for h in range(HEADS):
                cols = slice(h * head_dim, (h + 1) * head_dim)
                kv[layer, h, own, pl.ds(0, head_dim)] = key_rows[:, cols]
                kv[layer, h, own, pl.ds(head_dim, head_dim)] = value_rows[:, cols]

        each_tile(project)

        def kv_copy(h):
            mine = kv.at[layer, h, pl.ds(own_rows, rows)]
            return swap(mine, mine, kv_sem.at[layer, h])

        for h in range(HEADS):
            kv_copy(h).start()

        def attend(h, carry):
            cols = head_cols(h)
            kv_copy(h).wait()
            scores = dot(kv[layer, h, :, pl.ds(0, head_dim)], queries[layer, :, cols], NT)
            scores = scores + bias_col[...]
            row_max = jnp.max(scores, axis=0, keepdims=True)
            exponent = jnp.exp(scores - row_max)
            total = jnp.sum(exponent, axis=0, keepdims=True)
            mixed = dot(kv[layer, h, :, pl.ds(head_dim, head_dim)], exponent.astype(jnp.bfloat16), TN)
            attended[layer, :, cols] = jnp.transpose(mixed * (1.0 / total)).astype(jnp.bfloat16)
            log_totals[layer, pl.ds(h, 1), :] = row_max + jnp.log(total)
            return carry

        lax.fori_loop(0, HEADS, attend, 0)
        if layer == 0:
            for load in loads[1:]:
                load.wait()

        def dense(at):
            below = in_low[0, at, :].astype(jnp.float32) if layer == 0 else stream[at, :]
            branch = dot(attended[layer, at, :], w_out[layer]) + vector(2, layer, dim)
            valid_cells = valid[at, :]
            add_small(layer, 10, column_sum(below * below * valid_cells))
            add_small(layer, 11, column_sum(branch * branch * valid_cells))
            summed = below + branch
            centered = summed - row_mean(summed)
            inverse = lax.rsqrt(row_mean(centered * centered) + EPSILON)
            normed = centered * inverse
            norm1[layer, at, :] = normed
            inverse1[layer, at, :] = inverse
            first_out = normed * vector(3, layer, dim) + vector(4, layer, dim)
            mid = first_out.astype(jnp.bfloat16)
            mid_low[layer, at, :] = mid
            hidden = dot(mid, w_up[layer]) + vector(5, layer, 2 * dim)
            cdf = 0.5 + 0.5 * lax.erf(hidden * (0.5**0.5))
            slope[layer, at, :] = cdf + hidden * (
                jnp.exp(hidden * hidden * -0.5) * 0.3989422804014327
            )
            act = (hidden * cdf).astype(jnp.bfloat16)
            act_low[layer, at, :] = act
            ffn_out = dot(act, w_down[layer]) + vector(6, layer, dim)
            add_small(layer, 12, column_sum(ffn_out * ffn_out * valid_cells))
            summed = first_out + ffn_out
            centered = summed - row_mean(summed)
            inverse = lax.rsqrt(row_mean(centered * centered) + EPSILON)
            normed = centered * inverse
            norm2[layer, at, :] = normed
            inverse2[layer, at, :] = inverse
            out = normed * vector(7, layer, dim) + vector(8, layer, dim)
            if layer + 1 < LAYERS:
                stream[at, :] = out
                in_low[layer + 1, at, :] = out.astype(jnp.bfloat16)
            else:
                staged[0, at, :] = (out * valid_cells).astype(jnp.bfloat16)

        each_tile(dense)

    for layer in range(LAYERS):
        forward(layer)
    act_start()
    cot_arrive()

    jobs = []

    points = list(SCHEDULE)

    def begin(steps):
        jobs.append(list(steps))
        jobs[-1].pop(0)()

    def tick():
        for index in points.pop(0):
            if index < len(jobs) and jobs[index]:
                jobs[index].pop(0)()

    def reduce(part, total, recv):
        begin(reduce_job(part, total, recv, job_sem.at[len(jobs)], path(KINDS[len(jobs)])))

    def reduce_halves(part, total, recv):
        width = part.shape[1] // HALVES
        for n in range(HALVES):
            cols = pl.ds(n * width, width)
            reduce(
                part.at[:, cols],
                total.at[:, cols],
                recv.at[:, cols],
            )

    def backward(layer):
        groups = GROUPS[layer]
        group_heads = HEADS // groups
        group_width = group_heads * head_dim
        dkv_recv = dkv_recvs[layer]
        dq_t = slope.at[layer, :, pl.ds(0, dim)]

        def send_cols(group):
            return pl.ds(group * 2 * group_width, 2 * group_width)


        def enter(at):
            if layer == LAYERS - 1:
                up = cot_low[at, :].astype(jnp.float32) * valid[at, :]
            else:
                up = upstream[at, :]
            normed = norm2[layer, at, :]
            add_small(layer, 8, column_sum(up * normed))
            add_small(layer, 9, column_sum(up))
            scaled = up * vector(7, layer, dim)
            second = inverse2[layer, at, :] * (
                scaled - row_mean(scaled) - normed * row_mean(scaled * normed)
            )
            upstream[at, :] = second
            ffn = second.astype(jnp.bfloat16)
            ffn_low[at, :] = ffn
            add_small(layer, 7, column_sum(ffn.astype(jnp.float32)))

        each_tile(enter)
        g_down[layer] = dot(act_low[layer], ffn_low[...], TN).astype(jnp.bfloat16)
        tick()
        reduce(g_down.at[layer], t_down.at[layer], recv_down.at[layer])

        def dense(at):
            hidden = (dot(ffn_low[at, :], w_down[layer], NT) * slope[layer, at, :]).astype(
                jnp.bfloat16
            )
            proj_low[at, pl.ds(0, hidden.shape[1])] = hidden
            add_small(layer, 6, column_sum(hidden.astype(jnp.float32)))
            first = upstream[at, :] + dot(hidden, w_up[layer], NT)
            normed = norm1[layer, at, :]
            add_small(layer, 4, column_sum(first * normed))
            add_small(layer, 5, column_sum(first))
            scaled = first * vector(3, layer, dim)
            residual = inverse1[layer, at, :] * (
                scaled - row_mean(scaled) - normed * row_mean(scaled * normed)
            )
            upstream[at, :] = residual
            branch = residual.astype(jnp.bfloat16)
            branch_low[at, :] = branch
            add_small(layer, 3, column_sum(branch.astype(jnp.float32)))
            low = dot(branch, w_out[layer], NT).astype(jnp.bfloat16)
            attended_low[at, :] = low
            product = low.astype(jnp.float32) * attended[layer, at, :].astype(jnp.float32)
            lane = lax.broadcasted_iota(jnp.int32, (TILE, head_dim), 1)
            held = jnp.zeros((TILE, head_dim), jnp.float32)
            for h in range(HEADS):
                center = jnp.sum(product[:, h * head_dim : (h + 1) * head_dim], axis=-1, keepdims=True)
                held = jnp.where(lane == h, center, held)
            centers[:, at] = jnp.transpose(held)[:8, :]

        each_tile(dense, (tick,) * tiles)
        up_grad = dot(mid_low[layer], proj_low[:, pl.ds(0, 2 * dim)], TN).astype(jnp.bfloat16)
        g_mid[layer, pl.ds(0, dim), :] = up_grad[:, :dim]
        g_mid[layer, pl.ds(dim, dim), :] = up_grad[:, dim:]
        g_mid[layer, pl.ds(2 * dim, dim), :] = dot(attended[layer], branch_low[...], TN).astype(
            jnp.bfloat16
        )
        tick()
        reduce_halves(g_mid.at[layer], t_mid.at[layer], recv_mid.at[layer])

        def attend(group, base, first, keep):
            def step(i, carry):
                h = group * group_heads + i // tiles
                j = pl.multiple_of(lax.rem(i, tiles) * TILE, TILE)
                at = pl.ds(pl.multiple_of(base + j, TILE), TILE)
                cols = head_cols(h)
                key_rows = kv[layer, h, at, pl.ds(0, head_dim)]
                query_rows = queries[layer, :, cols]
                grads = attended_low[:, cols]
                probs = jnp.exp(
                    dot(key_rows, query_rows, NT) + bias_col[at, :] - log_totals[layer, pl.ds(h, 1), :]
                )
                value_part = dot(probs.astype(jnp.bfloat16), grads)
                probs_grad = dot(kv[layer, h, at, pl.ds(head_dim, head_dim)], grads, NT)
                scores_low = (probs * (probs_grad - centers[pl.ds(h, 1), :])).astype(
                    jnp.bfloat16
                )
                key_part = dot(scores_low, query_rows)
                query_part = dot(key_rows, scores_low, TN)
                if first:
                    query_part = jnp.where(j == 0, query_part, query_part + dq_t[cols, :])
                else:
                    query_part = query_part + dq_t[cols, :]
                dq_t[cols, :] = query_part
                inside = i // tiles * head_dim
                keep(pl.ds(j, TILE), pl.ds(pl.multiple_of(inside, head_dim), head_dim), key_part)
                keep(
                    pl.ds(j, TILE),
                    pl.ds(pl.multiple_of(group_width + inside, head_dim), head_dim),
                    value_part,
                )
                return carry

            lax.fori_loop(0, group_heads * tiles, step, 0)

        def dkv_copy(group):
            return swap(
                dkv_send.at[:, send_cols(group)], dkv_recv.at[group], dkv_sem.at[layer, group]
            )

        def attend_peer(group):
            def keep(at, cols, part):
                start = group * 2 * group_width + cols.start
                dkv_send[at, pl.ds(pl.multiple_of(start, head_dim), cols.size)] = part.astype(
                    jnp.bfloat16
                )

            attend(group, peer_rows, True, keep)
            dkv_copy(group).start()
            tick()

        def attend_own(group):
            def keep(at, cols, part):
                start = pl.multiple_of(dim + cols.start, head_dim)
                slope[layer, at, pl.ds(start, cols.size)] = part

            attend(group, own_rows, False, keep)
            tick()

        def finish_group(group):
            dkv_copy(group).wait()

            def finish(at):
                group_rows = pl.ds(group * group_width, group_width)
                query = jnp.transpose(dq_t[group_rows, at]).astype(jnp.bfloat16)
                pair = (
                    slope[layer, at, pl.ds(dim, 2 * group_width)] + dkv_recv[group, at, :].astype(jnp.float32)
                ).astype(jnp.bfloat16)
                for n, part in enumerate((query, pair[:, :group_width], pair[:, group_width:])):
                    proj_low[at, pl.ds(n * dim + group * group_width, group_width)] = part
                cols = pl.ds(group * group_width, group_width)
                small[pl.ds(layer * 16, 1), cols] += column_sum(query.astype(jnp.float32)) * scale
                small[pl.ds(layer * 16 + 1, 1), cols] += column_sum(
                    pair[:, group_width:].astype(jnp.float32)
                )

            each_tile(finish)
            parts = [
                proj_low[:, pl.ds(n * dim + group * group_width, group_width)] for n in range(3)
            ]
            grad = dot(in_low[layer], jnp.concatenate(parts, axis=1), TN)
            g_in[layer][group, :, pl.ds(0, group_width)] = (grad[:, :group_width] * scale).astype(
                jnp.bfloat16
            )
            g_in[layer][group, :, pl.ds(group_width, 2 * group_width)] = grad[
                :, group_width:
            ].astype(jnp.bfloat16)
            tick()
            reduce(
                g_in[layer].at[group],
                t_in[layer].at[group],
                recv_in[layer].at[group],
            )

        for group in range(groups):
            attend_peer(group)
            if group > 0:
                finish_group(group - 1)
            attend_own(group)
        finish_group(groups - 1)
        if layer == 0:
            begin(small_job(small, t_small, recv_small, job_sem.at[len(jobs)], path("D")))

        def pass_down(at):
            grad = (
                upstream[at, :]
                + dot(proj_low[at, pl.ds(0, dim)], w_in[layer, :, pl.ds(0, dim)], NT) * scale
                + dot(proj_low[at, pl.ds(dim, 2 * dim)], w_in[layer, :, pl.ds(dim, 2 * dim)], NT)
            )
            if layer > 0:
                upstream[at, :] = grad
            else:
                staged[1, at, :] = grad.astype(jnp.bfloat16)

        each_tile(pass_down)
        if layer == 0:
            xg_start(range(block_tables // 2))
            jobs.append([lambda: xg_start(range(block_tables // 2, block_tables))])
        tick()

    for layer in reversed(range(LAYERS)):
        backward(layer)
    tick()
    while any(jobs):
        for steps in jobs:
            if steps:
                steps.pop(0)()
    act_arrive()
    xg_arrive()
    x_left()
    cot_left()
    act_left()
    xg_left()


def widen_kernel(f_first, f_last, f_mid, f_down, f_act, f_xgrad, small, *refs):
    act, xgrad, in_weight, out_weight, up_weight, down_weight, root_means = refs[:7]
    low_act, low_xgrad, low_first, low_last, low_mid, low_down = refs[16:22]
    wide_act, wide_xgrad, wide_in, wide_out, wide_up, wide_down = refs[22:28]
    read_sem, write_sem = refs[28:]
    dim = f_act.shape[2]
    half = dim // 2

    def widened(values):
        return values.astype(jnp.float32)

    def table_part(source, low, wide, target):
        def convert():
            for k in range(source.shape[0]):
                wide[:, k, :] = widened(low[k])

        return (source, low), convert, [(wide, target)]

    def down_part(layer):
        def convert():
            wide_down[layer] = widened(low_down[layer])

        return (
            (f_down.at[layer], low_down.at[layer]),
            convert,
            [(wide_down.at[layer], down_weight.at[layer])],
        )

    def mid_part(layer):
        def convert():
            for n in range(2):
                wide_up[layer, :, pl.ds(n * dim, dim)] = widened(low_mid[layer, pl.ds(n * dim, dim), :])
            wide_out[layer] = widened(low_mid[layer, pl.ds(2 * dim, dim), :])

        return (
            (f_mid.at[layer], low_mid.at[layer]),
            convert,
            [
                (wide_up.at[layer], up_weight.at[layer]),
                (wide_out.at[layer], out_weight.at[layer]),
            ],
        )

    def in_part(layer, source, low, start):
        at = pl.ds(start, half)
        groups, width = source.shape[0], source.shape[2] // 3

        def convert():
            for group in range(groups):
                for n in range(3):
                    wide_in[layer, at, pl.ds((n * groups + group) * width, width)] = widened(
                        low[group, at, pl.ds(n * width, width)]
                    )

        return (
            (source.at[:, at], low.at[:, at]),
            convert,
            [(wide_in.at[layer, at], in_weight.at[layer, at])],
        )

    parts = [
        table_part(f_act, low_act, wide_act, act),
        table_part(f_xgrad, low_xgrad, wide_xgrad, xgrad),
    ]
    for layer, (source, low) in enumerate(((f_first, low_first), (f_last, low_last))):
        parts += [in_part(layer, source, low, 0), in_part(layer, source, low, half)]
        parts += [mid_part(layer), down_part(layer)]
    reads = [
        pltpu.make_async_copy(*part[0], read_sem.at[n]) for n, part in enumerate(parts)
    ]
    writes = []
    for copy in reads:
        copy.start()
    for copy, (_, convert, results) in zip(reads, parts):
        copy.wait()
        convert()
        for source, target in results:
            writes.append(pltpu.make_async_copy(source, target, write_sem.at[len(writes)]))
            writes[-1].start()
    for ref, row in zip(refs[7:16], (0, 1, 3, 4, 5, 6, 7, 8, 9)):
        for layer in range(LAYERS):
            ref[pl.ds(layer, 1), :] = small[pl.ds(layer * 16 + row, 1), pl.ds(0, ref.shape[1])]
    count = small[pl.ds(13, 1), pl.ds(0, 1)]
    for layer in range(LAYERS):
        sums = jnp.sum(small[pl.ds(layer * 16 + 8, 8), pl.ds(0, dim)], axis=-1, keepdims=True)
        for n in range(3):
            root_means[pl.ds(layer, 1), pl.ds(n, 1)] = jnp.sqrt(
                sums[2 + n : 3 + n, :] / (count * dim)
            )
    for write in writes:
        write.wait()


def table_device(tables, row_parts, *operands):
    (
        tables_in,
        in_weight,
        query_bias,
        value_bias,
        out_weight,
        out_bias,
        attn_gain,
        attn_shift,
        up_weight,
        up_bias,
        down_weight,
        down_bias,
        ffn_gain,
        ffn_shift,
        cotangent,
        lengths,
        train_counts,
    ) = operands
    local, block_tables, dim = tables_in.shape
    rows = local * block_tables
    seq = local * row_parts
    hidden = up_weight.shape[-1]
    head_dim = dim // HEADS
    f32, bf16 = jnp.float32, jnp.bfloat16
    vmem = pl.BlockSpec(memory_space=pltpu.VMEM)
    hbm = pl.BlockSpec(memory_space=pl.ANY)
    smem = pl.BlockSpec(memory_space=pltpu.SMEM)
    block = (block_tables, local, dim)
    dma = pltpu.SemaphoreType.DMA
    in_parts = [(groups, dim, 3 * dim // groups) for groups in GROUPS]
    mid = (LAYERS, 3 * dim, dim)
    shards = 8 * row_parts // 2

    def received(shape):
        height = shape[-2]
        return pltpu.VMEM(shape[:-2] + (height - height // shards, shape[-1]), bf16)

    act, xgrad, *sums, small = pl.pallas_call(
        functools.partial(table_kernel, local, block_tables, seq),
        out_shape=(
            jax.ShapeDtypeStruct(block, bf16),
            jax.ShapeDtypeStruct(block, bf16),
            jax.ShapeDtypeStruct(in_parts[0], bf16),
            jax.ShapeDtypeStruct(in_parts[1], bf16),
            jax.ShapeDtypeStruct(mid, bf16),
            jax.ShapeDtypeStruct(down_weight.shape, bf16),
            jax.ShapeDtypeStruct((LAYERS * 16, hidden), f32),
        ),
        in_specs=[hbm, hbm, smem, smem] + [hbm] * 4 + [vmem] * VECTORS,
        out_specs=(hbm,) * 6 + (vmem,),
        scratch_shapes=[
            pltpu.VMEM(in_weight.shape, bf16),
            pltpu.VMEM(out_weight.shape, bf16),
            pltpu.VMEM(up_weight.shape, bf16),
            pltpu.VMEM(down_weight.shape, bf16),
            pltpu.VMEM((LAYERS * VECTORS, hidden), f32),
            pltpu.VMEM(in_parts[0], bf16),
            pltpu.VMEM(in_parts[1], bf16),
            pltpu.VMEM(mid, bf16),
            pltpu.VMEM(down_weight.shape, bf16),
            pltpu.VMEM((LAYERS * 16, hidden), f32),
            pltpu.VMEM((LAYERS, rows, dim), bf16),
            pltpu.VMEM((rows, dim), bf16),
            pltpu.VMEM((rows, dim), f32),
            pltpu.VMEM((LAYERS, rows, dim), bf16),
            pltpu.VMEM((LAYERS, HEADS, seq, 2 * head_dim), bf16),
            pltpu.VMEM((LAYERS, rows, dim), bf16),
            pltpu.VMEM((LAYERS, 8, rows), f32),
            pltpu.VMEM((LAYERS, rows, dim), f32),
            pltpu.VMEM((LAYERS, rows, 1), f32),
            pltpu.VMEM((LAYERS, rows, dim), bf16),
            pltpu.VMEM((LAYERS, rows, hidden), f32),
            pltpu.VMEM((LAYERS, rows, hidden), bf16),
            pltpu.VMEM((LAYERS, rows, dim), f32),
            pltpu.VMEM((LAYERS, rows, 1), f32),
            pltpu.VMEM((2, 2 * block_tables, 128), jnp.int32),
            pltpu.VMEM((seq, 1), f32),
            pltpu.VMEM((rows, 1), f32),
            pltpu.VMEM((rows, dim), bf16),
            pltpu.VMEM((rows, dim), bf16),
            pltpu.VMEM((8, rows), f32),
            pltpu.VMEM((rows, 2 * dim), bf16),
            *[pltpu.VMEM((groups, rows, 2 * dim // groups), bf16) for groups in GROUPS],
            pltpu.VMEM((rows, 3 * dim), bf16),
            pltpu.VMEM((2, rows, dim), bf16),
        ]
        + [received(shape) for shape in (in_parts[0], in_parts[1], mid, down_weight.shape)]
        + [
            [
                pltpu.VMEM((1, LAYERS * 16, hidden // 2), f32),
                pltpu.VMEM((3, LAYERS * 16, hidden // 8), f32),
                pltpu.VMEM((3, LAYERS * 16, hidden // 8), f32),
            ]
        ]
        + [dma((block_tables,))] * 8
        + [
            dma((8,)),
            dma((LAYERS, HEADS, 2)),
            dma((LAYERS, HEADS, 2)),
            dma((2,)),
            dma((LAYERS * (1 + HALVES) + sum(GROUPS) + 1, 12)),
        ],
        compiler_params=pltpu.CompilerParams(
            collective_id=0, has_side_effects=True, vmem_limit_bytes=63 * 1024 * 1024
        ),
    )(
        jnp.swapaxes(tables_in, 0, 1),
        jnp.swapaxes(cotangent, 0, 1),
        lengths,
        train_counts,
        in_weight,
        out_weight,
        up_weight,
        down_weight,
        query_bias,
        value_bias,
        out_bias,
        attn_gain,
        attn_shift,
        up_bias,
        down_bias,
        ffn_gain,
        ffn_shift,
    )
    vector = jax.ShapeDtypeStruct((LAYERS, dim), f32)
    wide_vector = jax.ShapeDtypeStruct((LAYERS, hidden), f32)
    shapes = [
        jax.ShapeDtypeStruct(tables_in.shape, f32),
        jax.ShapeDtypeStruct(tables_in.shape, f32),
        jax.ShapeDtypeStruct(in_weight.shape, f32),
        jax.ShapeDtypeStruct(out_weight.shape, f32),
        jax.ShapeDtypeStruct(up_weight.shape, f32),
        jax.ShapeDtypeStruct(down_weight.shape, f32),
        jax.ShapeDtypeStruct((LAYERS, 3), f32),
    ] + [vector] * 5 + [wide_vector] + [vector] * 3
    outs = pl.pallas_call(
        widen_kernel,
        out_shape=shapes,
        in_specs=[hbm] * 6 + [vmem],
        out_specs=[hbm] * 6 + [vmem] * 10,
        scratch_shapes=[
            pltpu.VMEM(shape, dtype)
            for dtype, shapes_of in (
                (bf16, (block, block, *in_parts, mid, down_weight.shape)),
                (
                    f32,
                    (
                        tables_in.shape,
                        tables_in.shape,
                        in_weight.shape,
                        out_weight.shape,
                        up_weight.shape,
                        down_weight.shape,
                    ),
                ),
            )
            for shape in shapes_of
        ]
        + [dma((5 * LAYERS + 2,))] * 2,
        compiler_params=pltpu.CompilerParams(vmem_limit_bytes=62 * 1024 * 1024),
    )(*sums, act, xgrad, small)
    act, xgrad, g_in, g_out, g_up, g_down, root_means = outs[:7]
    query, value, out, gain1, shift1, up, down, gain2, shift2 = outs[7:]
    return (
        act,
        xgrad,
        g_in,
        query,
        value,
        g_out,
        out,
        gain1,
        shift1,
        g_up,
        up,
        g_down,
        down,
        gain2,
        shift2,
        root_means,
    )


def per_device(tables, row_parts, *operands):
    local, block_tables, dim = operands[0].shape
    fits = local * row_parts <= 1024 and local * block_tables % TILE == 0
    if tables == 4 and row_parts == 2 * block_tables and fits:
        return table_device(tables, row_parts, *operands)
    return gathered_device(*operands)


def solution(mesh):
    placed = (
        P("rows", "tables", None),
        P(),
        P(),
        P(),
        P(),
        P(),
        P(),
        P(),
        P(),
        P(),
        P(),
        P(),
        P(),
        P(),
        P("rows", "tables", None),
        P("tables"),
        P("tables"),
    )
    return jax.shard_map(
        functools.partial(per_device, mesh.shape["tables"], mesh.shape["rows"]),
        mesh=mesh,
        in_specs=placed,
        out_specs=(
            P("rows", "tables", None),
            P("rows", "tables", None),
            P(),
            P(),
            P(),
            P(),
            P(),
            P(),
            P(),
            P(),
            P(),
            P(),
            P(),
            P(),
            P(),
            P(),
        ),
        check_vma=False,
    )
```

```python
import functools
import math

import jax
import jax.numpy as jnp
from jax import lax
from jax.experimental import pallas as pl
from jax.experimental.pallas import tpu as pltpu
from jax.sharding import PartitionSpec as P

D = 512
HEADS = 4
LAYERS = 2


EPSILON = 1e-05
MASKED = -1e30


def norm_forward(values, gain_row, offsets):
    average = jnp.mean(values, axis=-1, keepdims=True)
    centered = values - average
    variance = jnp.mean(centered * centered, axis=-1, keepdims=True)
    inverse = lax.rsqrt(variance + EPSILON)
    normed = centered * inverse
    return (normed * gain_row + offsets, normed, inverse)


def norm_backward(upstream, normed, inverse, gain_row):
    scaled = upstream * gain_row
    average = jnp.mean(scaled, axis=-1, keepdims=True)
    projection = jnp.mean(scaled * normed, axis=-1, keepdims=True)
    return inverse * (scaled - average - normed * projection)


def gelu_exact(values):
    return jax.nn.gelu(values, approximate=False)


def split_heads(values):
    return values.reshape(values.shape[0], values.shape[1], HEADS, values.shape[2] // HEADS)


def merge_heads(values):
    return values.reshape(values.shape[0], values.shape[1], values.shape[2] * values.shape[3])


def table_scores(queries, key_rows, usable):
    scores = jnp.einsum(
        "ibhe,jbhe->bhij",
        split_heads(queries),
        split_heads(key_rows),
        preferred_element_type=jnp.float32,
    )
    return jnp.where(usable[:, None, None, :], scores, MASKED)


def row_sums(values):
    return jnp.sum(values.astype(jnp.float32), axis=(0, 1))


def gathered_device(
    tables_in,
    in_weight,
    query_bias,
    value_bias,
    out_weight,
    out_bias,
    attn_gain,
    attn_shift,
    up_weight,
    up_bias,
    down_weight,
    down_bias,
    ffn_gain,
    ffn_shift,
    cotangent,
    lengths,
    train_counts,
):
    local_rows = tables_in.shape[0]
    seq_rows = local_rows * lax.axis_size("rows")
    positions = lax.axis_index("rows") * local_rows + jnp.arange(local_rows, dtype=jnp.int32)
    valid_rows = (positions[:, None] < lengths[None, :]).astype(jnp.float32)
    valid_cells = valid_rows[:, :, None]
    usable = jnp.arange(seq_rows, dtype=jnp.int32)[None, :] < train_counts[:, None]
    score_scale = (D // HEADS) ** (-0.5)
    column_scale = jnp.concatenate(
        [jnp.full((D,), score_scale, jnp.float32), jnp.ones((2 * D,), jnp.float32)]
    )
    stream = tables_in.astype(jnp.float32)
    stored = []
    squares = []
    for layer_index in range(LAYERS):
        in_low = stream.astype(jnp.bfloat16)
        projected = jnp.einsum(
            "ibd,de->ibe", in_low, in_weight[layer_index], preferred_element_type=jnp.float32
        )
        queries = ((projected[:, :, :D] + query_bias[layer_index]) * score_scale).astype(
            jnp.bfloat16
        )
        key_rows = projected[:, :, D : 2 * D].astype(jnp.bfloat16)
        value_rows = (projected[:, :, 2 * D :] + value_bias[layer_index]).astype(jnp.bfloat16)
        all_keys, all_values = (
            lax.all_gather(key_rows, "rows", axis=0, tiled=True),
            lax.all_gather(value_rows, "rows", axis=0, tiled=True),
        )
        scores = table_scores(queries, all_keys, usable)
        row_max = jnp.max(scores, axis=-1, keepdims=True)
        exponent = jnp.exp(scores - row_max)
        row_total = jnp.sum(exponent, axis=-1, keepdims=True)
        probs_low = (exponent / row_total).astype(jnp.bfloat16)
        log_total = (row_max + jnp.log(row_total))[..., 0]
        attended = merge_heads(
            jnp.einsum(
                "bhij,jbhe->ibhe",
                probs_low,
                split_heads(all_values),
                preferred_element_type=jnp.float32,
            )
        ).astype(jnp.bfloat16)
        branch = (
            jnp.einsum(
                "ibd,de->ibe", attended, out_weight[layer_index], preferred_element_type=jnp.float32
            )
            + out_bias[layer_index]
        )
        first_out, first_norm, first_inverse = norm_forward(
            stream + branch, attn_gain[layer_index], attn_shift[layer_index]
        )
        mid_low = first_out.astype(jnp.bfloat16)
        hidden = (
            jnp.einsum(
                "ibd,df->ibf", mid_low, up_weight[layer_index], preferred_element_type=jnp.float32
            )
            + up_bias[layer_index]
        )
        act_low = gelu_exact(hidden).astype(jnp.bfloat16)
        ffn_out = (
            jnp.einsum(
                "ibf,fd->ibd", act_low, down_weight[layer_index], preferred_element_type=jnp.float32
            )
            + down_bias[layer_index]
        )
        second_out, second_norm, second_inverse = norm_forward(
            first_out + ffn_out, ffn_gain[layer_index], ffn_shift[layer_index]
        )
        squares.append(
            jnp.stack(
                [
                    jnp.sum(valid_cells * stream * stream),
                    jnp.sum(valid_cells * branch * branch),
                    jnp.sum(valid_cells * ffn_out * ffn_out),
                ]
            )
        )
        gathered = (all_keys, all_values)
        stored.append(
            (
                in_low,
                queries,
                key_rows,
                value_rows,
                gathered,
                log_total,
                attended,
                first_norm,
                first_inverse,
                mid_low,
                hidden,
                act_low,
                second_norm,
                second_inverse,
            )
        )
        stream = second_out
    activations = stream * valid_cells
    upstream = cotangent.astype(jnp.float32) * valid_cells
    layer_grads = [None] * LAYERS
    for layer_index in reversed(range(LAYERS)):
        (
            in_low,
            queries,
            key_rows,
            value_rows,
            gathered,
            log_total,
            attended,
            first_norm,
            first_inverse,
            mid_low,
            hidden,
            act_low,
            second_norm,
            second_inverse,
        ) = stored[layer_index]
        ffn_gain_grad = jnp.sum(upstream * second_norm, axis=(0, 1))
        ffn_shift_grad = jnp.sum(upstream, axis=(0, 1))
        second_grad = norm_backward(upstream, second_norm, second_inverse, ffn_gain[layer_index])
        ffn_low = second_grad.astype(jnp.bfloat16)
        down_weight_grad = jnp.einsum(
            "ibf,ibd->fd", act_low, ffn_low, preferred_element_type=jnp.float32
        )
        act_grad = jnp.einsum(
            "ibd,fd->ibf", ffn_low, down_weight[layer_index], preferred_element_type=jnp.float32
        )
        hidden_low = jax.vjp(gelu_exact, hidden)[1](act_grad)[0].astype(jnp.bfloat16)
        up_weight_grad = jnp.einsum(
            "ibd,ibf->df", mid_low, hidden_low, preferred_element_type=jnp.float32
        )
        first_grad = second_grad + jnp.einsum(
            "ibf,df->ibd", hidden_low, up_weight[layer_index], preferred_element_type=jnp.float32
        )
        attn_gain_grad = jnp.sum(first_grad * first_norm, axis=(0, 1))
        attn_shift_grad = jnp.sum(first_grad, axis=(0, 1))
        residual_grad = norm_backward(first_grad, first_norm, first_inverse, attn_gain[layer_index])
        branch_low = residual_grad.astype(jnp.bfloat16)
        out_weight_grad = jnp.einsum(
            "ibd,ibe->de", attended, branch_low, preferred_element_type=jnp.float32
        )
        attended_low = jnp.einsum(
            "ibe,de->ibd", branch_low, out_weight[layer_index], preferred_element_type=jnp.float32
        ).astype(jnp.bfloat16)
        all_keys, all_values = gathered
        scores = table_scores(queries, all_keys, usable)
        attn_probs = jnp.exp(scores - log_total[..., None])
        probs_low = attn_probs.astype(jnp.bfloat16)
        probs_grad = jnp.einsum(
            "ibhe,jbhe->bhij",
            split_heads(attended_low),
            split_heads(all_values),
            preferred_element_type=jnp.float32,
        )
        center = jnp.sum(attn_probs * probs_grad, axis=-1)
        scores_low = (attn_probs * (probs_grad - center[..., None])).astype(jnp.bfloat16)
        query_low = merge_heads(
            jnp.einsum(
                "bhij,jbhe->ibhe",
                scores_low,
                split_heads(all_keys),
                preferred_element_type=jnp.float32,
            )
        ).astype(jnp.bfloat16)
        key_part = jnp.einsum(
            "bhij,ibhe->jbhe", scores_low, split_heads(queries), preferred_element_type=jnp.float32
        )
        value_part = jnp.einsum(
            "bhij,ibhe->jbhe",
            probs_low,
            split_heads(attended_low),
            preferred_element_type=jnp.float32,
        )
        key_sums = lax.psum_scatter(
            jnp.concatenate([merge_heads(key_part), merge_heads(value_part)], axis=-1).astype(
                jnp.bfloat16
            ),
            "rows",
            scatter_dimension=0,
            tiled=True,
        )
        proj_low = jnp.concatenate([query_low, key_sums], axis=-1)
        in_weight_grad = (
            jnp.einsum("ibd,ibe->de", in_low, proj_low, preferred_element_type=jnp.float32)
            * column_scale
        )
        query_bias_grad = row_sums(query_low) * score_scale
        value_bias_grad = row_sums(proj_low[:, :, 2 * D :])
        weight_now = in_weight[layer_index]
        query_input = (
            jnp.einsum(
                "ibe,de->ibd", query_low, weight_now[:, :D], preferred_element_type=jnp.float32
            )
            * score_scale
        )
        other_input = jnp.einsum(
            "ibe,de->ibd", proj_low[:, :, D:], weight_now[:, D:], preferred_element_type=jnp.float32
        )
        upstream = residual_grad + query_input + other_input
        layer_grads[layer_index] = (
            in_weight_grad,
            query_bias_grad,
            value_bias_grad,
            out_weight_grad,
            row_sums(branch_low),
            attn_gain_grad,
            attn_shift_grad,
            up_weight_grad,
            row_sums(hidden_low),
            down_weight_grad,
            row_sums(ffn_low),
            ffn_gain_grad,
            ffn_shift_grad,
        )
    stacked = [
        jnp.stack([layer_grads[layer_index][member] for layer_index in range(LAYERS)])
        for member in range(13)
    ]
    totals = lax.psum(
        (
            stacked[0],
            stacked[1],
            stacked[2],
            stacked[3],
            stacked[4],
            stacked[5],
            stacked[6],
            stacked[7],
            stacked[8],
            stacked[9],
            stacked[10],
            stacked[11],
            stacked[12],
            jnp.stack(squares),
            jnp.sum(valid_rows),
        ),
        ("tables", "rows"),
    )
    root_means = jnp.sqrt(totals[13] / (totals[14] * D))
    return (
        activations,
        upstream,
        totals[0],
        totals[1],
        totals[2],
        totals[3],
        totals[4],
        totals[5],
        totals[6],
        totals[7],
        totals[8],
        totals[9],
        totals[10],
        totals[11],
        totals[12],
        root_means,
    )


MESH = pl.DeviceIdType.MESH
NT = (((1,), (1,)), ((), ()))
NN = (((1,), (0,)), ((), ()))
TN = (((0,), (0,)), ((), ()))
TILE = 512
VECTORS = 9
GROUPS = (4, 2)
HALVES = 2
PATHS = {
    "A": ("cxyz", "cyxz"),
    "B": ("cxynf", "cyxnf"),
    "N": ("cnyxf", "cnyxf"),
    "D": ("cdz", "cdz"),
}
KINDS = "ABNANBBAANDAD"
SCHEDULE = (
    (),
    (),
    (0,),
    (),
    (),
    (),
    (1, 2),
    (0,),
    (3,),
    (),
    (1,),
    (0, 2, 3, 4, 5, 1),
    (),
    (),
    (),
    (),
    (),
    (),
    (2, 3, 0, 1, 6, 7, 8),
    (5,),
    (),
    (2,),
    (4, 9),
    (),
    (1,),
    (),
    (
        10, 12, 3, 8, 11, 1, 6, 9, 0, 2, 5, 4, 12, 2, 8, 7, 5, 9, 12, 11, 1, 10, 8, 3, 6, 4, 2, 9,
        0, 5, 12, 10, 8, 11, 1, 7, 9, 4, 6, 5, 10, 2, 3, 9, 11, 4, 6, 7, 5, 9, 12, 13, 8, 11, 6, 3,
        4, 9, 5, 2, 7, 10, 1, 12, 11, 0, 6, 8, 4, 9, 7, 3, 2, 11, 10, 6, 5, 4, 11, 8, 7, 0, 1, 5, 6,
        7, 9, 4, 6,
    ),
)


def dot(left, right, dims=NN):
    return lax.dot_general(left, right, dims, preferred_element_type=jnp.float32)


def column_sum(values):
    return jnp.sum(values, axis=0, keepdims=True)


def row_mean(values):
    return jnp.mean(values, axis=-1, keepdims=True)


def send(source, target, sems, stage, device):
    return pltpu.make_async_remote_copy(
        src_ref=source,
        dst_ref=target,
        send_sem=sems.at[0],
        recv_sem=sems.at[1 + stage],
        device_id=device,
        device_id_type=MESH,
    )


def reduce_job(part, total, recv, sems, stages):
    rows, used = part.shape[0], 0
    base, height = 0, rows
    spread, gather, inbox, held = [], [], [], []
    last = len(stages) - 1
    for n, (own, peers) in enumerate(stages):
        height = height // (len(peers) + 1)

        def piece(index):
            return pl.ds(pl.multiple_of(base + index * height, height), height)

        mine = piece(own)
        inbox.append(recv.at[pl.ds(used, len(peers) * height)])
        spread.append(
            [
                send(part.at[piece(index)], recv.at[pl.ds(used + m * height, height)], sems, n, device)
                for m, (device, index) in enumerate(peers)
            ]
        )
        source = part if n == last else total
        gather.append(
            [send(source.at[mine], total.at[mine], sems, 5 + n, device) for device, _ in peers]
        )
        held.append((base + own * height, height, used, len(peers)))
        used += len(peers) * height
        base = base + own * height
    kept = pltpu.make_async_copy(part.at[mine], total.at[mine], sems.at[11])

    def wait_all(stage, n):
        send(inbox[n], inbox[n], sems, stage, stages[n][1][0][0]).wait()

    def start_all(copies):
        for copy in copies:
            copy.start()

    def add(n):
        start, size, offset, count = held[n]
        step = 128 if size % 128 == 0 else size

        def chunk(i, carry):
            at = pl.ds(pl.multiple_of(start + i * step, step), step)
            sums = part[at, :].astype(jnp.float32)
            for m in range(count):
                other = pl.ds(pl.multiple_of(offset + m * size + i * step, 16), step)
                sums = sums + recv[other, :].astype(jnp.float32)
            part[at, :] = sums.astype(part.dtype)
            return carry

        lax.fori_loop(0, size // step, chunk, 0)

    def first():
        start_all(spread[0])

    def fold(n):
        def run():
            wait_all(n, n)
            add(n)
            if n < last:
                start_all(spread[n + 1])
            else:
                kept.start()
                start_all(gather[n])

        return run

    def unfold(n):
        def run():
            wait_all(5 + n, n)
            if n == last:
                kept.wait()
            if n > 0:
                start_all(gather[n - 1])

        return run

    return [first] + [fold(n) for n in range(last + 1)] + [unfold(n) for n in range(last, -1, -1)]


def small_job(part, total, recv, sems, stages):
    base, width = 0, part.shape[1]
    spread, gather, held = [], [], []
    last = len(stages) - 1
    for n, (own, peers) in enumerate(stages):
        if n < last:
            width = width // (len(peers) + 1)

        def piece(index):
            return pl.ds(pl.multiple_of(base + index * width, width), width)

        mine = piece(own) if n < last else piece(0)
        spread.append(
            [
                send(part.at[:, piece(index) if n < last else mine], recv[n].at[m], sems, n, device)
                for m, (device, index) in enumerate(peers)
            ]
        )
        gather.append(
            [send(total.at[:, mine], total.at[:, mine], sems, 5 + n, device) for device, _ in peers]
        )
        held.append(mine)
        if n < last:
            base = base + own * width

    def wait_all(stage, n):
        send(recv[n], recv[n], sems, stage, stages[n][1][0][0]).wait()

    def start_all(copies):
        for copy in copies:
            copy.start()

    def first():
        start_all(spread[0])

    def fold(n):
        def run():
            wait_all(n, n)
            own = part[:, held[n]]
            if n < last:
                for m in range(len(stages[n][1])):
                    own = own + recv[n][m]
                part[:, held[n]] = own
                start_all(spread[n + 1])
            else:
                total[:, held[n]] = (own + recv[n][0]) + (recv[n][1] + recv[n][2])
                start_all(gather[n - 1])

        return run

    def unfold(n):
        def run():
            wait_all(5 + n, n)
            if n > 0:
                start_all(gather[n - 1])

        return run

    return [first] + [fold(n) for n in range(last + 1)] + [unfold(n) for n in range(last - 1, -1, -1)]


def table_kernel(
    local,
    block_tables,
    seq,
    x_hbm,
    cot_hbm,
    lengths_ref,
    counts_ref,
    w_in_hbm,
    w_out_hbm,
    w_up_hbm,
    w_down_hbm,
    *refs,
):
    vector_refs, refs = refs[:VECTORS], refs[VECTORS:]
    (
        act_hbm,
        xgrad_hbm,
        t_in_first,
        t_in_last,
        t_mid,
        t_down,
        t_small,
        w_in,
        w_out,
        w_up,
        w_down,
        vectors,
        g_in_first,
        g_in_last,
        g_mid,
        g_down,
        small,
        in_low,
        cot_low,
        stream,
        queries,
        kv,
        attended,
        log_totals,
        norm1,
        inverse1,
        mid_low,
        slope,
        act_low,
        norm2,
        inverse2,
        meta,
        bias_col,
        valid,
        ffn_low,
        attended_low,
        centers,
        dkv_send,
        dkv_recv_first,
        dkv_recv_last,
        proj_low,
        staged,
        recv_in_first,
        recv_in_last,
        recv_mid,
        recv_down,
        recv_small,
        x_send,
        x_recv,
        cot_send,
        cot_recv,
        act_send,
        act_recv,
        xg_send,
        xg_recv,
        local_sem,
        kv_sem,
        dkv_sem,
        meta_sem,
        job_sem,
    ) = refs
    upstream = stream
    t_in, g_in, recv_in = (t_in_first, t_in_last), (g_in_first, g_in_last), (recv_in_first, recv_in_last)
    branch_low = ffn_low
    dkv_recvs = (dkv_recv_first, dkv_recv_last)
    rows = block_tables * local
    dim = in_low.shape[-1]
    head_dim = dim // HEADS
    scale = head_dim**-0.5
    tiles = rows // TILE
    t = lax.axis_index("tables")
    r = lax.axis_index("rows")
    core = lax.rem(t, 2)
    side = r // block_tables
    slot = lax.rem(r, block_tables)
    peer = (t + 1 - 2 * core, r)
    own_rows = pl.multiple_of(core * rows, rows)
    peer_rows = pl.multiple_of((1 - core) * rows, rows)

    x_side, y_side, z_side = lax.rem(r, 2), t // 2, r // 2
    x_next = (t, r + 1 - 2 * x_side)
    y_next = (t + 2 - 4 * y_side, r)
    z_next = [
        (z_side + 1 - 2 * lax.rem(z_side, 2)),
        lax.rem(z_side + 2, 4),
        3 - z_side,
    ]
    z_peers = [((t, 2 * z + x_side), z) for z in z_next]

    def choose(first, second):
        return core * second + (1 - core) * first

    y_index = t + 2 - 4 * y_side
    corner = x_side + 2 * y_side
    corners = [
        (x_next, 1 - x_side + 2 * y_side),
        (y_next, x_side + 2 - 2 * y_side),
        ((y_index, x_next[1]), 3 - corner),
    ]
    sides = {
        "c": (core, [(peer, 1 - core)]),
        "x": (x_side, [(x_next, 1 - x_side)]),
        "y": (y_side, [(y_next, 1 - y_side)]),
        "n": (lax.rem(z_side, 2), [(z_peers[0][0], 1 - lax.rem(z_side, 2))]),
        "f": (z_side // 2, [(z_peers[1][0], 1 - z_side // 2)]),
        "d": (corner, corners),
        "z": (z_side, z_peers),
    }

    def both(first, second):
        if first == second:
            return sides[first]
        (one_own, [(one, one_index)]), (two_own, [(two, two_index)]) = sides[first], sides[second]
        device = (choose(one[0], two[0]), choose(one[1], two[1]))
        return choose(one_own, two_own), [(device, choose(one_index, two_index))]

    def path(kind):
        first, second = PATHS[kind]
        return [both(*pair) for pair in zip(first, second)]

    def partner(k):
        return (t - core + side, block_tables * core + k)

    def is_self(k):
        return jnp.logical_and(core == side, slot == k)

    barrier = pltpu.get_barrier_semaphore()
    greeted = [peer, x_next, y_next] + [device for device, _ in z_peers]
    for device in greeted:
        pl.semaphore_signal(barrier, inc=1, device_id=device, device_id_type=MESH)
    for k in range(block_tables):

        @pl.when(jnp.logical_not(is_self(k)))
        def _():
            pl.semaphore_signal(barrier, inc=1, device_id=partner(k), device_id_type=MESH)

    pl.semaphore_wait(
        barrier, len(greeted) + jnp.where(core == side, block_tables - 1, block_tables)
    )

    def spread(source, target, send_sem, recv_sem, own_sem):
        def remote(k, at):
            return pltpu.make_async_remote_copy(
                src_ref=source(k),
                dst_ref=target(at),
                send_sem=send_sem.at[k],
                recv_sem=recv_sem.at[at],
                device_id=partner(k),
                device_id_type=MESH,
            )

        def kept(k):
            return pltpu.make_async_copy(source(k), target(k), own_sem)

        def start(blocks=range(block_tables)):
            for k in blocks:

                @pl.when(is_self(k))
                def _():
                    kept(k).start()

                @pl.when(jnp.logical_not(is_self(k)))
                def _():
                    remote(k, slot).start()

        def arrive():
            for k in range(block_tables):

                @pl.when(is_self(k))
                def _():
                    kept(k).wait()

                @pl.when(jnp.logical_not(is_self(k)))
                def _():
                    remote(k, k).wait_recv()

        def left():
            for k in range(block_tables):

                @pl.when(jnp.logical_not(is_self(k)))
                def _():
                    remote(k, slot).wait_send()

        return start, arrive, left

    def by_table(ref):
        return lambda k: ref.at[k]

    def by_rows(ref):
        return lambda k: ref.at[pl.ds(k * local, local)]

    x_start, x_arrive, x_left = spread(by_table(x_hbm), by_rows(in_low.at[0]), x_send, x_recv, local_sem.at[0])
    cot_start, cot_arrive, cot_left = spread(by_table(cot_hbm), by_rows(cot_low), cot_send, cot_recv, local_sem.at[1])
    act_start, act_arrive, act_left = spread(by_rows(staged.at[0]), by_table(act_hbm), act_send, act_recv, local_sem.at[2])
    xg_start, xg_arrive, xg_left = spread(by_rows(staged.at[1]), by_table(xgrad_hbm), xg_send, xg_recv, local_sem.at[3])

    def swap(source, target, sems):
        return pltpu.make_async_remote_copy(
            src_ref=source,
            dst_ref=target,
            send_sem=sems.at[0],
            recv_sem=sems.at[1],
            device_id=peer,
            device_id_type=MESH,
        )

    x_start()
    loads = [
        pltpu.make_async_copy(source, target, local_sem.at[4 + n])
        for n, (source, target) in enumerate(
            ((w_in_hbm, w_in), (w_out_hbm, w_out), (w_up_hbm, w_up), (w_down_hbm, w_down))
        )
    ]
    for load in loads:
        load.start()
    for n, ref in enumerate(vector_refs):
        for layer in range(LAYERS):
            vectors[pl.ds(layer * VECTORS + n, 1), pl.ds(0, ref.shape[1])] = ref[...].astype(
                jnp.float32
            )[layer : layer + 1, :]
    for k in range(block_tables):
        meta[core, pl.ds(k, 1), :] = jnp.full((1, 128), lengths_ref[k], jnp.int32)
        meta[core, pl.ds(block_tables + k, 1), :] = jnp.full((1, 128), counts_ref[k], jnp.int32)
    meta_copy = swap(meta.at[core], meta.at[core], meta_sem)
    meta_copy.start()
    small[...] = jnp.zeros_like(small)
    meta_copy.wait()
    length = meta[side, pl.ds(slot, 1), :][:, :1]
    train = meta[side, pl.ds(slot + block_tables, 1), :][:, :1]
    bias_col[...] = jnp.where(lax.broadcasted_iota(jnp.int32, (seq, 1), 0) < train, 0.0, MASKED)
    valid[...] = jnp.where(
        lax.broadcasted_iota(jnp.int32, (rows, 1), 0) + core * rows < length, 1.0, 0.0
    )
    small[pl.ds(13, 1), pl.ds(0, 128)] = jnp.broadcast_to(column_sum(valid[...]), (1, 128))
    x_arrive()
    cot_start()
    loads[0].wait()

    def vector(index, layer, width):
        return vectors[pl.ds(layer * VECTORS + index, 1), pl.ds(0, width)]

    def add_small(layer, index, values):
        at = (pl.ds(layer * 16 + index, 1), pl.ds(0, values.shape[-1]))
        small[at] = small[at] + values

    def each_tile(body, after=()):
        def step(i, carry):
            body(pl.ds(pl.multiple_of(i * TILE, TILE), TILE))
            for n, run in enumerate(after):

                @pl.when(i == n)
                def _():
                    run()

            return carry

        lax.fori_loop(0, tiles, step, 0)

    def head_cols(h):
        return pl.ds(pl.multiple_of(h * head_dim, head_dim), head_dim)

    def forward(layer):
        def project(at):
            projected = dot(in_low[layer, at, :], w_in[layer, :, pl.ds(dim, 2 * dim)])
            own = pl.ds(pl.multiple_of(own_rows + at.start, TILE), TILE)
            key_rows = projected[:, :dim].astype(jnp.bfloat16)
            value_rows = (projected[:, dim:] + vector(1, layer, dim)).astype(jnp.bfloat16)
            for h in range(HEADS):
                cols = slice(h * head_dim, (h + 1) * head_dim)
                kv[layer, h, own, pl.ds(0, head_dim)] = key_rows[:, cols]
                kv[layer, h, own, pl.ds(head_dim, head_dim)] = value_rows[:, cols]

        each_tile(project)

        def kv_copy(h):
            mine = kv.at[layer, h, pl.ds(own_rows, rows)]
            return swap(mine, mine, kv_sem.at[layer, h])

        for h in range(HEADS):
            kv_copy(h).start()

        def ask(at):
            projected = dot(in_low[layer, at, :], w_in[layer, :, pl.ds(0, dim)])
            queries[layer, at, :] = ((projected + vector(0, layer, dim)) * scale).astype(
                jnp.bfloat16
            )

        each_tile(ask)

        def attend(h, carry):
            cols = head_cols(h)
            kv_copy(h).wait()
            scores = dot(kv[layer, h, :, pl.ds(0, head_dim)], queries[layer, :, cols], NT)
            scores = scores + bias_col[...]
            row_max = jnp.max(scores, axis=0, keepdims=True)
            exponent = jnp.exp(scores - row_max)
            total = jnp.sum(exponent, axis=0, keepdims=True)
            mixed = dot(kv[layer, h, :, pl.ds(head_dim, head_dim)], exponent.astype(jnp.bfloat16), TN)
            attended[layer, :, cols] = jnp.transpose(mixed * (1.0 / total)).astype(jnp.bfloat16)
            log_totals[layer, pl.ds(h, 1), :] = row_max + jnp.log(total)
            return carry

        lax.fori_loop(0, HEADS, attend, 0)
        if layer == 0:
            for load in loads[1:]:
                load.wait()

        def dense(at):
            below = in_low[0, at, :].astype(jnp.float32) if layer == 0 else stream[at, :]
            branch = dot(attended[layer, at, :], w_out[layer]) + vector(2, layer, dim)
            valid_cells = valid[at, :]
            add_small(layer, 10, column_sum(below * below * valid_cells))
            add_small(layer, 11, column_sum(branch * branch * valid_cells))
            summed = below + branch
            centered = summed - row_mean(summed)
            inverse = lax.rsqrt(row_mean(centered * centered) + EPSILON)
            normed = centered * inverse
            norm1[layer, at, :] = normed
            inverse1[layer, at, :] = inverse
            first_out = normed * vector(3, layer, dim) + vector(4, layer, dim)
            mid = first_out.astype(jnp.bfloat16)
            mid_low[layer, at, :] = mid
            hidden = dot(mid, w_up[layer]) + vector(5, layer, 2 * dim)
            cdf = 0.5 + 0.5 * lax.erf(hidden * (0.5**0.5))
            slope[layer, at, :] = cdf + hidden * (
                jnp.exp(hidden * hidden * -0.5) * 0.3989422804014327
            )
            act = (hidden * cdf).astype(jnp.bfloat16)
            act_low[layer, at, :] = act
            ffn_out = dot(act, w_down[layer]) + vector(6, layer, dim)
            add_small(layer, 12, column_sum(ffn_out * ffn_out * valid_cells))
            summed = first_out + ffn_out
            centered = summed - row_mean(summed)
            inverse = lax.rsqrt(row_mean(centered * centered) + EPSILON)
            normed = centered * inverse
            norm2[layer, at, :] = normed
            inverse2[layer, at, :] = inverse
            out = normed * vector(7, layer, dim) + vector(8, layer, dim)
            if layer + 1 < LAYERS:
                stream[at, :] = out
                in_low[layer + 1, at, :] = out.astype(jnp.bfloat16)
            else:
                staged[0, at, :] = (out * valid_cells).astype(jnp.bfloat16)

        each_tile(dense)

    for layer in range(LAYERS):
        forward(layer)
    act_start()
    cot_arrive()

    jobs = []

    points = list(SCHEDULE)

    def begin(steps):
        jobs.append(list(steps))
        jobs[-1].pop(0)()

    def tick():
        for index in points.pop(0):
            if index < len(jobs) and jobs[index]:
                jobs[index].pop(0)()

    def reduce(part, total, recv):
        begin(reduce_job(part, total, recv, job_sem.at[len(jobs)], path(KINDS[len(jobs)])))

    def reduce_halves(part, total, recv):
        width = part.shape[1] // HALVES
        for n in range(HALVES):
            cols = pl.ds(n * width, width)
            reduce(
                part.at[:, cols],
                total.at[:, cols],
                recv.at[:, cols],
            )

    def backward(layer):
        groups = GROUPS[layer]
        group_heads = HEADS // groups
        group_width = group_heads * head_dim
        dkv_recv = dkv_recvs[layer]
        dq_t = slope.at[layer, :, pl.ds(0, dim)]

        def send_cols(group):
            return pl.ds(group * 2 * group_width, 2 * group_width)


        def enter(at):
            if layer == LAYERS - 1:
                up = cot_low[at, :].astype(jnp.float32) * valid[at, :]
            else:
                up = upstream[at, :]
            normed = norm2[layer, at, :]
            add_small(layer, 8, column_sum(up * normed))
            add_small(layer, 9, column_sum(up))
            scaled = up * vector(7, layer, dim)
            second = inverse2[layer, at, :] * (
                scaled - row_mean(scaled) - normed * row_mean(scaled * normed)
            )
            upstream[at, :] = second
            ffn = second.astype(jnp.bfloat16)
            ffn_low[at, :] = ffn
            add_small(layer, 7, column_sum(ffn.astype(jnp.float32)))

        each_tile(enter)
        g_down[layer] = dot(act_low[layer], ffn_low[...], TN).astype(jnp.bfloat16)
        tick()
        reduce(g_down.at[layer], t_down.at[layer], recv_down.at[layer])

        def dense(at):
            hidden = (dot(ffn_low[at, :], w_down[layer], NT) * slope[layer, at, :]).astype(
                jnp.bfloat16
            )
            proj_low[at, pl.ds(0, hidden.shape[1])] = hidden
            add_small(layer, 6, column_sum(hidden.astype(jnp.float32)))
            first = upstream[at, :] + dot(hidden, w_up[layer], NT)
            normed = norm1[layer, at, :]
            add_small(layer, 4, column_sum(first * normed))
            add_small(layer, 5, column_sum(first))
            scaled = first * vector(3, layer, dim)
            residual = inverse1[layer, at, :] * (
                scaled - row_mean(scaled) - normed * row_mean(scaled * normed)
            )
            upstream[at, :] = residual
            branch = residual.astype(jnp.bfloat16)
            branch_low[at, :] = branch
            add_small(layer, 3, column_sum(branch.astype(jnp.float32)))
            low = dot(branch, w_out[layer], NT).astype(jnp.bfloat16)
            attended_low[at, :] = low
            product = low.astype(jnp.float32) * attended[layer, at, :].astype(jnp.float32)
            lane = lax.broadcasted_iota(jnp.int32, (TILE, head_dim), 1)
            held = jnp.zeros((TILE, head_dim), jnp.float32)
            for h in range(HEADS):
                center = jnp.sum(product[:, h * head_dim : (h + 1) * head_dim], axis=-1, keepdims=True)
                held = jnp.where(lane == h, center, held)
            centers[:, at] = jnp.transpose(held)[:8, :]

        each_tile(dense, (tick,) * tiles)
        up_grad = dot(mid_low[layer], proj_low[:, pl.ds(0, 2 * dim)], TN).astype(jnp.bfloat16)
        g_mid[layer, pl.ds(0, dim), :] = up_grad[:, :dim]
        g_mid[layer, pl.ds(dim, dim), :] = up_grad[:, dim:]
        g_mid[layer, pl.ds(2 * dim, dim), :] = dot(attended[layer], branch_low[...], TN).astype(
            jnp.bfloat16
        )
        tick()
        reduce_halves(g_mid.at[layer], t_mid.at[layer], recv_mid.at[layer])

        def attend(group, base, first, keep):
            def step(i, carry):
                h = group * group_heads + i // tiles
                j = pl.multiple_of(lax.rem(i, tiles) * TILE, TILE)
                at = pl.ds(pl.multiple_of(base + j, TILE), TILE)
                cols = head_cols(h)
                key_rows = kv[layer, h, at, pl.ds(0, head_dim)]
                query_rows = queries[layer, :, cols]
                grads = attended_low[:, cols]
                probs = jnp.exp(
                    dot(key_rows, query_rows, NT) + bias_col[at, :] - log_totals[layer, pl.ds(h, 1), :]
                )
                value_part = dot(probs.astype(jnp.bfloat16), grads)
                probs_grad = dot(kv[layer, h, at, pl.ds(head_dim, head_dim)], grads, NT)
                scores_low = (probs * (probs_grad - centers[pl.ds(h, 1), :])).astype(
                    jnp.bfloat16
                )
                key_part = dot(scores_low, query_rows)
                query_part = dot(key_rows, scores_low, TN)
                if first:
                    query_part = jnp.where(j == 0, query_part, query_part + dq_t[cols, :])
                else:
                    query_part = query_part + dq_t[cols, :]
                dq_t[cols, :] = query_part
                inside = i // tiles * head_dim
                keep(pl.ds(j, TILE), pl.ds(pl.multiple_of(inside, head_dim), head_dim), key_part)
                keep(
                    pl.ds(j, TILE),
                    pl.ds(pl.multiple_of(group_width + inside, head_dim), head_dim),
                    value_part,
                )
                return carry

            lax.fori_loop(0, group_heads * tiles, step, 0)

        def dkv_copy(group):
            return swap(
                dkv_send.at[:, send_cols(group)], dkv_recv.at[group], dkv_sem.at[layer, group]
            )

        def attend_peer(group):
            def keep(at, cols, part):
                start = group * 2 * group_width + cols.start
                dkv_send[at, pl.ds(pl.multiple_of(start, head_dim), cols.size)] = part.astype(
                    jnp.bfloat16
                )

            attend(group, peer_rows, True, keep)
            dkv_copy(group).start()
            tick()

        def attend_own(group):
            def keep(at, cols, part):
                start = pl.multiple_of(dim + cols.start, head_dim)
                slope[layer, at, pl.ds(start, cols.size)] = part

            attend(group, own_rows, False, keep)
            tick()

        def finish_group(group):
            dkv_copy(group).wait()

            def finish(at):
                group_rows = pl.ds(group * group_width, group_width)
                query = jnp.transpose(dq_t[group_rows, at]).astype(jnp.bfloat16)
                pair = (
                    slope[layer, at, pl.ds(dim, 2 * group_width)] + dkv_recv[group, at, :].astype(jnp.float32)
                ).astype(jnp.bfloat16)
                for n, part in enumerate((query, pair[:, :group_width], pair[:, group_width:])):
                    proj_low[at, pl.ds(n * dim + group * group_width, group_width)] = part
                cols = pl.ds(group * group_width, group_width)
                small[pl.ds(layer * 16, 1), cols] += column_sum(query.astype(jnp.float32)) * scale
                small[pl.ds(layer * 16 + 1, 1), cols] += column_sum(
                    pair[:, group_width:].astype(jnp.float32)
                )

            each_tile(finish)
            parts = [
                proj_low[:, pl.ds(n * dim + group * group_width, group_width)] for n in range(3)
            ]
            grad = dot(in_low[layer], jnp.concatenate(parts, axis=1), TN)
            g_in[layer][group, :, pl.ds(0, group_width)] = (grad[:, :group_width] * scale).astype(
                jnp.bfloat16
            )
            g_in[layer][group, :, pl.ds(group_width, 2 * group_width)] = grad[
                :, group_width:
            ].astype(jnp.bfloat16)
            tick()
            reduce(
                g_in[layer].at[group],
                t_in[layer].at[group],
                recv_in[layer].at[group],
            )

        for group in range(groups):
            attend_peer(group)
            if group > 0:
                finish_group(group - 1)
            attend_own(group)
        finish_group(groups - 1)
        if layer == 0:
            begin(small_job(small, t_small, recv_small, job_sem.at[len(jobs)], path("D")))

        def pass_down(at):
            grad = (
                upstream[at, :]
                + dot(proj_low[at, pl.ds(0, dim)], w_in[layer, :, pl.ds(0, dim)], NT) * scale
                + dot(proj_low[at, pl.ds(dim, 2 * dim)], w_in[layer, :, pl.ds(dim, 2 * dim)], NT)
            )
            if layer > 0:
                upstream[at, :] = grad
            else:
                staged[1, at, :] = grad.astype(jnp.bfloat16)

        each_tile(pass_down)
        if layer == 0:
            xg_start(range(block_tables // 2))
            jobs.append([lambda: xg_start(range(block_tables // 2, block_tables))])
        tick()

    for layer in reversed(range(LAYERS)):
        backward(layer)
    tick()
    while any(jobs):
        for steps in jobs:
            if steps:
                steps.pop(0)()
    act_arrive()
    xg_arrive()
    x_left()
    cot_left()
    act_left()
    xg_left()


def widen_kernel(f_first, f_last, f_mid, f_down, f_act, f_xgrad, small, *refs):
    act, xgrad, in_weight, out_weight, up_weight, down_weight, root_means = refs[:7]
    low_act, low_xgrad, low_first, low_last, low_mid, low_down = refs[16:22]
    wide_act, wide_xgrad, wide_in, wide_out, wide_up, wide_down = refs[22:28]
    read_sem, write_sem = refs[28:]
    dim = f_act.shape[2]
    half = dim // 2

    def widened(values):
        return values.astype(jnp.float32)

    def table_part(source, low, wide, target):
        def convert():
            for k in range(source.shape[0]):
                wide[:, k, :] = widened(low[k])

        return (source, low), convert, [(wide, target)]

    def down_part(layer):
        def convert():
            wide_down[layer] = widened(low_down[layer])

        return (
            (f_down.at[layer], low_down.at[layer]),
            convert,
            [(wide_down.at[layer], down_weight.at[layer])],
        )

    def mid_part(layer):
        def convert():
            for n in range(2):
                wide_up[layer, :, pl.ds(n * dim, dim)] = widened(low_mid[layer, pl.ds(n * dim, dim), :])
            wide_out[layer] = widened(low_mid[layer, pl.ds(2 * dim, dim), :])

        return (
            (f_mid.at[layer], low_mid.at[layer]),
            convert,
            [
                (wide_up.at[layer], up_weight.at[layer]),
                (wide_out.at[layer], out_weight.at[layer]),
            ],
        )

    def in_part(layer, source, low, start):
        at = pl.ds(start, half)
        groups, width = source.shape[0], source.shape[2] // 3

        def convert():
            for group in range(groups):
                for n in range(3):
                    wide_in[layer, at, pl.ds((n * groups + group) * width, width)] = widened(
                        low[group, at, pl.ds(n * width, width)]
                    )

        return (
            (source.at[:, at], low.at[:, at]),
            convert,
            [(wide_in.at[layer, at], in_weight.at[layer, at])],
        )

    parts = [
        table_part(f_act, low_act, wide_act, act),
        table_part(f_xgrad, low_xgrad, wide_xgrad, xgrad),
    ]
    for layer, (source, low) in enumerate(((f_first, low_first), (f_last, low_last))):
        parts += [in_part(layer, source, low, 0), in_part(layer, source, low, half)]
        parts += [mid_part(layer), down_part(layer)]
    reads = [
        pltpu.make_async_copy(*part[0], read_sem.at[n]) for n, part in enumerate(parts)
    ]
    writes = []
    for copy in reads:
        copy.start()
    for copy, (_, convert, results) in zip(reads, parts):
        copy.wait()
        convert()
        for source, target in results:
            writes.append(pltpu.make_async_copy(source, target, write_sem.at[len(writes)]))
            writes[-1].start()
    for ref, row in zip(refs[7:16], (0, 1, 3, 4, 5, 6, 7, 8, 9)):
        for layer in range(LAYERS):
            ref[pl.ds(layer, 1), :] = small[pl.ds(layer * 16 + row, 1), pl.ds(0, ref.shape[1])]
    count = small[pl.ds(13, 1), pl.ds(0, 1)]
    for layer in range(LAYERS):
        sums = jnp.sum(small[pl.ds(layer * 16 + 8, 8), pl.ds(0, dim)], axis=-1, keepdims=True)
        for n in range(3):
            root_means[pl.ds(layer, 1), pl.ds(n, 1)] = jnp.sqrt(
                sums[2 + n : 3 + n, :] / (count * dim)
            )
    for write in writes:
        write.wait()


def table_device(tables, row_parts, *operands):
    (
        tables_in,
        in_weight,
        query_bias,
        value_bias,
        out_weight,
        out_bias,
        attn_gain,
        attn_shift,
        up_weight,
        up_bias,
        down_weight,
        down_bias,
        ffn_gain,
        ffn_shift,
        cotangent,
        lengths,
        train_counts,
    ) = operands
    local, block_tables, dim = tables_in.shape
    rows = local * block_tables
    seq = local * row_parts
    hidden = up_weight.shape[-1]
    head_dim = dim // HEADS
    f32, bf16 = jnp.float32, jnp.bfloat16
    vmem = pl.BlockSpec(memory_space=pltpu.VMEM)
    hbm = pl.BlockSpec(memory_space=pl.ANY)
    smem = pl.BlockSpec(memory_space=pltpu.SMEM)
    block = (block_tables, local, dim)
    dma = pltpu.SemaphoreType.DMA
    in_parts = [(groups, dim, 3 * dim // groups) for groups in GROUPS]
    mid = (LAYERS, 3 * dim, dim)
    shards = 8 * row_parts // 2

    def received(shape):
        height = shape[-2]
        return pltpu.VMEM(shape[:-2] + (height - height // shards, shape[-1]), bf16)

    act, xgrad, *sums, small = pl.pallas_call(
        functools.partial(table_kernel, local, block_tables, seq),
        out_shape=(
            jax.ShapeDtypeStruct(block, bf16),
            jax.ShapeDtypeStruct(block, bf16),
            jax.ShapeDtypeStruct(in_parts[0], bf16),
            jax.ShapeDtypeStruct(in_parts[1], bf16),
            jax.ShapeDtypeStruct(mid, bf16),
            jax.ShapeDtypeStruct(down_weight.shape, bf16),
            jax.ShapeDtypeStruct((LAYERS * 16, hidden), f32),
        ),
        in_specs=[hbm, hbm, smem, smem] + [hbm] * 4 + [vmem] * VECTORS,
        out_specs=(hbm,) * 6 + (vmem,),
        scratch_shapes=[
            pltpu.VMEM(in_weight.shape, bf16),
            pltpu.VMEM(out_weight.shape, bf16),
            pltpu.VMEM(up_weight.shape, bf16),
            pltpu.VMEM(down_weight.shape, bf16),
            pltpu.VMEM((LAYERS * VECTORS, hidden), f32),
            pltpu.VMEM(in_parts[0], bf16),
            pltpu.VMEM(in_parts[1], bf16),
            pltpu.VMEM(mid, bf16),
            pltpu.VMEM(down_weight.shape, bf16),
            pltpu.VMEM((LAYERS * 16, hidden), f32),
            pltpu.VMEM((LAYERS, rows, dim), bf16),
            pltpu.VMEM((rows, dim), bf16),
            pltpu.VMEM((rows, dim), f32),
            pltpu.VMEM((LAYERS, rows, dim), bf16),
            pltpu.VMEM((LAYERS, HEADS, seq, 2 * head_dim), bf16),
            pltpu.VMEM((LAYERS, rows, dim), bf16),
            pltpu.VMEM((LAYERS, 8, rows), f32),
            pltpu.VMEM((LAYERS, rows, dim), f32),
            pltpu.VMEM((LAYERS, rows, 1), f32),
            pltpu.VMEM((LAYERS, rows, dim), bf16),
            pltpu.VMEM((LAYERS, rows, hidden), f32),
            pltpu.VMEM((LAYERS, rows, hidden), bf16),
            pltpu.VMEM((LAYERS, rows, dim), f32),
            pltpu.VMEM((LAYERS, rows, 1), f32),
            pltpu.VMEM((2, 2 * block_tables, 128), jnp.int32),
            pltpu.VMEM((seq, 1), f32),
            pltpu.VMEM((rows, 1), f32),
            pltpu.VMEM((rows, dim), bf16),
            pltpu.VMEM((rows, dim), bf16),
            pltpu.VMEM((8, rows), f32),
            pltpu.VMEM((rows, 2 * dim), bf16),
            *[pltpu.VMEM((groups, rows, 2 * dim // groups), bf16) for groups in GROUPS],
            pltpu.VMEM((rows, 3 * dim), bf16),
            pltpu.VMEM((2, rows, dim), bf16),
        ]
        + [received(shape) for shape in (in_parts[0], in_parts[1], mid, down_weight.shape)]
        + [
            [
                pltpu.VMEM((1, LAYERS * 16, hidden // 2), f32),
                pltpu.VMEM((3, LAYERS * 16, hidden // 8), f32),
                pltpu.VMEM((3, LAYERS * 16, hidden // 8), f32),
            ]
        ]
        + [dma((block_tables,))] * 8
        + [
            dma((8,)),
            dma((LAYERS, HEADS, 2)),
            dma((LAYERS, HEADS, 2)),
            dma((2,)),
            dma((LAYERS * (1 + HALVES) + sum(GROUPS) + 1, 12)),
        ],
        compiler_params=pltpu.CompilerParams(
            collective_id=0, has_side_effects=True, vmem_limit_bytes=63 * 1024 * 1024
        ),
    )(
        jnp.swapaxes(tables_in, 0, 1),
        jnp.swapaxes(cotangent, 0, 1),
        lengths,
        train_counts,
        in_weight,
        out_weight,
        up_weight,
        down_weight,
        query_bias,
        value_bias,
        out_bias,
        attn_gain,
        attn_shift,
        up_bias,
        down_bias,
        ffn_gain,
        ffn_shift,
    )
    vector = jax.ShapeDtypeStruct((LAYERS, dim), f32)
    wide_vector = jax.ShapeDtypeStruct((LAYERS, hidden), f32)
    shapes = [
        jax.ShapeDtypeStruct(tables_in.shape, f32),
        jax.ShapeDtypeStruct(tables_in.shape, f32),
        jax.ShapeDtypeStruct(in_weight.shape, f32),
        jax.ShapeDtypeStruct(out_weight.shape, f32),
        jax.ShapeDtypeStruct(up_weight.shape, f32),
        jax.ShapeDtypeStruct(down_weight.shape, f32),
        jax.ShapeDtypeStruct((LAYERS, 3), f32),
    ] + [vector] * 5 + [wide_vector] + [vector] * 3
    outs = pl.pallas_call(
        widen_kernel,
        out_shape=shapes,
        in_specs=[hbm] * 6 + [vmem],
        out_specs=[hbm] * 6 + [vmem] * 10,
        scratch_shapes=[
            pltpu.VMEM(shape, dtype)
            for dtype, shapes_of in (
                (bf16, (block, block, *in_parts, mid, down_weight.shape)),
                (
                    f32,
                    (
                        tables_in.shape,
                        tables_in.shape,
                        in_weight.shape,
                        out_weight.shape,
                        up_weight.shape,
                        down_weight.shape,
                    ),
                ),
            )
            for shape in shapes_of
        ]
        + [dma((5 * LAYERS + 2,))] * 2,
        compiler_params=pltpu.CompilerParams(vmem_limit_bytes=62 * 1024 * 1024),
    )(*sums, act, xgrad, small)
    act, xgrad, g_in, g_out, g_up, g_down, root_means = outs[:7]
    query, value, out, gain1, shift1, up, down, gain2, shift2 = outs[7:]
    return (
        act,
        xgrad,
        g_in,
        query,
        value,
        g_out,
        out,
        gain1,
        shift1,
        g_up,
        up,
        g_down,
        down,
        gain2,
        shift2,
        root_means,
    )


def per_device(tables, row_parts, *operands):
    local, block_tables, dim = operands[0].shape
    fits = local * row_parts <= 1024 and local * block_tables % TILE == 0
    if tables == 4 and row_parts == 2 * block_tables and fits:
        return table_device(tables, row_parts, *operands)
    return gathered_device(*operands)


def solution(mesh):
    placed = (
        P("rows", "tables", None),
        P(),
        P(),
        P(),
        P(),
        P(),
        P(),
        P(),
        P(),
        P(),
        P(),
        P(),
        P(),
        P(),
        P("rows", "tables", None),
        P("tables"),
        P("tables"),
    )
    return jax.shard_map(
        functools.partial(per_device, mesh.shape["tables"], mesh.shape["rows"]),
        mesh=mesh,
        in_specs=placed,
        out_specs=(
            P("rows", "tables", None),
            P("rows", "tables", None),
            P(),
            P(),
            P(),
            P(),
            P(),
            P(),
            P(),
            P(),
            P(),
            P(),
            P(),
            P(),
            P(),
            P(),
        ),
        check_vma=False,
    )
```
